32 devices in a mesh: dp: 16 (over z, y, x), tensor: 2 (over core).
Axes of the slice: x: 2, y: 2, z: 4, core: 2. Of those that a mesh axis runs over, the one named last changes fastest.
Arguments:
- tokens: bfloat16 [2, 128, 197, 512], P(None, 'dp'), may hold values from -6 to 6
- held: int32 [2, 16], P(None, 'dp'), may hold values from 1 to 8, as said below
- routes: int32 [2, 128, 197, 2], P(None, 'dp'), may hold values from 0 to 7, all different within a row; in each aligned block of 1576 rows (0 to 1575, 1576 to 3151, ..., all dimensions but the last counted through in order) at most 630 rows name the same one
- ln1_gain: bfloat16 [512], P('dp'), may hold values from 0.099609375 to 1.8984375
- qkv_weight: bfloat16 [3, 512, 512], P(None, 'dp', 'tensor'), may hold values from -0.25 to 0.25
- out_weight: bfloat16 [512, 512], P('tensor', 'dp'), may hold values from -1 to 1
- ln2_gain: bfloat16 [512], P('dp'), may hold values from 0.099609375 to 1.8984375
- router_weight: bfloat16 [512, 8], P('dp'), may hold values from -0.125 to 0.125
- expert_in: bfloat16 [8, 512, 2048], P(None, 'dp', 'tensor'), may hold values from -0.25 to 0.25
- expert_out: bfloat16 [8, 2048, 512], P(None, 'tensor', 'dp'), may hold values from -0.1875 to 0.1875
- grad_out: bfloat16 [2, 128, 197, 512], P(None, 'dp'), may hold values from -6 to 6
Outputs:
- block_out: bfloat16 [2, 128, 197, 512], P(None, 'dp')
- grad_tokens: bfloat16 [2, 128, 197, 512], P(None, 'dp')
- grad_ln1_gain: float32 [512], P('dp')
- grad_qkv: float32 [3, 512, 512], P(None, 'dp', 'tensor')
- grad_out_weight: float32 [512, 512], P('tensor', 'dp')
- grad_ln2_gain: float32 [512], P('dp')
- grad_router: float32 [512, 8], P('dp')
- grad_expert_in: float32 [8, 512, 2048], P(None, 'dp', 'tensor')
- grad_expert_out: float32 [8, 2048, 512], P(None, 'tensor', 'dp')
The draws below stay inside these ranges and needn't reach their ends.
Inputs may be any that keep to these rules, and one draw needn't show every extreme that they name: `held`: the live images of a group are its first ones; some group of some micro-batch holds 8 and some holds 1. `routes`: the two experts of a token differ; among the tokens of one index of dp in one micro-batch no expert is named more than 630 times, a bound that some block reaches in some of them.
All inputs are finite; a program needn't handle non-finite values.
Results may differ from the reference program's by a relative error of at most 0.012.
Values may be sent and summed in bfloat16 or wider, within the bound.
No kernel may reach another device: no remote copies, remote signals or barrier semaphores. Data moves between devices by JAX's collectives and lax.ppermute only.
A program may use at most 384 MiB of HBM per device.

```python
import math
import jax
import jax.numpy as jnp
import numpy as np
from jax import lax

D = 512
HEADS = 8
HD = 64
F = 2048
EXPERTS = 8
SEQ = 197
MICRO = 2
IMG_SLOT = 8
IMAGES_MB = 128
CAP = 630


def draw_held(key, part):
    key = jax.random.fold_in(key, 11)
    first, second = jax.random.split(key)
    groups = IMAGES_MB // IMG_SLOT
    total = MICRO * groups
    values = jax.random.randint(first, (total,), 1, IMG_SLOT + 1).astype(jnp.int32)
    where = jax.random.randint(second, (), 0, total).astype(jnp.int32)
    values = values.at[where].set(IMG_SLOT)
    values = values.at[(where + 1) % total].set(1)
    return values.reshape(MICRO, groups)


def block_levels(rng, shape, shards, low, high):
    def one(dim, shards_of):
        heights = jax.random.uniform(jax.random.fold_in(jax.random.fold_in(rng, 6), dim), (shards_of,), jnp.float32, low / len(shards), high / len(shards))
        return jnp.repeat(jnp.exp(heights), shape[dim] // shards_of).reshape((-1,) + (1,) * (len(shape) - dim - 1))

    loudness = one(*shards[0])
    for cut in shards[1:]:
        loudness = loudness * one(*cut)
    return loudness


def deal_out(stream_key, own, number, rows, count, top, reach, slope):
    ranking = jax.random.permutation(stream_key, count)
    crowded, ordinary = shares(count, rows * top, reach, slope, True), shares(count, rows * top, reach, slope, False)
    places = jnp.arange(count)

    def named(lengths, turn):
        used = int((lengths > 0).sum())
        fixed = max(1, used // 4)
        passed = fixed + (places - fixed + turn * (used - fixed)) % max(1, count - fixed)
        return jnp.zeros((count,), jnp.int32).at[ranking[jnp.where(places < fixed, places, passed)]].set(jnp.asarray(lengths, jnp.int32))

    lengths = jnp.where(number % 4 == 0, named(crowded, number // 4), named(ordinary, number - number // 4 - 1))
    mixed = jax.random.permutation(jax.random.fold_in(own, 3), count)
    giver, sink = mixed[0:count // 2 * 2:2], mixed[1:count // 2 * 2:2]
    margin = jnp.minimum(lengths[giver] - 1, reach - lengths[sink]) // 2
    margin = jnp.where((giver == ranking[0]) | (sink == ranking[0]) | (lengths[sink] == 0), 0, jnp.maximum(margin, 0))
    passed = jax.random.randint(jax.random.fold_in(own, 4), (count // 2,), 0, 1 << 20) % (margin + 1)
    lengths = lengths.at[giver].add(-passed).at[sink].add(passed)
    items = jnp.searchsorted(jnp.cumsum(lengths), jnp.arange(rows * top), side="right").astype(jnp.int32)
    listing = items.reshape(top, rows).T
    listing = listing[jax.random.permutation(jax.random.fold_in(own, 1), rows)]
    turn = jax.random.randint(jax.random.fold_in(own, 2), (rows, 1), 0, top)
    return jnp.take_along_axis(listing, (jnp.arange(top)[None, :] + turn) % top, axis=1)


def shares(number_of, total, limit, skew, full):
    weights = [(1 << 20) // math.isqrt(rank ** skew) + 1 for rank in range(1, number_of + 1)]
    largest = limit if full else min(limit, max(-(-total // number_of), total * weights[0] // sum(weights)))
    least = 1 if total - largest >= number_of - 1 else 0
    given, spare = [largest] + [least] * (number_of - 1), total - largest - least * (number_of - 1)
    while spare > 0:
        candidates = [i for i in range(1, number_of) if given[i] < largest] or [i for i in range(1, number_of) if given[i] < limit]
        pool, left = sum([weights[i] for i in candidates]), spare
        for i in candidates:
            extra = min(limit - given[i], max(1, left * weights[i] // pool), spare)
            given[i] = given[i] + extra
            spare = spare - extra
    return np.array(given)


def gaussian(own_key, shape, scale, reach, shards=(), kind=jnp.bfloat16):
    values = jax.random.normal(own_key, shape, jnp.float32) * scale
    if len(shards) > 0:
        values = block_levels(own_key, shape, shards, -0.22, 0.18) * values
    return jnp.clip(values, min=-reach, max=reach).astype(kind)


def setup_inputs(seed: int = 0) -> dict:
    splits = jax.random.split(jax.random.key(seed), 12)
    tokens = gaussian(splits[0], (MICRO, IMAGES_MB, SEQ, D), 1.0, 6.0, ((1, 16),))
    held = draw_held(jax.random.fold_in(splits[11], 71), 0)
    routes_keys = jax.random.split(jax.random.fold_in(splits[2], 1), MICRO * IMAGES_MB * SEQ // (IMG_SLOT * SEQ))
    routes_turns = jax.random.permutation(jax.random.fold_in(splits[2], 3), MICRO * IMAGES_MB * SEQ // (IMG_SLOT * SEQ))
    routes = jax.vmap(lambda own, number: deal_out(jax.random.fold_in(splits[2], 2), own, number, IMG_SLOT * SEQ, EXPERTS, 2, CAP, 2))(routes_keys, routes_turns).reshape((MICRO, IMAGES_MB, SEQ, 2))
    ln1_gain = jnp.clip(1.0 + 0.18 * jax.random.normal(splits[3], (D,), jnp.float32), 0.099609375, 1.8984375).astype(jnp.bfloat16)
    qkv_weight = gaussian(splits[4], (3, D, D), D ** -0.5, 0.25, ((1, 16), (2, 2)))
    out_weight = gaussian(splits[5], (D, D), (D // 16) ** -0.5, 1.0, ((0, 2), (1, 16)))
    ln2_gain = jnp.clip(1.0 + 0.18 * jax.random.normal(splits[6], (D,), jnp.float32), 0.099609375, 1.8984375).astype(jnp.bfloat16)
    router_weight = gaussian(splits[7], (D, EXPERTS), (4 * D) ** -0.5, 0.125, ((0, 16),))
    expert_in = gaussian(splits[8], (EXPERTS, D, F), D ** -0.5, 0.25, ((1, 16), (2, 2)))
    expert_out = gaussian(splits[9], (EXPERTS, F, D), (F // 2) ** -0.5, 0.1875, ((1, 2), (2, 16)))
    grad_out = gaussian(splits[10], (MICRO, IMAGES_MB, SEQ, D), 1.0, 6.0, ((1, 16),))
    return dict(tokens=tokens, held=held, routes=routes, ln1_gain=ln1_gain, qkv_weight=qkv_weight, out_weight=out_weight, ln2_gain=ln2_gain, router_weight=router_weight, expert_in=expert_in, expert_out=expert_out, grad_out=grad_out)


@jax.custom_vjp
def low(v):
    return lax.optimization_barrier(v.astype(jnp.bfloat16)).astype(jnp.float32)

@jax.custom_vjp
def low_back(v):
    return v

def low_keep(v):
    return (low(v), None)

def low_pass(kept, grad):
    return (grad,)

def back_keep(v):
    return (v, None)

def back_low(kept, grad):
    return (low(grad),)
low.defvjp(low_keep, low_pass)
low_back.defvjp(back_keep, back_low)

def highest(spec, left, right):
    return jnp.einsum(spec, left, right, precision=lax.Precision.HIGHEST)

def normalize(values):
    centre = values - lax.optimization_barrier(jnp.mean(values, -1, keepdims=True))
    spread = lax.optimization_barrier(jnp.mean(centre * centre, -1, keepdims=True))
    return centre * lax.rsqrt(spread + 1e-06)

def route_slots(chosen, experts):
    flat = chosen.reshape(-1)
    onehot = (flat[:, None] == jnp.arange(experts, dtype=jnp.int32)[None, :]).astype(jnp.int32)
    before = jnp.cumsum(onehot, 0) - onehot
    place = lax.optimization_barrier(jnp.sum(before * onehot, 1)).astype(jnp.int32)
    owner = jnp.zeros((experts, CAP), jnp.int32).at[flat, place].set(jnp.arange(flat.shape[0], dtype=jnp.int32) // 2)
    return (flat, place, owner)

def block_forward(params, block_rows, chosen, live_rows):
    gain1, w_qkv, w_out, gain2, w_router, w_in, w_back = params
    rows = IMG_SLOT * SEQ
    inputs = block_rows.reshape(rows, D)
    act1 = low(normalize(inputs) * gain1)
    proj = low(low_back(highest('rd,jdc->jrc', act1, w_qkv)))
    split = proj.reshape(3, IMG_SLOT, SEQ, HEADS, HD)
    scores = low_back(HD ** (-0.5) * highest('ishd,ithd->ihst', split[0], split[1]))
    probs = low(jax.nn.softmax(scores, -1))
    attended = low(low_back(highest('ihst,ithd->ishd', probs, split[2]).reshape(rows, D)))
    branch = low_back(highest('rc,cd->rd', attended, w_out))
    middle = inputs + branch
    act2 = low(normalize(middle) * gain2)
    logits = highest('rd,de->re', act2, w_router)
    gates = jax.nn.softmax(jnp.take_along_axis(logits, chosen, 1), -1)
    flat, place, owner = route_slots(chosen, EXPERTS)
    inner = low_back(highest('ecd,edf->ecf', act2[owner], w_in))
    hidden = low(jax.nn.gelu(inner, approximate=False))
    result = low_back(highest('ecf,efd->ecd', hidden, w_back))
    per_route = result[flat, place].reshape(rows, 2, D)
    mixed = lax.optimization_barrier(jnp.sum(gates[:, :, None] * per_route, 1))
    return ((middle + mixed) * live_rows).reshape(IMG_SLOT, SEQ, D)

def reference(tokens, held, routes, ln1_gain, qkv_weight, out_weight, ln2_gain, router_weight, expert_in, expert_out, grad_out):
    groups = IMAGES_MB // IMG_SLOT
    count = MICRO * groups
    live = (jnp.arange(IMG_SLOT, dtype=jnp.int32)[None, None, :] < held[:, :, None]).astype(jnp.float32)
    live_rows = jnp.broadcast_to(live.reshape(count, IMG_SLOT, 1), (count, IMG_SLOT, SEQ)).reshape(count, IMG_SLOT * SEQ, 1)
    chosen = routes.reshape(count, IMG_SLOT * SEQ, 2).astype(jnp.int32)
    params = tuple((w.astype(jnp.float32) for w in (ln1_gain, qkv_weight, out_weight, ln2_gain, router_weight, expert_in, expert_out)))
    inputs = tokens.astype(jnp.float32)

    def forward(values, weights):
        blocks = values.reshape(count, IMG_SLOT, SEQ, D)
        step_fn = jax.checkpoint(lambda item: block_forward(weights, item[0], item[1], item[2]))
        outputs = lax.map(step_fn, (blocks, chosen, live_rows))
        return outputs.reshape(MICRO, IMAGES_MB, SEQ, D)
    result, pullback = jax.vjp(forward, inputs, params)
    grad_inputs, grad_params = pullback(grad_out.astype(jnp.float32))
    return (result.astype(jnp.bfloat16), grad_inputs.astype(jnp.bfloat16), grad_params[0], grad_params[1], grad_params[2], grad_params[3], grad_params[4], grad_params[5], grad_params[6])
```

```python
import functools

import jax
import jax.numpy as jnp
from jax import lax
from jax.experimental import pallas as pl
from jax.experimental.pallas import tpu as pltpu
from jax.sharding import PartitionSpec as P

F32 = jnp.float32
BF16 = jnp.bfloat16
HD = 64
SEQ = 197
ROWS = 208
SLOTS = 1280
SPAN = 1536
WIN = 128
TILE = 256
EXPERTS = 8
LANES = 128
GROUP = 1
VMEM = 58 * 1024 * 1024

LIVE, START, TOTAL, TABLE = 8, 32, 160, 256


def nt(a, b):
    return lax.dot_general(a, b, (((1,), (1,)), ((), ())), preferred_element_type=F32)


def tn(a, b):
    return lax.dot_general(a, b, (((0,), (0,)), ((), ())), preferred_element_type=F32)


def mm(a, b):
    return jnp.dot(a, b, preferred_element_type=F32)


def iota(shape, dim):
    return lax.broadcasted_iota(jnp.int32, shape, dim)


def layer_stats(values):
    centre = values - jnp.mean(values, -1, keepdims=True)
    factor = lax.rsqrt(jnp.mean(centre * centre, -1, keepdims=True) + 1e-06)
    return centre * factor, factor


def norm_back(grad, normed, factor):
    return factor * (
        grad - jnp.mean(grad, -1, keepdims=True) - normed * jnp.mean(grad * normed, -1, keepdims=True)
    )


def gelu_both(u):
    a = jnp.abs(u) * 0.7071067811865476
    t = 1.0 / (1.0 + 0.3275911 * a)
    bell = jnp.exp(-a * a)
    poly = t * (
        0.127414796 + t * (-0.142248368 + t * (0.7107068705 + t * (-0.7265760135 + t * 0.5307027145)))
    )
    tail = poly * bell
    phi = jnp.where(u >= 0.0, 1.0 - tail, tail)
    return u * phi, phi + u * bell * 0.3989422804014327


def split_low(values):
    high = values.astype(BF16).astype(F32)
    return high, values - high


def load_weights(info, parts, weights, sems, rel, rows):
    c, me = info[0], info[1]
    copies = []
    for side, part in enumerate(parts):
        t = c ^ side
        for k, r in enumerate(rel):
            where = pl.multiple_of((me ^ r) * rows, 16)
            copies.append(
                pltpu.make_async_copy(part.at[k], weights.at[t, pl.ds(where, rows), :], sems.at[side, k])
            )
    for copy in copies:
        copy.start()
    for copy in copies:
        copy.wait()


def head_mask(which):
    lane = iota((ROWS, LANES), 1)
    return (lane < HD) if which == 0 else (lane >= HD)


def forward_kernel(rel, rows, info, tok, mask, *refs):
    i = pl.program_id(0)
    w_parts, refs = refs[:-10], refs[-10:]
    src, mid, proj, att, lse, gates, weights, gains, xs, sems = refs
    shares, _, cols = weights.shape
    local = (cols - LANES) // 4
    aux_at = 4 * local

    @pl.when(i == 0)
    def _():
        load_weights(info, w_parts, weights, sems, rel, rows)
        gains[...] = weights[0, :, aux_at:].astype(F32).T[0:16, :]

    @pl.when(info[LIVE + i] == 1)
    def _():
        xs[192:ROWS, :] = jnp.zeros((ROWS - 192, 512), F32)
        xs[0:SEQ, :] = tok[0, 0].astype(F32)
        x = xs[...]
        normed, _ = layer_stats(x)
        act = (normed * gains[8:9, :]).astype(BF16)
        for t in range(shares):
            proj[0, :, t * 3 * local : (t + 1) * 3 * local] = mm(act, weights[t, :, 0 : 3 * local]).astype(BF16)
        key_ok = iota((ROWS, ROWS), 1) < SEQ
        lane = iota((ROWS, LANES), 1)
        saved = jnp.zeros((ROWS, LANES), F32)
        for t in range(shares):
            for p in range(local // LANES):
                at = t * 3 * local + p * LANES
                q = proj[0, :, at : at + LANES]
                k = proj[0, :, at + local : at + local + LANES]
                v = proj[0, :, at + 2 * local : at + 2 * local + LANES]
                halves = []
                for h in range(2):
                    qm = jnp.where(head_mask(h), q.astype(F32), 0.0).astype(BF16)
                    s = jnp.where(key_ok, nt(qm, k) * (HD**-0.5), -1e30)
                    top = jnp.max(s, -1, keepdims=True)
                    e = jnp.exp(s - top)
                    total = jnp.sum(e, -1, keepdims=True)
                    probs = (e * (1.0 / total)).astype(BF16)
                    halves.append(mm(probs, v))
                    saved = jnp.where(lane == (t * local + p * LANES) // HD + h, top + jnp.log(total), saved)
                att[0, :, t * local + p * LANES : t * local + (p + 1) * LANES] = jnp.where(
                    lane < HD, halves[0], halves[1]
                ).astype(BF16)
        lse[0] = saved
        branch = nt(att[0, :, 0:local], weights[0, :, 3 * local : aux_at])
        for t in range(1, shares):
            branch = branch + nt(att[0, :, t * local : (t + 1) * local], weights[t, :, 3 * local : aux_at])
        middle = x + branch
        mid[0] = middle
        normed2, _ = layer_stats(middle)
        act2 = (normed2 * gains[9:10, :]).astype(BF16)
        src[0, :, 0:512] = act2
        chosen = mask[0, 0].astype(F32)
        logits = jnp.where(chosen > 0.0, mm(act2, weights[0, :, aux_at:]), -1e30)
        top = jnp.max(logits, -1, keepdims=True)
        e = jnp.exp(logits - top) * chosen
        gate = e / jnp.maximum(jnp.sum(e, -1, keepdims=True), 0.5)
        gates[0] = gate
        high, low = split_low(gate)
        src[0, :, 512:640] = (high + pltpu.roll(low, 8, 1)).astype(BF16)


def dispatch_kernel(count, info, own, oth, gy, mask, x_hbm, xbuf, tbuf, pbuf, sems):
    i = pl.program_id(0)

    @pl.when(i == 0)
    def _():
        for e in range(EXPERTS):

            @pl.loop(0, SPAN // TILE)
            def _(k):
                xbuf[e, pl.ds(pl.multiple_of(k * TILE, TILE), TILE), :] = jnp.zeros((TILE, 1152), BF16)

        tbuf[...] = jnp.zeros(tbuf.shape, BF16)
        pbuf[...] = jnp.full(pbuf.shape, -4096.0, F32)

    @pl.when(info[LIVE + i] == 1)
    def _():
        @pl.when(i < count)
        def _():
            tbuf[0:ROWS, 0:512] = own[0, :, 0:512]
            tbuf[0:ROWS, 1024:1152] = own[0, :, 512:640]

        @pl.when(i >= count)
        def _():
            tbuf[0:ROWS, 0:512] = oth[0, :, 0:512]
            tbuf[0:ROWS, 1024:1152] = oth[0, :, 512:640]

        tbuf[0:SEQ, 512:1024] = gy[0, 0]
        chosen = mask[0, 0]
        lower = (iota((ROWS, ROWS), 0) > iota((ROWS, ROWS), 1)).astype(F32).astype(BF16)
        pbuf[0:ROWS, :] = jnp.where(chosen.astype(F32) > 0.0, mm(lower, chosen), -4096.0)
        place = pbuf[...].T
        slot = iota((WIN, TILE), 0).astype(F32)

        def window(w):
            picks = []
            for e in range(EXPERTS):
                off = (info[START + i * 8 + e] % 16 - WIN * w).astype(F32)
                picks.append(jnp.where(slot == place[e : e + 1, :] + off, 1.0, 0.0).astype(BF16))
            pick = jnp.concatenate(picks, 0)
            for n in range(3):
                cols = slice(n * 384, (n + 1) * 384)
                part = mm(pick, tbuf[:, cols]).astype(BF16)
                for e in range(EXPERTS):
                    first = pl.multiple_of(info[START + i * 8 + e] // 16 * 16 + WIN * w, 16)
                    rows = pl.ds(first, WIN)
                    xbuf[e, rows, cols] = xbuf[e, rows, cols] + part[e * WIN : (e + 1) * WIN]

        window(0)

        @pl.when(needs_second(info, i))
        def _():
            window(1)

    @pl.when(i == 15)
    def _():
        for start in (True, False):
            for e in range(EXPERTS):
                for k in range(SLOTS // TILE):

                    @pl.when(k * TILE < info[TOTAL + e])
                    def _():
                        rows = pl.ds(k * TILE, TILE)
                        copy = pltpu.make_async_copy(xbuf.at[e, rows, :], x_hbm.at[e, rows, :], sems.at[e, k])
                        if start:
                            copy.start()
                        else:
                            copy.wait()


def window_end(info, i, e):
    begin = info[START + i * 8 + e]
    end = info[START + i * 8 + 8 + e]
    return end - begin // 16 * 16


def needs_second(info, i):
    most = window_end(info, i, 0)
    for e in range(1, EXPERTS):
        most = jnp.maximum(most, window_end(info, i, e))
    return most > WIN


def expert_kernel(
    first, rel_in, rel_out, order_in, order_out, rows, n_in, n_out, info, x, *refs
):
    pieces_in, refs = refs[:n_in], refs[n_in:]
    pieces_out, refs = refs[:n_out], refs[n_out:]
    n_grad = 1 if len(rel_in) == 1 else 2
    y = refs[0]
    grads_in, grads_out = refs[1 : 1 + n_grad], refs[1 + n_grad : 1 + 2 * n_grad]
    w_in, w_out, acc_in, acc_out, sems = refs[1 + 2 * n_grad :]
    e, t = pl.program_id(0), pl.program_id(1)
    expert = first + e
    me = info[1]

    @pl.when(t == 0)
    def _():
        copies = []
        for side, (pieces, rel, buf) in enumerate(((pieces_in, rel_in, w_in), (pieces_out, rel_out, w_out))):
            k = 0
            for piece in pieces:
                for b in range(piece.shape[0]):
                    where = pl.multiple_of((me ^ rel[k]) * rows, 16)
                    copies.append(
                        pltpu.make_async_copy(piece.at[b, e], buf.at[pl.ds(where, rows), :], sems.at[side, k])
                    )
                    k += 1
        for copy in copies:
            copy.start()
        for copy in copies:
            copy.wait()
        acc_in[...] = jnp.zeros(acc_in.shape, F32)
        acc_out[...] = jnp.zeros(acc_out.shape, F32)

    @pl.when(t * TILE < info[TOTAL + expert])
    def _():
        rows_x = x[0, :, 0:512]
        rows_g = x[0, :, 512:1024]
        lane = iota((TILE, LANES), 1)
        mine = (lane == expert) | (lane == expert + 8)
        gate = jnp.sum(jnp.where(mine, x[0, :, 1024:1152].astype(F32), 0.0), -1, keepdims=True)
        inner = mm(rows_x, w_in[...])
        act, slope = gelu_both(inner)
        hid = act.astype(BF16)
        out = nt(hid, w_out[...])
        g = rows_g.astype(F32)
        deo = (gate * g).astype(BF16)
        dinner = (mm(deo, w_out[...]) * slope).astype(BF16)
        dgate = jnp.sum(g * out, -1, keepdims=True)
        high, low = split_low(dgate)
        y[0, :, 0:512] = (gate * out).astype(BF16)
        y[0, :, 512:1024] = nt(dinner, w_in[...]).astype(BF16)
        y[0, :, 1024:1152] = jnp.where(
            lane == expert, high, jnp.where(lane == expert + 8, low, 0.0)
        ).astype(BF16)
        acc_in[...] += tn(rows_x, dinner)
        acc_out[...] += tn(deo, hid)

    @pl.when(t == pl.num_programs(1) - 1)
    def _():
        for acc, outs, order in ((acc_in, grads_in, order_in), (acc_out, grads_out, order_out)):
            half = len(order) // len(outs)
            for k, r in enumerate(order):
                where = pl.multiple_of((me ^ r) * rows, 16)
                outs[k // half][k % half, 0] = acc[pl.ds(where, rows), :].astype(BF16)


def combine_kernel(base, info, y_hbm, mask, out, ybuf, acc, sems):
    i = pl.program_id(0)
    slot = i % 2

    def copies(j, buf, w):
        for e in range(EXPERTS):
            first = pl.multiple_of(info[START + (base + j) * 8 + e] // 16 * 16 + WIN * w, 16)
            yield pltpu.make_async_copy(
                y_hbm.at[e, pl.ds(first, WIN), :],
                ybuf.at[buf, pl.ds(e * WIN, WIN), :],
                sems.at[buf, e],
            )

    def fetch(j, buf):
        @pl.when(info[LIVE + base + j] == 1)
        def _():
            for copy in copies(j, buf, 0):
                copy.start()

    @pl.when(i == 0)
    def _():
        fetch(i, slot)

    @pl.when(i + 1 < pl.num_programs(0))
    def _():
        fetch(i + 1, 1 - slot)

    @pl.when(info[LIVE + base + i] == 1)
    def _():
        for copy in copies(i, slot, 0):
            copy.wait()
        chosen = mask[0, 0]
        lower = (iota((ROWS, ROWS), 0) > iota((ROWS, ROWS), 1)).astype(F32).astype(BF16)
        place = jnp.where(chosen.astype(F32) > 0.0, mm(lower, chosen), -4096.0)
        lane = iota((ROWS, WIN), 1).astype(F32)

        def window(w):
            picks = []
            for e in range(EXPERTS):
                begin = info[START + (base + i) * 8 + e]
                limit = info[TOTAL + e] - begin // 16 * 16 - WIN * w

                @pl.when(limit < WIN)
                def _():
                    part = ybuf[slot, e * WIN : (e + 1) * WIN, :].astype(F32)
                    keep = iota((WIN, 1152), 0) < limit
                    ybuf[slot, e * WIN : (e + 1) * WIN, :] = jnp.where(keep, part, 0.0).astype(BF16)

                off = (begin % 16 - WIN * w).astype(F32)
                picks.append(jnp.where(lane == place[:, e : e + 1] + off, 1.0, 0.0).astype(BF16))
            return mm(jnp.concatenate(picks, 1), ybuf[slot])

        acc[...] = window(0)

        @pl.when(needs_second(info, base + i))
        def _():
            for copy in copies(i, slot, 1):
                copy.start()
            for copy in copies(i, slot, 1):
                copy.wait()
            acc[...] += window(1)

        if out.dtype == F32:
            out[0] = acc[...]
        else:
            out[0, :, 0:1024] = acc[:, 0:1024].astype(BF16)
            aux = acc[:, 1024:1152]
            both = jnp.where(iota((ROWS, LANES), 1) < 8, aux + pltpu.roll(aux, LANES - 8, 1), 0.0)
            high, low = split_low(both)
            out[0, :, 1024:1152] = (high + pltpu.roll(low, 8, 1)).astype(BF16)


def backward_kernel(
    rel,
    order,
    rows,
    info,
    tok,
    gy_ref,
    comb_own,
    comb_oth,
    mid,
    proj,
    att,
    lse,
    gates,
    *refs,
):
    i = pl.program_id(0)
    c, me = info[0], info[1]
    scratch, refs = refs[-11:], refs[:-11]
    weights, gains, twice, xs, gs, dproj, acc_qkv, acc_out, acc_router, acc_gain, sems = scratch
    shares, _, cols = weights.shape
    w_parts, refs = refs[:shares], refs[shares:]
    block_out, grad_tok = refs[:2]
    grads = refs[2:]
    local = (cols - LANES) // 4
    aux_at = 4 * local

    @pl.when(i == 0)
    def _():
        load_weights(info, w_parts, weights, sems, rel, rows)
        aux = weights[0, :, aux_at:].astype(F32)
        gains[...] = aux.T[0:16, :]
        lane = iota((512, LANES), 1)
        router = jnp.where(lane < 8, aux, 0.0)
        twice[...] = (router + pltpu.roll(router, 8, 1)).astype(BF16)
        acc_qkv[...] = jnp.zeros(acc_qkv.shape, F32)
        acc_out[...] = jnp.zeros(acc_out.shape, F32)
        acc_router[...] = jnp.zeros(acc_router.shape, F32)
        acc_gain[...] = jnp.zeros(acc_gain.shape, F32)

    @pl.when(info[LIVE + i] == 0)
    def _():
        block_out[...] = jnp.zeros(block_out.shape, BF16)
        grad_tok[...] = jnp.zeros(grad_tok.shape, BF16)

    @pl.when(info[LIVE + i] == 1)
    def _():
        xs[192:ROWS, :] = jnp.zeros((ROWS - 192, 512), F32)
        xs[0:SEQ, :] = tok[0, 0].astype(F32)
        gs[192:ROWS, :] = jnp.zeros((ROWS - 192, 512), F32)
        gs[0:SEQ, :] = gy_ref[0, 0].astype(F32)
        gy = gs[...]
        lane = iota((ROWS, LANES), 1)
        middle = mid[0]
        mixed = comb_own[0, :, 0:512] + comb_oth[0, :, 0:512].astype(F32)
        block_out[0] = (middle + mixed)[0:SEQ, :].astype(BF16)
        normed2, factor2 = layer_stats(middle)
        act2 = (normed2 * gains[9:10, :]).astype(BF16)
        gate = gates[0]
        aux = comb_own[0, :, 1024:1152] + comb_oth[0, :, 1024:1152].astype(F32)
        dgate = jnp.where(lane < 8, aux + pltpu.roll(aux, LANES - 8, 1), 0.0)
        dlogits = gate * (dgate - jnp.sum(gate * dgate, -1, keepdims=True))
        high, low = split_low(dlogits)
        packed = (high + pltpu.roll(low, 8, 1)).astype(BF16)
        acc_router[...] += tn(act2, packed)
        dact2 = (
            comb_own[0, :, 512:1024] + comb_oth[0, :, 512:1024].astype(F32) + nt(packed, twice[...])
        )
        acc_gain[9:10, :] += jnp.sum(dact2 * normed2, 0, keepdims=True)
        dmiddle = gy + norm_back(dact2 * gains[9:10, :], normed2, factor2)
        gs[...] = dmiddle
        dbranch = dmiddle.astype(BF16)
        x = xs[...]
        normed1, factor1 = layer_stats(x)
        act1 = (normed1 * gains[8:9, :]).astype(BF16)
        key_ok = iota((ROWS, ROWS), 1) < SEQ
        for t in range(shares):
            acc_out[t] += tn(dbranch, att[0, :, t * local : (t + 1) * local])
            datt_t = mm(dbranch, weights[t, :, 3 * local : aux_at]).astype(BF16)
            for p in range(local // LANES):
                at = t * 3 * local + p * LANES
                q = proj[0, :, at : at + LANES]
                k = proj[0, :, at + local : at + local + LANES]
                v = proj[0, :, at + 2 * local : at + 2 * local + LANES]
                datt = datt_t[:, p * LANES : (p + 1) * LANES]
                parts = []
                for h in range(2):
                    qm = jnp.where(head_mask(h), q.astype(F32), 0.0).astype(BF16)
                    dm = jnp.where(head_mask(h), datt.astype(F32), 0.0).astype(BF16)
                    head = (t * local + p * LANES) // HD + h
                    s = nt(qm, k) * (HD**-0.5) - lse[0, :, head : head + 1]
                    probs = jnp.where(key_ok, jnp.exp(jnp.where(key_ok, s, 0.0)), 0.0)
                    dprobs = nt(dm, v)
                    ds = (probs * (dprobs - jnp.sum(dprobs * probs, -1, keepdims=True))).astype(BF16)
                    parts.append((mm(ds, k), tn(ds, q), tn(probs.astype(BF16), datt)))
                for j in range(3):
                    both = jnp.where(lane < HD, parts[0][j], parts[1][j])
                    if j < 2:
                        both = both * (HD**-0.5)
                    dproj[:, at + j * local : at + j * local + LANES] = both.astype(BF16)
        dact1 = jnp.zeros((ROWS, 512), F32)
        for t in range(shares):
            dp = dproj[:, t * 3 * local : (t + 1) * 3 * local]
            acc_qkv[t] += tn(act1, dp)
            dact1 = dact1 + nt(dp, weights[t, :, 0 : 3 * local])
        acc_gain[8:9, :] += jnp.sum(dact1 * normed1, 0, keepdims=True)
        total = gs[...] + norm_back(dact1 * gains[8:9, :], normed1, factor1)
        grad_tok[0] = total[0:SEQ, :].astype(BF16)

    @pl.when(i == pl.num_programs(0) - 1)
    def _():
        lane = iota((512, LANES), 1)
        router = acc_router[...]
        aux = jnp.where(lane < 8, router + pltpu.roll(router, LANES - 8, 1), acc_gain[...].T)
        acc_router[...] = aux
        for k, r in enumerate(order):
            where = pl.ds(pl.multiple_of((me ^ r) * rows, 16), rows)
            for side, out in enumerate(grads):
                out[k, :, 0 : 3 * local] = acc_qkv[c ^ side, where, :].astype(BF16)
                out[k, :, 3 * local : aux_at] = acc_out[c ^ side, where, :].astype(BF16)
                out[k, :, aux_at:] = acc_router[where, :].astype(BF16)


def swap(n, bit):
    return [(i, i ^ bit) for i in range(n)]


def relatives(order):
    rel = [0]
    for bit in order:
        rel = rel + [r ^ (1 << bit) for r in rel]
    return tuple(rel)


def scatter_order(order):
    out = [0]
    for bit in reversed(order):
        out = out + [r ^ (1 << bit) for r in out]
    return tuple(out)


def hyper_gather(shard, order, n):
    pieces = [shard[None]]
    for bit in order:
        send = pieces[0] if len(pieces) == 1 else jnp.concatenate(pieces, 0)
        pieces.append(lax.ppermute(send, "dp", swap(n, 1 << bit)))
    return pieces


def hyper_scatter(keep, send, order, n):
    for step, bit in enumerate(order):
        got = lax.ppermute(send, "dp", swap(n, 1 << bit))
        if step == len(order) - 1:
            return (keep.astype(F32) + got.astype(F32))[0]
        half = keep.shape[0] // 2
        send = keep[half:] + got[half:]
        keep = keep[:half] + got[:half]


def any_spec():
    return pl.BlockSpec(memory_space=pl.ANY)


def params():
    return pltpu.CompilerParams(vmem_limit_bytes=VMEM)


def shape(s, d):
    return jax.ShapeDtypeStruct(s, d)


def body(
    n,
    shares,
    tokens,
    held,
    routes,
    ln1_gain,
    qkv_weight,
    out_weight,
    ln2_gain,
    router_weight,
    expert_in,
    expert_out,
    grad_out,
):
    rows = qkv_weight.shape[1]
    width = expert_in.shape[2]
    local = qkv_weight.shape[2]
    pack = 4 * local + LANES
    mine_count = 16 // shares
    per_micro = 8 // shares
    fast = rows % 16 == 0 and n & (n - 1) == 0
    c = lax.axis_index("tensor")
    me = lax.axis_index("dp")
    bits = n.bit_length() - 1
    if fast:
        order_a = tuple(reversed(range(bits)))
        order_b = order_a[:-2] + (order_a[-1], order_a[-2])
        block = rows
    else:
        order_a = order_b = ()
        block = 512
    rel_a, rel_b = relatives(order_a), relatives(order_b)
    back_a, back_b = tuple(reversed(order_a)), tuple(reversed(order_b))
    scat_a, scat_b = scatter_order(back_a), scatter_order(back_b)
    blocks = len(rel_a)

    aux = jnp.concatenate(
        [router_weight, ln1_gain[:, None], ln2_gain[:, None], jnp.zeros((rows, LANES - 10), BF16)], 1
    )
    small = jnp.concatenate([qkv_weight[0], qkv_weight[1], qkv_weight[2], out_weight.T, aux], 1)
    if fast:
        w_own = jnp.concatenate(hyper_gather(small, order_a, n), 0)
    else:
        w_own = lax.all_gather(small, "dp", axis=0, tiled=True)[None]

    def across(a, r):
        return lax.ppermute(a, "tensor", swap(shares, r))

    w_parts = [w_own] + [across(w_own, r) for r in range(1, shares)]

    weights = []
    back = jnp.swapaxes(expert_out, 1, 2)
    for at in range(0, EXPERTS, GROUP):
        pair = []
        for shard, order in ((expert_in[at : at + GROUP], order_a), (back[at : at + GROUP], order_b)):
            if fast:
                pair.append(hyper_gather(shard, order, n))
            else:
                pair.append([lax.all_gather(shard, "dp", axis=1, tiled=True)[None]])
        weights.append(pair)

    live = jnp.arange(8, dtype=jnp.int32)[None, :] < held
    lane = jnp.arange(LANES, dtype=jnp.int32)
    picked = (routes[..., 0:1] == lane) | (routes[..., 1:2] == lane)
    picked = (picked & live[:, :, None, None]).astype(BF16)
    mask = jnp.pad(picked, ((0, 0), (0, 0), (0, ROWS - SEQ), (0, 0)))
    counts = jnp.sum(
        (routes[..., None] == jnp.arange(EXPERTS, dtype=jnp.int32)).astype(jnp.int32), (2, 3)
    ) * live.astype(jnp.int32)[:, :, None]

    def own_first(a):
        a = a.reshape((2, per_micro, shares) + a.shape[2:])
        out = []
        for r in range(shares):
            part = a[:, :, 0]
            for t in range(1, shares):
                part = jnp.where(c ^ r == t, a[:, :, t], part)
            out.append(part.reshape((mine_count,) + a.shape[3:]))
        return jnp.concatenate(out, 0)

    counts = own_first(counts)
    live_list = own_first(live.astype(jnp.int32))
    ends = jnp.sum(
        jnp.where(jnp.arange(16)[:, None, None] >= jnp.arange(16)[None, :, None], counts[None], 0), 1
    )
    info = jnp.concatenate(
        [
            jnp.stack([c, me]).astype(jnp.int32),
            jnp.zeros((LIVE - 2,), jnp.int32),
            live_list,
            jnp.zeros((START - LIVE - 16,), jnp.int32),
            (ends - counts).reshape(-1),
            ends[15],
            jnp.zeros((TABLE - TOTAL - EXPERTS,), jnp.int32),
        ]
    )

    def image(i, s):
        j = i % mine_count
        return (j // per_micro, shares * (j % per_micro) + (s[0] ^ (i // mine_count)), 0, 0)

    tok_spec = pl.BlockSpec((1, 1, SEQ, 512), image)
    mask_spec = pl.BlockSpec((1, 1, ROWS, LANES), image)

    def row_spec(cols):
        return pl.BlockSpec((1, ROWS, cols), lambda i, s: (i, 0, 0))

    src, mid, proj, att, lse, gates = pl.pallas_call(
        functools.partial(forward_kernel, rel_a, block),
        grid_spec=pltpu.PrefetchScalarGridSpec(
            num_scalar_prefetch=1,
            grid=(mine_count,),
            in_specs=[tok_spec, mask_spec] + [any_spec()] * shares,
            out_specs=[row_spec(640), row_spec(512), row_spec(1536), row_spec(512), row_spec(LANES), row_spec(LANES)],
            scratch_shapes=[
                pltpu.VMEM((shares, 512, pack), BF16),
                pltpu.VMEM((16, 512), F32),
                pltpu.VMEM((ROWS, 512), F32),
                pltpu.SemaphoreType.DMA((shares, blocks)),
            ],
        ),
        out_shape=[
            shape((mine_count, ROWS, 640), BF16),
            shape((mine_count, ROWS, 512), F32),
            shape((mine_count, ROWS, 1536), BF16),
            shape((mine_count, ROWS, 512), BF16),
            shape((mine_count, ROWS, LANES), F32),
            shape((mine_count, ROWS, LANES), F32),
        ],
        compiler_params=params(),
        cost_estimate=pl.CostEstimate(flops=15 * 10**9, bytes_accessed=20 * 10**6, transcendentals=3 * 10**6),
        name="forward",
    )(info, tokens, mask, *w_parts)

    src_oth = [across(src, r) for r in range(1, shares)]
    src_oth = src_oth[0] if shares == 2 else jnp.concatenate(src_oth, 0)

    rows_x = pl.pallas_call(
        functools.partial(dispatch_kernel, mine_count),
        grid_spec=pltpu.PrefetchScalarGridSpec(
            num_scalar_prefetch=1,
            grid=(16,),
            in_specs=[
                pl.BlockSpec((1, ROWS, 640), lambda i, s: (jnp.minimum(i, mine_count - 1), 0, 0)),
                pl.BlockSpec((1, ROWS, 640), lambda i, s: (jnp.maximum(i - mine_count, 0), 0, 0)),
                tok_spec,
                mask_spec,
            ],
            out_specs=any_spec(),
            scratch_shapes=[
                pltpu.VMEM((EXPERTS, SPAN, 1152), BF16),
                pltpu.VMEM((TILE, 1152), BF16),
                pltpu.VMEM((TILE, LANES), F32),
                pltpu.SemaphoreType.DMA((EXPERTS, SLOTS // TILE)),
            ],
        ),
        out_shape=shape((EXPERTS, SLOTS, 1152), BF16),
        compiler_params=params(),
        cost_estimate=pl.CostEstimate(flops=12 * 10**9, bytes_accessed=30 * 10**6, transcendentals=0),
        name="dispatch",
    )(info, src, src_oth, grad_out, mask)

    tiles = SLOTS // TILE
    y_parts = []
    shards_in, shards_out = [], []
    for number, at in enumerate(range(0, EXPERTS, GROUP)):
        pieces_in, pieces_out = weights[number]

        def tile_at(e, t, s, at=at):
            last = jnp.maximum((s[TOTAL + at + e] + TILE - 1) // TILE - 1, 0)
            return jnp.minimum(t, last)

        halves = [blocks // 2] * 2 if blocks > 1 else [1]
        grad_specs = [pl.BlockSpec((h, 1, block, width), lambda e, t, s: (0, e, 0, 0)) for h in halves]
        grad_shapes = [shape((h, GROUP, block, width), BF16) for h in halves]
        got = pl.pallas_call(
            functools.partial(
                expert_kernel, at, rel_a, rel_b, scat_a, scat_b, block, len(pieces_in), len(pieces_out)
            ),
            grid_spec=pltpu.PrefetchScalarGridSpec(
                num_scalar_prefetch=1,
                grid=(GROUP, tiles),
                in_specs=[pl.BlockSpec((1, TILE, 1152), lambda e, t, s, at=at, f=tile_at: (at + e, f(e, t, s), 0))]
                + [any_spec()] * (len(pieces_in) + len(pieces_out)),
                out_specs=[pl.BlockSpec((1, TILE, 1152), lambda e, t, s, f=tile_at: (e, f(e, t, s), 0))]
                + grad_specs
                + grad_specs,
                scratch_shapes=[
                    pltpu.VMEM((512, width), BF16),
                    pltpu.VMEM((512, width), BF16),
                    pltpu.VMEM((512, width), F32),
                    pltpu.VMEM((512, width), F32),
                    pltpu.SemaphoreType.DMA((2, blocks)),
                ],
            ),
            out_shape=[shape((GROUP, SPAN, 1152), BF16)] + grad_shapes + grad_shapes,
            compiler_params=params(),
            cost_estimate=pl.CostEstimate(
                flops=GROUP * 5 * 10**9, bytes_accessed=GROUP * 12 * 10**6, transcendentals=GROUP * 10**6
            ),
            name="expert",
        )(info, rows_x, *pieces_in, *pieces_out)
        y_parts.append(got[0])
        if fast:
            shards_in.append(hyper_scatter(got[1], got[2], back_a, n))
            shards_out.append(hyper_scatter(got[3], got[4], back_b, n))
        else:
            shards_in.append(lax.psum_scatter(got[1][0], "dp", scatter_dimension=1, tiled=True).astype(F32))
            shards_out.append(lax.psum_scatter(got[2][0], "dp", scatter_dimension=1, tiled=True).astype(F32))
    rows_y = jnp.concatenate(y_parts, 0)

    def combine(base, dtype):
        return pl.pallas_call(
            functools.partial(combine_kernel, base),
            grid_spec=pltpu.PrefetchScalarGridSpec(
                num_scalar_prefetch=1,
                grid=(mine_count,),
                in_specs=[
                    any_spec(),
                    pl.BlockSpec((1, 1, ROWS, LANES), lambda i, s: image(i + base, s)),
                ],
                out_specs=row_spec(1152),
                scratch_shapes=[
                    pltpu.VMEM((2, EXPERTS * WIN, 1152), BF16),
                    pltpu.VMEM((ROWS, 1152), F32),
                    pltpu.SemaphoreType.DMA((2, EXPERTS)),
                ],
            ),
            out_shape=shape((mine_count, ROWS, 1152), dtype),
            compiler_params=params(),
            cost_estimate=pl.CostEstimate(flops=5 * 10**9, bytes_accessed=25 * 10**6, transcendentals=0),
            name="combine",
        )(info, rows_y, mask)

    comb_oth = [across(combine(mine_count * r, BF16), r) for r in range(1, shares)]
    comb_oth = comb_oth[0] if shares == 2 else sum(a.astype(F32) for a in comb_oth).astype(BF16)
    comb_own = combine(0, F32)

    small_spec = pl.BlockSpec((blocks, block, pack), lambda i, s: (0, 0, 0))
    tok_out = pl.BlockSpec((1, SEQ, 512), lambda i, s: (i, 0, 0))
    out_own, tok_own, *grads = pl.pallas_call(
        functools.partial(backward_kernel, rel_a, scat_a, block),
        grid_spec=pltpu.PrefetchScalarGridSpec(
            num_scalar_prefetch=1,
            grid=(mine_count,),
            in_specs=[
                tok_spec,
                tok_spec,
                row_spec(1152),
                row_spec(1152),
                row_spec(512),
                row_spec(1536),
                row_spec(512),
                row_spec(LANES),
                row_spec(LANES),
            ]
            + [any_spec()] * shares,
            out_specs=[tok_out, tok_out] + [small_spec] * shares,
            scratch_shapes=[
                pltpu.VMEM((shares, 512, pack), BF16),
                pltpu.VMEM((16, 512), F32),
                pltpu.VMEM((512, LANES), BF16),
                pltpu.VMEM((ROWS, 512), F32),
                pltpu.VMEM((ROWS, 512), F32),
                pltpu.VMEM((ROWS, 1536), BF16),
                pltpu.VMEM((shares, 512, 3 * local), F32),
                pltpu.VMEM((shares, 512, local), F32),
                pltpu.VMEM((512, LANES), F32),
                pltpu.VMEM((LANES, 512), F32),
                pltpu.SemaphoreType.DMA((shares, blocks)),
            ],
        ),
        out_shape=[
            shape((mine_count, SEQ, 512), BF16),
            shape((mine_count, SEQ, 512), BF16),
        ]
        + [shape((blocks, block, pack), BF16)] * shares,
        compiler_params=params(),
        cost_estimate=pl.CostEstimate(flops=25 * 10**9, bytes_accessed=30 * 10**6, transcendentals=3 * 10**6),
        name="backward",
    )(info, tokens, grad_out, comb_own, comb_oth, mid, proj, att, lse, gates, *w_parts)

    both = grads[0].astype(F32)
    for r in range(1, shares):
        both = both + across(grads[r], r).astype(F32)
    both = both.astype(BF16)
    if fast:
        half = blocks // 2
        mine = hyper_scatter(both[:half], both[half:], back_a, n)
    else:
        mine = lax.psum_scatter(both[0], "dp", scatter_dimension=0, tiled=True).astype(F32)

    def whole(own):
        parts = [own] + [across(own, r) for r in range(1, shares)]
        parts = [a.reshape(2, per_micro, 1, SEQ, 512) for a in parts]
        out = []
        for t in range(shares):
            part = parts[0]
            for r in range(1, shares):
                part = jnp.where(c ^ r == t, parts[r], part)
            out.append(part)
        return jnp.concatenate(out, 2).reshape(2, 8, SEQ, 512)

    return (
        whole(out_own),
        whole(tok_own),
        mine[:, 4 * local + 8],
        jnp.stack([mine[:, j * local : (j + 1) * local] for j in range(3)]),
        mine[:, 3 * local : 4 * local].T,
        mine[:, 4 * local + 9],
        mine[:, 4 * local : 4 * local + 8],
        jnp.concatenate(shards_in, 0),
        jnp.swapaxes(jnp.concatenate(shards_out, 0), 1, 2),
    )


def solution(mesh):
    placed = (
        P(None, "dp", None, None),
        P(None, "dp"),
        P(None, "dp", None, None),
        P("dp"),
        P(None, "dp", "tensor"),
        P("tensor", "dp"),
        P("dp"),
        P("dp", None),
        P(None, "dp", "tensor"),
        P(None, "tensor", "dp"),
        P(None, "dp", None, None),
    )
    return jax.shard_map(
        functools.partial(body, mesh.shape["dp"], mesh.shape["tensor"]),
        mesh=mesh,
        in_specs=placed,
        out_specs=(
            P(None, "dp", None, None),
            P(None, "dp", None, None),
            P("dp"),
            P(None, "dp", "tensor"),
            P("tensor", "dp"),
            P("dp"),
            P("dp", None),
            P(None, "dp", "tensor"),
            P(None, "tensor", "dp"),
        ),
        check_vma=False,
    )
```

```python
import functools

import jax
import jax.numpy as jnp
from jax import lax
from jax.experimental import pallas as pl
from jax.experimental.pallas import tpu as pltpu
from jax.sharding import PartitionSpec as P

F32 = jnp.float32
BF16 = jnp.bfloat16
HD = 64
SEQ = 197
ROWS = 208
SLOTS = 1280
SPAN = 1536
SCALE = 100
FEW = 16
MOST = 640
TILE = 256
TILES = 40
EXPERTS = 8
LANES = 128
CALLS = ((0, 4), (4, 2), (6, 2))
GROUPS = ((0,), (1, 2))
FAR = (0, 8, 4, 12)
VMEM = 58 * 1024 * 1024

LIVE, START, TOTAL, TABLE = 8, 32, 160, 256
OWNER, PART, FIRST, RING = 256, 296, 336, 344
AROUND = (0, 4, 8, 12, 14, 10, 6, 2)
FIRST_FAR, THEN_FAR = (4, 3, -3), (2, -2, 1, -1, 0)


def nt(a, b):
    return lax.dot_general(a, b, (((1,), (1,)), ((), ())), preferred_element_type=F32)


def tn(a, b):
    return lax.dot_general(a, b, (((0,), (0,)), ((), ())), preferred_element_type=F32)


def mm(a, b):
    return jnp.dot(a, b, preferred_element_type=F32)


def iota(shape, dim):
    return lax.broadcasted_iota(jnp.int32, shape, dim)


def layer_stats(values):
    centre = values - jnp.mean(values, -1, keepdims=True)
    factor = lax.rsqrt(jnp.mean(centre * centre, -1, keepdims=True) + 1e-06)
    return centre * factor, factor


def norm_back(grad, normed, factor):
    return factor * (
        grad - jnp.mean(grad, -1, keepdims=True) - normed * jnp.mean(grad * normed, -1, keepdims=True)
    )


def gelu_both(u):
    t = 1.0 / (1.0 + (0.3275911 * 0.7071067811865476) * jnp.abs(u))
    bell = jnp.exp(u * (u * -0.5))
    poly = t * (
        0.127414796 + t * (-0.142248368 + t * (0.7107068705 + t * (-0.7265760135 + t * 0.5307027145)))
    )
    tail = poly * bell
    phi = jnp.where(u >= 0.0, 1.0 - tail, tail)
    return u * phi, phi + u * bell * 0.3989422804014327


def split_low(values):
    high = values.astype(BF16).astype(F32)
    return high, values - high


def load_weights(info, parts, weights, sems, rel, rows):
    c, me = info[0], info[1]
    copies = []
    for side, part in enumerate(parts):
        t = c ^ side
        for k, r in enumerate(rel):
            where = pl.multiple_of((me ^ r) * rows, 16)
            copies.append(
                pltpu.make_async_copy(part.at[k], weights.at[t, pl.ds(where, rows), :], sems.at[side, k])
            )
    for copy in copies:
        copy.start()
    for copy in copies:
        copy.wait()


def head_mask(which):
    lane = iota((ROWS, LANES), 1)
    return (lane < HD) if which == 0 else (lane >= HD)


def forward_kernel(rel, rows, info, tok, mask, *refs):
    i = pl.program_id(0)
    w_parts, refs = refs[:-10], refs[-10:]
    src, mid, proj, att, lse, gates, weights, gains, xs, sems = refs
    shares, _, cols = weights.shape
    local = (cols - LANES) // 4
    aux_at = 4 * local

    @pl.when(i == 0)
    def _():
        load_weights(info, w_parts, weights, sems, rel, rows)
        gains[...] = weights[0, :, aux_at:].astype(F32).T[0:16, :]

    @pl.when(info[LIVE + i] == 1)
    def _():
        xs[192:ROWS, :] = jnp.zeros((ROWS - 192, 512), F32)
        xs[0:SEQ, :] = tok[0, 0].astype(F32)
        x = xs[...]
        normed, _ = layer_stats(x)
        act = (normed * gains[8:9, :]).astype(BF16)
        for t in range(shares):
            proj[0, :, t * 3 * local : (t + 1) * 3 * local] = mm(act, weights[t, :, 0 : 3 * local]).astype(BF16)
        key_ok = iota((ROWS, ROWS), 1) < SEQ
        lane = iota((ROWS, LANES), 1)
        saved = jnp.zeros((ROWS, LANES), F32)
        for t in range(shares):
            for p in range(local // LANES):
                at = t * 3 * local + p * LANES
                q = proj[0, :, at : at + LANES]
                k = proj[0, :, at + local : at + local + LANES]
                v = proj[0, :, at + 2 * local : at + 2 * local + LANES]
                halves = []
                for h in range(2):
                    qm = jnp.where(head_mask(h), q.astype(F32), 0.0).astype(BF16)
                    s = jnp.where(key_ok, nt(qm, k) * (HD**-0.5), -1e30)
                    top = jnp.max(s, -1, keepdims=True)
                    e = jnp.exp(s - top)
                    total = jnp.sum(e, -1, keepdims=True)
                    probs = (e * (1.0 / total)).astype(BF16)
                    halves.append(mm(probs, v))
                    saved = jnp.where(lane == (t * local + p * LANES) // HD + h, top + jnp.log(total), saved)
                att[0, :, t * local + p * LANES : t * local + (p + 1) * LANES] = jnp.where(
                    lane < HD, halves[0], halves[1]
                ).astype(BF16)
        lse[0] = saved
        branch = nt(att[0, :, 0:local], weights[0, :, 3 * local : aux_at])
        for t in range(1, shares):
            branch = branch + nt(att[0, :, t * local : (t + 1) * local], weights[t, :, 3 * local : aux_at])
        middle = x + branch
        mid[0] = middle
        normed2, _ = layer_stats(middle)
        act2 = (normed2 * gains[9:10, :]).astype(BF16)
        src[0, :, 0:512] = act2
        chosen = mask[0, 0].astype(F32)
        logits = jnp.where(chosen > 0.0, mm(act2, weights[0, :, aux_at:]), -1e30)
        top = jnp.max(logits, -1, keepdims=True)
        e = jnp.exp(logits - top) * chosen
        gate = e / jnp.maximum(jnp.sum(e, -1, keepdims=True), 0.5)
        gates[0] = gate
        high, low = split_low(gate)
        src[0, :, 512:640] = (high + pltpu.roll(low, 8, 1)).astype(BF16)


def blocks_of(info, i, e):
    begin, end = info[START + i * 8 + e], info[START + i * 8 + 8 + e]
    first = begin // FEW
    return first, jnp.where(end > begin, (end + FEW - 1) // FEW - first, 0)


def places(info, i, mask):
    chosen = mask[0, 0]
    lower = (iota((ROWS, ROWS), 0) > iota((ROWS, ROWS), 1)).astype(F32).astype(BF16)
    lane = iota((1, LANES), 1)
    shift = jnp.zeros((1, LANES), F32)
    base = 0
    for e in range(EXPERTS):
        _, count = blocks_of(info, i, e)
        shift = jnp.where(lane == e, (base * FEW + info[START + i * 8 + e] % FEW).astype(F32), shift)
        base = base + count
    return jnp.where(chosen.astype(F32) > 0.0, mm(lower, chosen) + shift, -1.0)


def dispatch_kernel(with_act, count, info, *refs):
    i = pl.program_id(0)
    if with_act:
        own, oth, mask, x_hbm, xbuf, tbuf, pbuf, res, sems = refs
    else:
        gy, mask, x_hbm, xbuf, tbuf, pbuf, res, sems = refs
    cols = res.shape[1]

    @pl.when(i == 0)
    def _():
        tbuf[...] = jnp.zeros(tbuf.shape, BF16)
        pbuf[...] = jnp.full(pbuf.shape, -1.0, F32)

    @pl.when(info[LIVE + i] == 1)
    def _():
        if with_act:

            @pl.when(i < count)
            def _():
                tbuf[0:ROWS, :] = own[0]

            @pl.when(i >= count)
            def _():
                tbuf[0:ROWS, :] = oth[0]
        else:
            tbuf[0:SEQ, :] = gy[0, 0]
        pbuf[0:ROWS, :] = places(info, i, mask)
        place = pbuf[...].T[0:EXPERTS, :]
        high = jnp.max(place, 0, keepdims=True)
        low = jnp.min(jnp.where(place < 0.0, 4096.0, place), 0, keepdims=True)
        row = iota((MOST, TILE), 0).astype(F32)
        pick = jnp.where((row == high) | (row == low), 1.0, 0.0).astype(BF16)
        res[...] = mm(pick, tbuf[...]).astype(BF16)
        base = 0
        for e in range(EXPERTS):
            first, blocks = blocks_of(info, i, e)
            off = info[START + i * 8 + e] % FEW

            @pl.when(blocks > 0)
            def _():
                to = pl.ds(pl.multiple_of(first * FEW, FEW), FEW)
                new = res[pl.ds(pl.multiple_of(base * FEW, FEW), FEW), :].astype(F32)
                old = xbuf[e, to, :].astype(F32)
                xbuf[e, to, :] = jnp.where(iota((FEW, cols), 0) < off, old, new).astype(BF16)

            def move(k, carry):
                to = pl.ds(pl.multiple_of((first + k) * FEW, FEW), FEW)
                xbuf[e, to, :] = res[pl.ds(pl.multiple_of((base + k) * FEW, FEW), FEW), :]
                return carry

            lax.fori_loop(1, blocks, move, 0)
            base = base + blocks

    @pl.when(i == 15)
    def _():
        for e in range(EXPERTS):
            end = pl.multiple_of((info[TOTAL + e] + FEW - 1) // FEW * FEW, FEW)
            xbuf[e, pl.ds(end, TILE), :] = jnp.zeros((TILE, cols), BF16)
        for start in (True, False):
            for e in range(EXPERTS):
                for k in range(SLOTS // TILE):

                    @pl.when(k * TILE < jnp.maximum(info[TOTAL + e], 1))
                    def _():
                        rows = pl.ds(k * TILE, TILE)
                        copy = pltpu.make_async_copy(xbuf.at[e, rows, :], x_hbm.at[e, rows, :], sems.at[e, k])
                        if start:
                            copy.start()
                        else:
                            copy.wait()


def expert_kernel(number, plan, fast, rows, n_pieces, info, xa, xg, *refs):
    pieces, refs = refs[:n_pieces], refs[n_pieces:]
    w_in, w_out, acc_in, acc_out, sems = refs[-5:]
    y, grads = refs[0], refs[1:-5]
    i = pl.program_id(0)
    n = info[FIRST + number + 1] - info[FIRST + number]
    at = info[FIRST + number] + jnp.minimum(i, n - 1)
    expert = info[OWNER + at]
    slot = expert % 2

    def owned_by(far, flip):
        return pl.multiple_of((info[RING + far % 8] ^ flip) * rows, 16)

    def copies(ex, to, start):
        for side, (entries, buf) in enumerate(zip(plan, (w_in, w_out))):
            for k, (owner, sources) in enumerate(entries):
                where = owned_by(*owner) if isinstance(owner, tuple) else owner * rows
                for ref, b, low, high in sources:
                    copy = pltpu.make_async_copy(
                        pieces[ref].at[b, ex - low], buf.at[to, pl.ds(where, rows), :], sems.at[to, side, k]
                    )

                    @pl.when((ex >= low) & (ex < high))
                    def _():
                        if start:
                            copy.start()
                        else:
                            copy.wait()

    @pl.when(i == 0)
    def _():
        copies(expert, slot, True)

    @pl.when((info[PART + at] == 0) & (i < n))
    def _():
        copies(expert, slot, False)

        @pl.when(expert + 1 < sum(CALLS[number]))
        def _():
            copies(expert + 1, 1 - slot, True)

    @pl.when(i < n)
    def _():
        rows_x = xa[0, :, 0:512]
        g = xg[0].astype(F32)
        lane = iota((TILE, LANES), 1)
        mine = (lane == expert) | (lane == expert + 8)
        gate = jnp.sum(jnp.where(mine, xa[0, :, 512:640].astype(F32), 0.0), -1, keepdims=True)
        inner = mm(rows_x, w_in[slot])
        act, slope = gelu_both(inner)
        hid = act.astype(BF16)
        out = nt(hid, w_out[slot])
        deo = (gate * g).astype(BF16)
        dinner = (mm(deo, w_out[slot]) * slope).astype(BF16)
        dgate = jnp.sum(g * out, -1, keepdims=True)
        high, low = split_low(dgate)
        y[0, :, 0:512] = (gate * out).astype(BF16)
        y[0, :, 512:1024] = nt(dinner, w_in[slot]).astype(BF16)
        y[0, :, 1024:1152] = jnp.where(lane == expert, high, jnp.where(lane == expert + 8, low, 0.0)).astype(BF16)

        @pl.when(info[PART + at] == 0)
        def _():
            acc_in[...] = tn(rows_x, dinner)
            acc_out[...] = tn(deo, hid)

        @pl.when(info[PART + at] > 0)
        def _():
            acc_in[...] += tn(rows_x, dinner)
            acc_out[...] += tn(deo, hid)

    @pl.when((i == n - 1) | ((i < n) & (info[PART + at + 1] == 0)))
    def _():
        if fast:
            sent, turned = grads[:8], grads[8:]
            for k, far in enumerate(FIRST_FAR + THEN_FAR):
                here, there = pl.ds(owned_by(far, 0), rows), pl.ds(owned_by(far, 1), rows)
                sent[k][0, 0] = acc_in[here, :].astype(BF16)
                sent[k][1, 0] = acc_out[here, :].astype(BF16)
                sent[k][2, 0] = acc_out[there, :].astype(BF16)
                to, place = (0, k) if k < len(FIRST_FAR) else (1, k - len(FIRST_FAR))
                turned[to][place, 0] = acc_in[there, :].astype(BF16)
        else:
            grads[0][0] = acc_in[...].astype(BF16)
            grads[1][0] = acc_out[...].astype(BF16)


def at_call(expert):
    return [(k, expert - first) for k, (first, count) in enumerate(CALLS) if first <= expert < first + count][0]


def add_kernel(step, counts, *refs):
    e = pl.program_id(0)
    calls, total = len(counts), sum(counts)
    ways = 1 if step in (0, 3) else 2
    half = total // 2

    def pick(parts):
        value = parts[0][...].astype(F32)
        for k in range(1, calls):
            value = jnp.where(e < sum(counts[:k]), value, parts[k][...].astype(F32))
        return value

    sums = []
    for _ in range(ways):
        q, x, refs = pick(refs[:calls]), pick(refs[calls : 2 * calls]), refs[2 * calls :]
        sums.append((q[0:1] + x, q[1:3]))
    if step == 0:
        for out, here in zip(refs, (e < half, e >= half)):

            @pl.when(here)
            def _():
                out[0:1] = sums[0][0].astype(BF16)
                out[1:3] = sums[0][1].astype(BF16)
    elif step == 3:
        up, down, first, second, third = refs
        first[...] = (sums[0][0] + up[0:1].astype(F32) + down[0:1].astype(F32))[0]
        rest = sums[0][1] + up[1:3].astype(F32) + down[1:3].astype(F32)
        second[...] = rest[0]
        third[...] = rest[1].astype(BF16)
    else:
        for k in range(2):
            arrived, out = refs[k][...].astype(F32), refs[2 + k]
            if step == 1:
                arrived = jnp.where((e < half) if k == 0 else (e >= half), arrived, 0.0)
            out[0:1] = (sums[k][0] + arrived[0:1]).astype(BF16)
            out[1:3] = (sums[k][1] + arrived[1:3]).astype(BF16)


def combine_kernel(base, info, *refs):
    y_parts, (mask, out, ybuf, sems) = refs[:-4], refs[-4:]
    i = pl.program_id(0)
    slot = i % 2

    def fetch(j, buf, start):
        @pl.when(info[LIVE + base + j] == 1)
        def _():
            at = 0
            for e in range(EXPERTS):
                first, blocks = blocks_of(info, base + j, e)

                def move(k, carry, e=e, first=first, at=at):
                    copy = pltpu.make_async_copy(
                        y_parts[at_call(e)[0]].at[at_call(e)[1], pl.ds(pl.multiple_of((first + k) * FEW, FEW), FEW), :],
                        ybuf.at[buf, pl.ds(pl.multiple_of((at + k) * FEW, FEW), FEW), :],
                        sems.at[buf],
                    )
                    if start:
                        copy.start()
                    else:
                        copy.wait()
                    return carry

                lax.fori_loop(0, blocks, move, 0)
                at = at + blocks

    @pl.when(i == 0)
    def _():
        ybuf[...] = jnp.zeros(ybuf.shape, BF16)
        fetch(i, slot, True)

    @pl.when(i + 1 < pl.num_programs(0))
    def _():
        fetch(i + 1, 1 - slot, True)

    fetch(i, slot, False)

    @pl.when(info[LIVE + base + i] == 1)
    def _():
        place = places(info, base + i, mask)
        high = jnp.max(place, -1, keepdims=True)
        low = jnp.min(jnp.where(place < 0.0, 4096.0, place), -1, keepdims=True)
        lane = iota((ROWS, MOST), 1).astype(F32)
        pick = jnp.where((lane == high) | (lane == low), 1.0, 0.0).astype(BF16)
        if out.dtype == F32:
            out[0] = mm(pick, ybuf[slot])
        else:
            out[0, :, 0:1024] = mm(pick, ybuf[slot, :, 0:1024]).astype(BF16)
            aux = mm(pick, ybuf[slot, :, 1024:1152])
            both = jnp.where(iota((ROWS, LANES), 1) < 8, aux + pltpu.roll(aux, LANES - 8, 1), 0.0)
            high, low = split_low(both)
            out[0, :, 1024:1152] = (high + pltpu.roll(low, 8, 1)).astype(BF16)


def assemble_kernel(shares, info, *refs):
    parts, (out, scratch) = refs[:-2], refs[-2:]
    c = info[0]
    for micro in range(2):

        @pl.when(pl.program_id(0) == micro)
        def _():
            for side in range(shares):
                some = [(a, j) for a in parts[3 * side : 3 * side + 3] for j in range(a.shape[0])]
                here = some[: len(some) // 2] if micro == 0 else some[len(some) // 2 :]
                for slot, (part, j) in enumerate(here):
                    for k in range(4):
                        values = part[j, 0:SEQ, k * LANES : (k + 1) * LANES].astype(F32)
                        scratch[k, pl.ds(shares * slot + (c ^ side), SEQ, stride=8), :] = values

    for k in range(4):
        out[0, :, :, k * LANES : (k + 1) * LANES] = scratch[k].reshape(SEQ, 8, LANES).astype(BF16)


def backward_kernel(
    base,
    rel,
    order,
    rows,
    info,
    tok,
    gy_ref,
    comb_own,
    comb_oth,
    mid,
    proj,
    att,
    lse,
    gates,
    *refs,
):
    i = pl.program_id(0)
    c, me = info[0], info[1]
    scratch, refs = refs[-11:], refs[:-11]
    weights, gains, twice, xs, gs, dproj, acc_qkv, acc_out, acc_router, acc_gain, sems = scratch
    shares, _, cols = weights.shape
    w_parts, refs = refs[:shares], refs[shares:]
    block_out, grad_tok = refs[:2]
    grads = refs[2:]
    local = (cols - LANES) // 4
    aux_at = 4 * local

    @pl.when(i == 0)
    def _():
        load_weights(info, w_parts, weights, sems, rel, rows)
        aux = weights[0, :, aux_at:].astype(F32)
        gains[...] = aux.T[0:16, :]
        lane = iota((512, LANES), 1)
        router = jnp.where(lane < 8, aux, 0.0)
        twice[...] = (router + pltpu.roll(router, 8, 1)).astype(BF16)
        acc_qkv[...] = jnp.zeros(acc_qkv.shape, F32)
        acc_out[...] = jnp.zeros(acc_out.shape, F32)
        acc_router[...] = jnp.zeros(acc_router.shape, F32)
        acc_gain[...] = jnp.zeros(acc_gain.shape, F32)

    @pl.when(info[LIVE + base + i] == 0)
    def _():
        block_out[...] = jnp.zeros(block_out.shape, BF16)
        grad_tok[...] = jnp.zeros(grad_tok.shape, BF16)

    @pl.when(info[LIVE + base + i] == 1)
    def _():
        xs[192:ROWS, :] = jnp.zeros((ROWS - 192, 512), F32)
        xs[0:SEQ, :] = tok[0, 0].astype(F32)
        gs[192:ROWS, :] = jnp.zeros((ROWS - 192, 512), F32)
        gs[0:SEQ, :] = gy_ref[0, 0].astype(F32)
        gy = gs[...]
        lane = iota((ROWS, LANES), 1)
        middle = mid[0]
        mixed = comb_own[0, :, 0:512] + comb_oth[0, :, 0:512].astype(F32)
        block_out[0] = (middle + mixed).astype(BF16)
        normed2, factor2 = layer_stats(middle)
        act2 = (normed2 * gains[9:10, :]).astype(BF16)
        gate = gates[0]
        aux = comb_own[0, :, 1024:1152] + comb_oth[0, :, 1024:1152].astype(F32)
        dgate = jnp.where(lane < 8, aux + pltpu.roll(aux, LANES - 8, 1), 0.0)
        dlogits = gate * (dgate - jnp.sum(gate * dgate, -1, keepdims=True))
        high, low = split_low(dlogits)
        packed = (high + pltpu.roll(low, 8, 1)).astype(BF16)
        acc_router[...] += tn(act2, packed)
        dact2 = (
            comb_own[0, :, 512:1024] + comb_oth[0, :, 512:1024].astype(F32) + nt(packed, twice[...])
        )
        acc_gain[9:10, :] += jnp.sum(dact2 * normed2, 0, keepdims=True)
        dmiddle = gy + norm_back(dact2 * gains[9:10, :], normed2, factor2)
        gs[...] = dmiddle
        dbranch = dmiddle.astype(BF16)
        x = xs[...]
        normed1, factor1 = layer_stats(x)
        act1 = (normed1 * gains[8:9, :]).astype(BF16)
        key_ok = iota((ROWS, ROWS), 1) < SEQ
        for t in range(shares):
            acc_out[t] += tn(dbranch, att[0, :, t * local : (t + 1) * local])
            datt_t = mm(dbranch, weights[t, :, 3 * local : aux_at]).astype(BF16)
            for p in range(local // LANES):
                at = t * 3 * local + p * LANES
                q = proj[0, :, at : at + LANES]
                k = proj[0, :, at + local : at + local + LANES]
                v = proj[0, :, at + 2 * local : at + 2 * local + LANES]
                datt = datt_t[:, p * LANES : (p + 1) * LANES]
                parts = []
                for h in range(2):
                    qm = jnp.where(head_mask(h), q.astype(F32), 0.0).astype(BF16)
                    dm = jnp.where(head_mask(h), datt.astype(F32), 0.0).astype(BF16)
                    head = (t * local + p * LANES) // HD + h
                    s = nt(qm, k) * (HD**-0.5) - lse[0, :, head : head + 1]
                    probs = jnp.where(key_ok, jnp.exp(jnp.where(key_ok, s, 0.0)), 0.0)
                    dprobs = nt(dm, v)
                    ds = (probs * (dprobs - jnp.sum(dprobs * probs, -1, keepdims=True))).astype(BF16)
                    parts.append((mm(ds, k), tn(ds, q), tn(probs.astype(BF16), datt)))
                for j in range(3):
                    both = jnp.where(lane < HD, parts[0][j], parts[1][j])
                    if j < 2:
                        both = both * (HD**-0.5)
                    dproj[:, at + j * local : at + j * local + LANES] = both.astype(BF16)
        dact1 = jnp.zeros((ROWS, 512), F32)
        for t in range(shares):
            dp = dproj[:, t * 3 * local : (t + 1) * 3 * local]
            acc_qkv[t] += tn(act1, dp)
            dact1 = dact1 + nt(dp, weights[t, :, 0 : 3 * local])
        acc_gain[8:9, :] += jnp.sum(dact1 * normed1, 0, keepdims=True)
        total = gs[...] + norm_back(dact1 * gains[8:9, :], normed1, factor1)
        grad_tok[0] = total.astype(BF16)

    @pl.when(i == pl.num_programs(0) - 1)
    def _():
        lane = iota((512, LANES), 1)
        router = acc_router[...]
        aux = jnp.where(lane < 8, router + pltpu.roll(router, LANES - 8, 1), acc_gain[...].T)
        acc_router[...] = aux
        for k, r in enumerate(order):
            where = pl.ds(pl.multiple_of((me ^ r) * rows, 16), rows)
            for side, out in enumerate(grads):
                out[k, :, 0 : 3 * local] = acc_qkv[c ^ side, where, :].astype(BF16)
                out[k, :, 3 * local : aux_at] = acc_out[c ^ side, where, :].astype(BF16)
                out[k, :, aux_at:] = acc_router[where, :].astype(BF16)


def swap(n, bit):
    return [(i, i ^ bit) for i in range(n)]


def hop(a, n, bits):
    return lax.ppermute(a, "dp", swap(n, bits))


def plus(*parts):
    return sum(a.astype(F32) for a in parts).astype(BF16)


def order(token, *lists):
    out = list(lax.optimization_barrier((token, *[a for arrays in lists for a in arrays])))
    got, out = [out[0]], out[1:]
    for arrays in lists:
        got.append(out[: len(arrays)])
        out = out[len(arrays) :]
    return got


def in_turn(kernel, operands):
    def run(info, earlier, *refs):
        ran, refs = refs[operands], refs[:operands] + refs[operands + 1 :]

        @pl.when(pl.program_id(0) == 0)
        def _():
            ran[...] = jnp.zeros(ran.shape, F32)

        kernel(info, *refs)

    return run


def cost(microseconds):
    return pl.CostEstimate(flops=int(microseconds * SCALE), bytes_accessed=1000, transcendentals=0)


def call(kernel, grid, token, args, in_specs, out_specs, out_shape, scratch, name, microseconds):
    token, info = token
    got = pl.pallas_call(
        in_turn(kernel, len(args)),
        grid_spec=pltpu.PrefetchScalarGridSpec(
            num_scalar_prefetch=1,
            grid=grid,
            in_specs=[any_spec()] + in_specs,
            out_specs=[pl.BlockSpec((8, LANES), lambda i, s: (0, 0))] + out_specs,
            scratch_shapes=scratch,
        ),
        out_shape=[shape((8, LANES), F32)] + out_shape,
        compiler_params=params(),
        cost_estimate=cost(microseconds),
        name=name,
    )(info, token, *args)
    return (got[0], info), got[1:]


def ring(a, n, way):
    pairs = []
    for at, here in enumerate(AROUND):
        there = AROUND[(at + way) % len(AROUND)]
        pairs += [(here, there), (here ^ 1, there ^ 1)]
    return lax.ppermute(a, "dp", pairs)


def shifted(r):
    return tuple(z ^ r for z in FAR)


def gather_line(shard, n, others):
    near = shard[None]
    near = jnp.concatenate([near, hop(near, n, 8)], 0)
    near = jnp.concatenate([near, hop(near, n, 4)], 0)
    return order(near, others)


def gather_square(near, n, others):
    by_x, by_y = hop(near, n, 1), hop(near, n, 2)
    by_x, (by_y, *others) = order(by_x, [by_y, *others])
    whole = jnp.concatenate([near, by_x, by_y, hop(by_y[:2], n, 1), hop(by_x[2:], n, 2)], 0)
    return whole, others, by_x


def scatter_far(far, n):
    half = plus(far[:2], hop(far[2:], n, 4))
    return (half[0].astype(F32) + hop(half[1:], n, 8)[0].astype(F32))


def scatter_small(whole, n):
    here, by_x, by_y, both = whole[0:4], whole[4:8], whole[8:12], whole[12:16]
    by_y = jnp.concatenate([plus(by_y[:2], hop(both[:2], n, 1)), by_y[2:]], 0)
    by_x = jnp.concatenate([by_x[:2], plus(by_x[2:], hop(both[2:], n, 2))], 0)
    return scatter_far(plus(here, hop(by_x, n, 1), hop(by_y, n, 2)), n)


def any_spec():
    return pl.BlockSpec(memory_space=pl.ANY)


def params():
    return pltpu.CompilerParams(vmem_limit_bytes=VMEM)


def shape(s, d):
    return jax.ShapeDtypeStruct(s, d)


def body(
    n,
    shares,
    tokens,
    held,
    routes,
    ln1_gain,
    qkv_weight,
    out_weight,
    ln2_gain,
    router_weight,
    expert_in,
    expert_out,
    grad_out,
):
    rows = qkv_weight.shape[1]
    width = expert_in.shape[2]
    local = qkv_weight.shape[2]
    pack = 4 * local + LANES
    mine_count = 16 // shares
    per_micro = 8 // shares
    fast = n == 16 and rows % 16 == 0
    c = lax.axis_index("tensor")
    me = lax.axis_index("dp")
    if fast:
        block = rows
        rel = FAR + shifted(1) + shifted(2) + shifted(3)
        orders = (FAR, shifted(1), shifted(2), shifted(3))
    else:
        block = 512
        rel = (0,)
        orders = ((0,),)
    blocks = len(rel)
    spot = me if fast else jnp.zeros((), jnp.int32)

    live = jnp.arange(8, dtype=jnp.int32)[None, :] < held
    lane = jnp.arange(LANES, dtype=jnp.int32)
    picked = (routes[..., 0:1] == lane) | (routes[..., 1:2] == lane)
    picked = (picked & live[:, :, None, None]).astype(BF16)
    mask = jnp.pad(picked, ((0, 0), (0, 0), (0, ROWS - SEQ), (0, 0)))
    counts = jnp.sum(
        (routes[..., None] == jnp.arange(EXPERTS, dtype=jnp.int32)).astype(jnp.int32), (2, 3)
    ) * live.astype(jnp.int32)[:, :, None]

    def own_first(a):
        a = a.reshape((2, per_micro, shares) + a.shape[2:])
        out = []
        for r in range(shares):
            part = a[:, :, 0]
            for t in range(1, shares):
                part = jnp.where(c ^ r == t, a[:, :, t], part)
            out.append(part.reshape((mine_count,) + a.shape[3:]))
        return jnp.concatenate(out, 0)

    counts = own_first(counts)
    live_list = own_first(live.astype(jnp.int32))
    ends = jnp.sum(
        jnp.where(jnp.arange(16)[:, None, None] >= jnp.arange(16)[None, :, None], counts[None], 0), 1
    )
    tiles = jnp.maximum((ends[15] + TILE - 1) // TILE, 1)
    numbers = jnp.arange(EXPERTS)
    tile_ends = jnp.sum(jnp.where(numbers[:, None] >= numbers[None, :], tiles[None, :], 0), 1)
    listed = jnp.arange(TILES)
    passed = (listed[:, None] >= tile_ends[None, :]).astype(jnp.int32)
    owner = jnp.minimum(jnp.sum(passed, 1), EXPERTS - 1)
    part = listed - jnp.sum(passed * tiles[None, :], 1)
    places = jnp.array(AROUND, jnp.int32)
    at = jnp.sum(jnp.where(places == (spot & 14), numbers, 0))
    around = jnp.sum(jnp.where((at + numbers)[:, None] % 8 == numbers[None, :], places[None, :], 0), 1) | (spot & 1)
    call_ends = [tile_ends[first + count - 1] for first, count in CALLS]
    call_starts = jnp.stack([jnp.zeros((), jnp.int32), *call_ends])
    info = jnp.concatenate(
        [
            jnp.stack([c, spot]).astype(jnp.int32),
            jnp.zeros((LIVE - 2,), jnp.int32),
            live_list,
            jnp.zeros((START - LIVE - 16,), jnp.int32),
            (ends - counts).reshape(-1),
            ends[15],
            jnp.zeros((TABLE - TOTAL - EXPERTS,), jnp.int32),
            owner,
            part,
            call_starts,
            jnp.zeros((RING - FIRST - 1 - len(CALLS),), jnp.int32),
            around,
        ]
    ).astype(jnp.int32)

    aux = jnp.concatenate(
        [router_weight, ln1_gain[:, None], ln2_gain[:, None], jnp.zeros((rows, LANES - 10), BF16)], 1
    )
    small = jnp.concatenate([qkv_weight[0], qkv_weight[1], qkv_weight[2], out_weight.T, aux], 1)
    if fast:
        line, (mask, info) = gather_line(small, n, [mask, info])
        w_own, (tokens, grad_out), by_x = gather_square(line, n, [tokens, grad_out])
    else:
        w_own = lax.all_gather(small, "dp", axis=0, tiled=True)[None]

    def across(a, r):
        return lax.ppermute(a, "tensor", swap(shares, r))

    shard = jnp.stack([expert_in, jnp.swapaxes(expert_out, 1, 2)])
    half = EXPERTS // 2

    def next_ring(two):
        return [ring(two[0], n, 1), ring(two[1], n, -1)]

    def over_x(blocks, axis=0):
        return hop(jnp.concatenate([b[:1] for b in blocks], axis), n, 1)

    if not fast:
        gathered = lax.all_gather(shard, "dp", axis=2, tiled=True)
        plan = [[(0, [(0, side, 0, EXPERTS)])] for side in range(2)]
    else:
        x0 = [hop(shard[1:], n, 1), hop(shard[:1], n, 1)]
        shard, x0, _ = order(shard, x0, [by_x])
        one = next_ring([jnp.concatenate([shard, x0[0]], 0)] * 2)
        plan = [[], []]
        for side in range(2):
            plan[side].append(((0, 0), [(0, side, 0, EXPERTS)]))
            plan[side].append(((0, 1), [(2 - side, 0, 0, EXPERTS)]))
            for k in range(1, 4):
                for b, far in enumerate((-k, k)):
                    plan[side].append(((far, 0), [(2 * k + 1 + b, side, 0, EXPERTS)]))
                    other = (2 * k + 1 + b, 2, 0, EXPERTS) if side == 1 else (10 + k, b, 0, EXPERTS)
                    plan[side].append(((far, 1), [other]))
            plan[side].append(((4, 0), [(9, side, 0, half), (10, side, half, EXPERTS)]))
            others = [(9, 2, 0, half), (10, 2, half, EXPERTS)] if side == 1 else [(14, 0, 0, EXPERTS)]
            plan[side].append(((4, 1), others))

    w_parts = [w_own] + [across(w_own, r) for r in range(1, shares)]

    def image(i, s):
        j = i % mine_count
        return (j // per_micro, shares * (j % per_micro) + (s[0] ^ (i // mine_count)), 0, 0)

    tok_spec = pl.BlockSpec((1, 1, SEQ, 512), image)
    mask_spec = pl.BlockSpec((1, 1, ROWS, LANES), image)

    def row_spec(cols):
        return pl.BlockSpec((1, ROWS, cols), lambda i, s: (i, 0, 0))

    def dispatch(token, with_act, cols, specs, args):
        return call(
            functools.partial(dispatch_kernel, with_act, mine_count),
            (16,),
            token,
            args + [mask],
            specs + [mask_spec],
            [any_spec()],
            [shape((EXPERTS, SLOTS, cols), BF16)],
            [
                pltpu.VMEM((EXPERTS, SPAN, cols), BF16),
                pltpu.VMEM((TILE, cols), BF16),
                pltpu.VMEM((TILE, LANES), F32),
                pltpu.VMEM((MOST, cols), BF16),
                pltpu.SemaphoreType.DMA((EXPERTS, SLOTS // TILE)),
            ],
            "dispatch",
            20,
        )

    token = (mask[0, 0, :8, :].astype(F32), info)
    if fast:
        first, one = order(token[0], one)
        token = (first, info)
        two = next_ring(one)
        x1 = over_x(one)
    token, (src, mid, proj, att, lse, gates) = call(
        functools.partial(forward_kernel, rel, block),
        (mine_count,),
        token,
        [tokens, mask, *w_parts],
        [tok_spec, mask_spec] + [any_spec()] * shares,
        [row_spec(640), row_spec(512), row_spec(1536), row_spec(512), row_spec(LANES), row_spec(LANES)],
        [
            shape((mine_count, ROWS, 640), BF16),
            shape((mine_count, ROWS, 512), F32),
            shape((mine_count, ROWS, 1536), BF16),
            shape((mine_count, ROWS, 512), BF16),
            shape((mine_count, ROWS, LANES), F32),
            shape((mine_count, ROWS, LANES), F32),
        ],
        [
            pltpu.VMEM((shares, 512, pack), BF16),
            pltpu.VMEM((16, 512), F32),
            pltpu.VMEM((ROWS, 512), F32),
            pltpu.SemaphoreType.DMA((shares, blocks)),
        ],
        "forward",
        23,
    )

    if fast:
        first, (src, mid, proj, att, lse, gates), two, (x1,) = order(
            token[0], [src, mid, proj, att, lse, gates], two, [x1]
        )
        token = (first, info)
        three = next_ring(two)
        x2 = over_x(two)
    src_oth = [across(src, r) for r in range(1, shares)]
    src_oth = src_oth[0] if shares == 2 else jnp.concatenate(src_oth, 0)
    token, (rows_a,) = dispatch(
        token,
        True,
        640,
        [
            pl.BlockSpec((1, ROWS, 640), lambda i, s: (jnp.minimum(i, mine_count - 1), 0, 0)),
            pl.BlockSpec((1, ROWS, 640), lambda i, s: (jnp.maximum(i - mine_count, 0), 0, 0)),
        ],
        [src, src_oth],
    )
    if fast:
        first, (rows_a,), three, (x2,) = order(token[0], [rows_a], three, [x2])
        token = (first, info)
        four = [ring(three[0][:, :half], n, 1), ring(three[1][:, half:], n, -1)]
        x3 = over_x(three)
    token, (rows_g,) = dispatch(token, False, 512, [tok_spec], [grad_out])

    def run_experts(token, number, pieces):
        opening, count = CALLS[number]

        def tile_at(i, s):
            at = jnp.minimum(s[FIRST + number] + i, s[FIRST + number + 1] - 1)
            return s[OWNER + at], s[PART + at]

        def out_at(i, s):
            e, t = tile_at(i, s)
            return e - opening, t, 0

        if fast:
            grad_specs = [pl.BlockSpec((3, 1, block, width), lambda i, s: (0, out_at(i, s)[0], 0, 0))] * 8
            grad_shapes = [shape((3, count, block, width), BF16)] * 8
            for far in (FIRST_FAR, THEN_FAR):
                grad_specs.append(
                    pl.BlockSpec((len(far), 1, block, width), lambda i, s: (0, out_at(i, s)[0], 0, 0))
                )
                grad_shapes.append(shape((len(far), count, block, width), BF16))
        else:
            grad_specs = [pl.BlockSpec((1, block, width), lambda i, s: (out_at(i, s)[0], 0, 0))] * 2
            grad_shapes = [shape((count, block, width), BF16)] * 2
        return call(
            functools.partial(expert_kernel, number, plan, fast, block, len(pieces)),
            (count * SLOTS // TILE,),
            token,
            [rows_a, rows_g, *pieces],
            [
                pl.BlockSpec((1, TILE, 640), lambda i, s: (*tile_at(i, s), 0)),
                pl.BlockSpec((1, TILE, 512), lambda i, s: (*tile_at(i, s), 0)),
            ]
            + [any_spec()] * len(pieces),
            [pl.BlockSpec((1, TILE, 1152), out_at)] + grad_specs,
            [shape((count, SPAN, 1152), BF16)] + grad_shapes,
            [
                pltpu.VMEM((2, 512, width), BF16),
                pltpu.VMEM((2, 512, width), BF16),
                pltpu.VMEM((512, width), F32),
                pltpu.VMEM((512, width), F32),
                pltpu.SemaphoreType.DMA((2, 2, blocks)),
            ],
            "expert",
            10 * count,
        )

    def combine(token, base, dtype):
        return call(
            functools.partial(combine_kernel, base),
            (mine_count,),
            token,
            [*y_parts, mask],
            [any_spec()] * len(y_parts) + [pl.BlockSpec((1, 1, ROWS, LANES), lambda i, s: image(i + base, s))],
            [row_spec(1152)],
            [shape((mine_count, ROWS, 1152), dtype)],
            [pltpu.VMEM((2, MOST, 1152), BF16), pltpu.SemaphoreType.DMA((2,))],
            "combine",
            14,
        )

    def turn(k, side):
        return hop(got[k][9 + side], n, 1)

    def ring_sums(group, step, ks, *arrived):
        counts = [CALLS[c][1] for c in GROUPS[group]]
        total = sum(counts)
        half = total // 2
        args, specs = [], []

        def add_spec(size, place, begin, count):
            specs.append(
                pl.BlockSpec((size, 1, block, width), lambda e: (place, jnp.clip(e - begin, 0, count - 1), 0, 0))
            )

        for k in ks:
            side, place = (0, k) if k < len(FIRST_FAR) else (1, k - len(FIRST_FAR))
            for c, begin in zip(GROUPS[group], (0, counts[0])):
                args.append(got[c][1 + k])
                add_spec(3, 0, begin, CALLS[c][1])
            for c, begin in zip(GROUPS[group], (0, counts[0])):
                args.append(turns[c][side])
                add_spec(1, place, begin, CALLS[c][1])
        for k, a in enumerate(arrived):
            args.append(a)
            add_spec(3, 0, k * half if step == 1 else 0, half if step == 1 else total)
        if step == 3:
            out_specs = [pl.BlockSpec((1, block, width), lambda e: (e, 0, 0))] * 3
            out_shape = [shape((total, block, width), t) for t in (F32, F32, BF16)]
        else:
            size = half if step == 0 else total
            out_specs = [
                pl.BlockSpec(
                    (3, 1, block, width), lambda e, b=(k * half if step == 0 else 0): (0, jnp.clip(e - b, 0, size - 1), 0, 0)
                )
                for k in range(2)
            ]
            out_shape = [shape((3, size, block, width), BF16)] * 2
        return pl.pallas_call(
            functools.partial(add_kernel, step, counts),
            grid=(total,),
            in_specs=specs,
            out_specs=out_specs,
            out_shape=out_shape,
            compiler_params=params(),
            cost_estimate=cost(3),
            name="add",
        )(*args)

    def round_on(group, step, ks, arrived=()):
        up, down = ring_sums(group, step, ks, *arrived)
        return [ring(up, n, 1), ring(down, n, -1)]

    def finish(group, arrived):
        first, second, third = ring_sums(group, 3, (7,), *arrived)
        return first, second + hop(third, n, 1).astype(F32)

    got, turns, rounds = [], [], []
    if fast:
        first, (rows_g,), four = order(token[0], [rows_g], four)
        token = (first, info)
        x4 = over_x(four, 1)
        pieces = (shard, *x0, *one, *two, *three, *four, x1, x2, x3, x4)
        token, some = run_experts(token, 0, pieces)
        first, some = order(token[0], some)
        got.append(some)
        turns = [[turn(0, 0)]]
        token, some = run_experts((first, info), 1, pieces)
        first, some, turns[0], got[0] = order(token[0], some, turns[0], got[0])
        got.append(some)
        rounds.append(round_on(0, 0, (0,)))
        turns[0].append(turn(0, 1))
        turns.append([turn(1, 0)])
        token, some = run_experts((first, info), 2, pieces)
        first, some, rounds[0], turns[0], turns[1], got[1] = order(
            token[0], some, rounds[0], turns[0], turns[1], got[1]
        )
        got.append(some)
        rounds[0] = round_on(0, 1, (1, 2), rounds[0])
        turns[1].append(turn(1, 1))
        turns.append([turn(2, 0)])
        token = (first, info)
    else:
        for number in range(len(CALLS)):
            token, some = run_experts(token, number, (gathered,))
            got.append(some)
    y_parts = [some[0] for some in got]

    comb_oth = []
    for r in range(1, shares):
        token, (sent,) = combine(token, mine_count * r, BF16)
        if fast:
            first, (sent,), rounds[0] = order(token[0], [sent], rounds[0])
            token = (first, info)
            rounds[0] = round_on(0, 2, (3, 4), rounds[0])
        comb_oth.append(across(sent, r))
    comb_oth = comb_oth[0] if shares == 2 else sum(a.astype(F32) for a in comb_oth).astype(BF16)
    token, (comb_own,) = combine(token, 0, F32)
    if fast:
        first, (comb_own, comb_oth), rounds[0], turns[1], turns[2], got[2] = order(
            token[0], [comb_own, comb_oth], rounds[0], turns[1], turns[2], got[2]
        )
        token = (first, info)
        turns[2].append(turn(2, 1))
        rounds[0] = round_on(0, 2, (5, 6), rounds[0])
        rounds.append(round_on(1, 0, (0,)))

    small_spec = pl.BlockSpec((blocks, block, pack), lambda i, s: (0, 0, 0))
    tok_out = pl.BlockSpec((1, ROWS, 512), lambda i, s: (i, 0, 0))
    def backward(token, base, count):

        def later(spec):
            return pl.BlockSpec(spec.block_shape, lambda i, s: spec.index_map(i + base, s))

        return call(
            functools.partial(backward_kernel, base, rel, rel, block),
            (count,),
            token,
            [tokens, grad_out, comb_own, comb_oth, mid, proj, att, lse, gates, *w_parts],
            [
                later(spec)
                for spec in (
                    tok_spec,
                    tok_spec,
                    row_spec(1152),
                    row_spec(1152),
                    row_spec(512),
                    row_spec(1536),
                    row_spec(512),
                    row_spec(LANES),
                    row_spec(LANES),
                )
            ]
            + [any_spec()] * shares,
            [tok_out, tok_out] + [small_spec] * shares,
            [shape((count, ROWS, 512), BF16)] * 2 + [shape((blocks, block, pack), BF16)] * shares,
            [
                pltpu.VMEM((shares, 512, pack), BF16),
                pltpu.VMEM((16, 512), F32),
                pltpu.VMEM((512, LANES), BF16),
                pltpu.VMEM((ROWS, 512), F32),
                pltpu.VMEM((ROWS, 512), F32),
                pltpu.VMEM((ROWS, 1536), BF16),
                pltpu.VMEM((shares, 512, 3 * local), F32),
                pltpu.VMEM((shares, 512, local), F32),
                pltpu.VMEM((512, LANES), F32),
                pltpu.VMEM((LANES, 512), F32),
                pltpu.SemaphoreType.DMA((shares, blocks)),
            ],
            "backward",
            22,
        )

    parts = []
    some = mine_count // 2
    token, part = backward(token, 0, some)
    if fast:
        first, part, rounds[0], rounds[1], turns[2] = order(token[0], part, rounds[0], rounds[1], turns[2])
        token = (first, info)
        rounds[1] = round_on(1, 1, (1, 2), rounds[1])
        total = [finish(0, rounds[0])]
    parts.append(part)
    token, part = backward(token, some, some // 2)
    if fast:
        first, part, rounds[1] = order(token[0], part, rounds[1])
        token = (first, info)
        rounds[1] = round_on(1, 2, (3, 4), rounds[1])
    parts.append(part)
    token, part = backward(token, some + some // 2, some // 2)
    if fast:
        first, part, rounds[1] = order(token[0], part, rounds[1])
    parts.append(part)
    grads = [[part[2 + r] for part in parts] for r in range(shares)]
    both = sum(a.astype(F32) for a in grads[0])
    for r in range(1, shares):
        both = both + across(plus(*grads[r]), r).astype(F32)
    both = both.astype(BF16)
    if fast:
        mine = scatter_small(both, n)
    else:
        mine = lax.psum_scatter(both[0], "dp", scatter_dimension=0, tiled=True).astype(F32)

    if fast:
        rounds[1] = round_on(1, 2, (5, 6), rounds[1])
        total.append(finish(1, rounds[1]))
        sums_in, sums_out = [[t[side] for t in total] for side in range(2)]
    else:
        sums_in, sums_out = [
            [lax.psum_scatter(g[side], "dp", scatter_dimension=1, tiled=True).astype(F32) for g in got]
            for side in (1, 2)
        ]

    def whole(which):
        pieces = []
        for r in range(shares):
            pieces += [across(part[which], r) if r else part[which] for part in parts]
        out = pl.pallas_call(
            functools.partial(assemble_kernel, shares),
            grid_spec=pltpu.PrefetchScalarGridSpec(
                num_scalar_prefetch=1,
                grid=(2,),
                in_specs=[pl.BlockSpec(a.shape, lambda i, s: (0, 0, 0)) for a in pieces],
                out_specs=pl.BlockSpec((1, SEQ, 8, 512), lambda i, s: (i, 0, 0, 0)),
                scratch_shapes=[pltpu.VMEM((4, SEQ * 8, LANES), F32)],
            ),
            out_shape=shape((2, SEQ, 8, 512), BF16),
            compiler_params=params(),
            cost_estimate=cost(6),
            name="assemble",
        )(info, *pieces)
        return jnp.swapaxes(out, 1, 2)

    return (
        whole(0),
        whole(1),
        mine[:, 4 * local + 8],
        jnp.stack([mine[:, j * local : (j + 1) * local] for j in range(3)]),
        mine[:, 3 * local : 4 * local].T,
        mine[:, 4 * local + 9],
        mine[:, 4 * local : 4 * local + 8],
        jnp.concatenate(sums_in, 0),
        jnp.swapaxes(jnp.concatenate(sums_out, 0), 1, 2),
    )


def solution(mesh):
    placed = (
        P(None, "dp", None, None),
        P(None, "dp"),
        P(None, "dp", None, None),
        P("dp"),
        P(None, "dp", "tensor"),
        P("tensor", "dp"),
        P("dp"),
        P("dp", None),
        P(None, "dp", "tensor"),
        P(None, "tensor", "dp"),
        P(None, "dp", None, None),
    )
    return jax.shard_map(
        functools.partial(body, mesh.shape["dp"], mesh.shape["tensor"]),
        mesh=mesh,
        in_specs=placed,
        out_specs=(
            P(None, "dp", None, None),
            P(None, "dp", None, None),
            P("dp"),
            P(None, "dp", "tensor"),
            P("tensor", "dp"),
            P("dp"),
            P("dp", None),
            P(None, "dp", "tensor"),
            P(None, "tensor", "dp"),
        ),
        check_vma=False,
    )
```

```python
import functools

import jax
import jax.numpy as jnp
from jax import lax
from jax.experimental import pallas as pl
from jax.experimental.pallas import tpu as pltpu
from jax.sharding import PartitionSpec as P

F32 = jnp.float32
BF16 = jnp.bfloat16
HD = 64
SEQ = 197
ROWS = 208
SLOTS = 1280
SPAN = 1536
SCALE = 100
FEW = 16
MOST = 640
TILE = 256
TILES = 40
EXPERTS = 8
LANES = 128
CALLS = ((0, 4), (4, 2), (6, 2))
GROUPS = ((0,), (1, 2))
FAR = (0, 8, 4, 12)
VMEM = 58 * 1024 * 1024

LIVE, START, TOTAL, TABLE = 8, 32, 160, 256
OWNER, PART, FIRST, RING = 256, 296, 336, 344
AROUND = (0, 4, 8, 12, 14, 10, 6, 2)
FIRST_FAR, THEN_FAR = (4, 3, -3), (2, -2, 1, -1, 0)


def nt(a, b):
    return lax.dot_general(a, b, (((1,), (1,)), ((), ())), preferred_element_type=F32)


def tn(a, b):
    return lax.dot_general(a, b, (((0,), (0,)), ((), ())), preferred_element_type=F32)


def mm(a, b):
    return jnp.dot(a, b, preferred_element_type=F32)


def iota(shape, dim):
    return lax.broadcasted_iota(jnp.int32, shape, dim)


def layer_stats(values):
    centre = values - jnp.mean(values, -1, keepdims=True)
    factor = lax.rsqrt(jnp.mean(centre * centre, -1, keepdims=True) + 1e-06)
    return centre * factor, factor


def norm_back(grad, normed, factor):
    return factor * (
        grad - jnp.mean(grad, -1, keepdims=True) - normed * jnp.mean(grad * normed, -1, keepdims=True)
    )


def gelu_both(u):
    t = 1.0 / (1.0 + (0.3275911 * 0.7071067811865476) * jnp.abs(u))
    bell = jnp.exp(u * (u * -0.5))
    poly = t * (
        0.127414796 + t * (-0.142248368 + t * (0.7107068705 + t * (-0.7265760135 + t * 0.5307027145)))
    )
    tail = poly * bell
    phi = jnp.where(u >= 0.0, 1.0 - tail, tail)
    return u * phi, phi + u * bell * 0.3989422804014327


def split_low(values):
    high = values.astype(BF16).astype(F32)
    return high, values - high


def load_weights(info, parts, weights, sems, rel, rows):
    c, me = info[0], info[1]
    copies = []
    for side, part in enumerate(parts):
        t = c ^ side
        for k, r in enumerate(rel):
            where = pl.multiple_of((me ^ r) * rows, 16)
            copies.append(
                pltpu.make_async_copy(part.at[k], weights.at[t, pl.ds(where, rows), :], sems.at[side, k])
            )
    for copy in copies:
        copy.start()
    for copy in copies:
        copy.wait()


def head_mask(which):
    lane = iota((ROWS, LANES), 1)
    return (lane < HD) if which == 0 else (lane >= HD)


def forward_kernel(rel, rows, info, tok, mask, *refs):
    i = pl.program_id(0)
    w_parts, refs = refs[:-10], refs[-10:]
    src, mid, proj, att, lse, gates, weights, gains, xs, sems = refs
    shares, _, cols = weights.shape
    local = (cols - LANES) // 4
    aux_at = 4 * local

    @pl.when(i == 0)
    def _():
        load_weights(info, w_parts, weights, sems, rel, rows)
        gains[...] = weights[0, :, aux_at:].astype(F32).T[0:16, :]

    @pl.when(info[LIVE + i] == 1)
    def _():
        xs[192:ROWS, :] = jnp.zeros((ROWS - 192, 512), F32)
        xs[0:SEQ, :] = tok[0, 0].astype(F32)
        x = xs[...]
        normed, _ = layer_stats(x)
        act = (normed * gains[8:9, :]).astype(BF16)
        for t in range(shares):
            proj[0, :, t * 3 * local : (t + 1) * 3 * local] = mm(act, weights[t, :, 0 : 3 * local]).astype(BF16)
        key_ok = iota((ROWS, ROWS), 1) < SEQ
        lane = iota((ROWS, LANES), 1)
        saved = jnp.zeros((ROWS, LANES), F32)
        for t in range(shares):
            for p in range(local // LANES):
                at = t * 3 * local + p * LANES
                q = proj[0, :, at : at + LANES]
                k = proj[0, :, at + local : at + local + LANES]
                v = proj[0, :, at + 2 * local : at + 2 * local + LANES]
                halves = []
                for h in range(2):
                    qm = jnp.where(head_mask(h), q.astype(F32), 0.0).astype(BF16)
                    s = jnp.where(key_ok, nt(qm, k) * (HD**-0.5), -1e30)
                    top = jnp.max(s, -1, keepdims=True)
                    e = jnp.exp(s - top)
                    total = jnp.sum(e, -1, keepdims=True)
                    probs = (e * (1.0 / total)).astype(BF16)
                    halves.append(mm(probs, v))
                    saved = jnp.where(lane == (t * local + p * LANES) // HD + h, top + jnp.log(total), saved)
                att[0, :, t * local + p * LANES : t * local + (p + 1) * LANES] = jnp.where(
                    lane < HD, halves[0], halves[1]
                ).astype(BF16)
        lse[0] = saved
        branch = nt(att[0, :, 0:local], weights[0, :, 3 * local : aux_at])
        for t in range(1, shares):
            branch = branch + nt(att[0, :, t * local : (t + 1) * local], weights[t, :, 3 * local : aux_at])
        middle = x + branch
        mid[0] = middle
        normed2, _ = layer_stats(middle)
        act2 = (normed2 * gains[9:10, :]).astype(BF16)
        src[0, :, 0:512] = act2
        chosen = mask[0, 0].astype(F32)
        logits = jnp.where(chosen > 0.0, mm(act2, weights[0, :, aux_at:]), -1e30)
        top = jnp.max(logits, -1, keepdims=True)
        e = jnp.exp(logits - top) * chosen
        gate = e / jnp.maximum(jnp.sum(e, -1, keepdims=True), 0.5)
        gates[0] = gate
        high, low = split_low(gate)
        src[0, :, 512:640] = (high + pltpu.roll(low, 8, 1)).astype(BF16)


def blocks_of(info, i, e):
    begin, end = info[START + i * 8 + e], info[START + i * 8 + 8 + e]
    first = begin // FEW
    return first, jnp.where(end > begin, (end + FEW - 1) // FEW - first, 0)


def places(info, i, mask):
    chosen = mask[0, 0]
    lower = (iota((ROWS, ROWS), 0) > iota((ROWS, ROWS), 1)).astype(F32).astype(BF16)
    lane = iota((1, LANES), 1)
    shift = jnp.zeros((1, LANES), F32)
    base = 0
    for e in range(EXPERTS):
        _, count = blocks_of(info, i, e)
        shift = jnp.where(lane == e, (base * FEW + info[START + i * 8 + e] % FEW).astype(F32), shift)
        base = base + count
    return jnp.where(chosen.astype(F32) > 0.0, mm(lower, chosen) + shift, -1.0)


def dispatch_kernel(with_act, count, info, *refs):
    i = pl.program_id(0)
    if with_act:
        own, oth, mask, x_hbm, xbuf, tbuf, pbuf, res, sems = refs
    else:
        gy, mask, x_hbm, xbuf, tbuf, pbuf, res, sems = refs
    cols = res.shape[1]

    @pl.when(i == 0)
    def _():
        tbuf[...] = jnp.zeros(tbuf.shape, BF16)
        pbuf[...] = jnp.full(pbuf.shape, -1.0, F32)

    @pl.when(info[LIVE + i] == 1)
    def _():
        if with_act:

            @pl.when(i < count)
            def _():
                tbuf[0:ROWS, :] = own[0]

            @pl.when(i >= count)
            def _():
                tbuf[0:ROWS, :] = oth[0]
        else:
            tbuf[0:SEQ, :] = gy[0, 0]
        pbuf[0:ROWS, :] = places(info, i, mask)
        place = pbuf[...].T[0:EXPERTS, :]
        high = jnp.max(place, 0, keepdims=True)
        low = jnp.min(jnp.where(place < 0.0, 4096.0, place), 0, keepdims=True)
        row = iota((MOST, TILE), 0).astype(F32)
        pick = jnp.where((row == high) | (row == low), 1.0, 0.0).astype(BF16)
        res[...] = mm(pick, tbuf[...]).astype(BF16)
        base = 0
        for e in range(EXPERTS):
            first, blocks = blocks_of(info, i, e)
            off = info[START + i * 8 + e] % FEW

            @pl.when(blocks > 0)
            def _():
                to = pl.ds(pl.multiple_of(first * FEW, FEW), FEW)
                new = res[pl.ds(pl.multiple_of(base * FEW, FEW), FEW), :].astype(F32)
                old = xbuf[e, to, :].astype(F32)
                xbuf[e, to, :] = jnp.where(iota((FEW, cols), 0) < off, old, new).astype(BF16)

            def move(k, carry):
                to = pl.ds(pl.multiple_of((first + k) * FEW, FEW), FEW)
                xbuf[e, to, :] = res[pl.ds(pl.multiple_of((base + k) * FEW, FEW), FEW), :]
                return carry

            lax.fori_loop(1, blocks, move, 0)
            base = base + blocks

    @pl.when(i == 15)
    def _():
        for e in range(EXPERTS):
            end = pl.multiple_of((info[TOTAL + e] + FEW - 1) // FEW * FEW, FEW)
            xbuf[e, pl.ds(end, TILE), :] = jnp.zeros((TILE, cols), BF16)
        for start in (True, False):
            for e in range(EXPERTS):
                for k in range(SLOTS // TILE):

                    @pl.when(k * TILE < jnp.maximum(info[TOTAL + e], 1))
                    def _():
                        rows = pl.ds(k * TILE, TILE)
                        copy = pltpu.make_async_copy(xbuf.at[e, rows, :], x_hbm.at[e, rows, :], sems.at[e, k])
                        if start:
                            copy.start()
                        else:
                            copy.wait()


def expert_kernel(number, plan, fast, rows, n_pieces, info, xa, xg, *refs):
    pieces, refs = refs[:n_pieces], refs[n_pieces:]
    w_in, w_out, acc_in, acc_out, staged, sems, sent_sems = refs[-7:]
    y, grads = refs[0], refs[1:-7]
    i = pl.program_id(0)
    n = info[FIRST + number + 1] - info[FIRST + number]
    at = info[FIRST + number] + jnp.minimum(i, n - 1)
    expert = info[OWNER + at]
    slot = expert % 2

    def owned_by(far, flip):
        return pl.multiple_of((info[RING + far % 8] ^ flip) * rows, 16)

    def copies(ex, to, start):
        for side, (entries, buf) in enumerate(zip(plan, (w_in, w_out))):
            for k, (owner, sources) in enumerate(entries):
                where = owned_by(*owner) if isinstance(owner, tuple) else owner * rows
                for ref, b, low, high in sources:
                    copy = pltpu.make_async_copy(
                        pieces[ref].at[b, ex - low], buf.at[to, pl.ds(where, rows), :], sems.at[to, side, k]
                    )

                    @pl.when((ex >= low) & (ex < high))
                    def _():
                        if start:
                            copy.start()
                        else:
                            copy.wait()

    @pl.when(i == 0)
    def _():
        copies(expert, slot, True)

    @pl.when((info[PART + at] == 0) & (i < n))
    def _():
        copies(expert, slot, False)

        @pl.when(expert + 1 < sum(CALLS[number]))
        def _():
            copies(expert + 1, 1 - slot, True)

    @pl.when(i < n)
    def _():
        rows_x = xa[0, :, 0:512]
        g = xg[0].astype(F32)
        lane = iota((TILE, LANES), 1)
        mine = (lane == expert) | (lane == expert + 8)
        gate = jnp.sum(jnp.where(mine, xa[0, :, 512:640].astype(F32), 0.0), -1, keepdims=True)
        inner = mm(rows_x, w_in[slot])
        act, slope = gelu_both(inner)
        hid = act.astype(BF16)
        out = nt(hid, w_out[slot])
        deo = (gate * g).astype(BF16)
        dinner = (mm(deo, w_out[slot]) * slope).astype(BF16)
        dgate = jnp.sum(g * out, -1, keepdims=True)
        high, low = split_low(dgate)
        y[0, :, 0:512] = (gate * out).astype(BF16)
        y[0, :, 512:1024] = nt(dinner, w_in[slot]).astype(BF16)
        y[0, :, 1024:1152] = jnp.where(lane == expert, high, jnp.where(lane == expert + 8, low, 0.0)).astype(BF16)

        @pl.when(info[PART + at] == 0)
        def _():
            acc_in[...] = tn(rows_x, dinner)
            acc_out[...] = tn(deo, hid)

        @pl.when(info[PART + at] > 0)
        def _():
            acc_in[...] += tn(rows_x, dinner)
            acc_out[...] += tn(deo, hid)

    def sends(to, start):
        if fast:
            parts = []
            for k, far in enumerate(FIRST_FAR + THEN_FAR):
                turned, place = (8, k) if k < len(FIRST_FAR) else (9, k - len(FIRST_FAR))
                parts += [
                    (0, owned_by(far, 0), grads[k].at[0, to]),
                    (1, owned_by(far, 0), grads[k].at[1, to]),
                    (1, owned_by(far, 1), grads[k].at[2, to]),
                    (0, owned_by(far, 1), grads[turned].at[place, to]),
                ]
        else:
            parts = [(side, 0, grads[side].at[to]) for side in range(2)]
        for k, (side, where, out) in enumerate(parts):
            copy = pltpu.make_async_copy(staged.at[side, pl.ds(where, rows), :], out, sent_sems.at[k])
            if start:
                copy.start()
            else:
                copy.wait()

    opening = CALLS[number][0]

    @pl.when((i == n - 1) | ((i < n) & (info[PART + at + 1] == 0)))
    def _():
        @pl.when(expert > opening)
        def _():
            sends(expert - opening - 1, False)

        staged[0] = acc_in[...].astype(BF16)
        staged[1] = acc_out[...].astype(BF16)
        sends(expert - opening, True)

    @pl.when(i == pl.num_programs(0) - 1)
    def _():
        sends(CALLS[number][1] - 1, False)


def at_call(expert):
    return [(k, expert - first) for k, (first, count) in enumerate(CALLS) if first <= expert < first + count][0]


def add_kernel(step, counts, *refs):
    second = pl.program_id(0) == 1
    calls = len(counts)
    ways = 1 if step in (0, 3) else 2

    def pick(parts):
        if calls == 1:
            return parts[0][...].astype(F32)
        return jnp.where(second, parts[1][...].astype(F32), parts[0][...].astype(F32))

    sums = []
    for _ in range(ways):
        q, x, refs = pick(refs[:calls]), pick(refs[calls : 2 * calls]), refs[2 * calls :]
        sums.append((q[0:1] + x, q[1:3]))
    if step == 0:
        for out, here in zip(refs, (jnp.logical_not(second), second)):

            @pl.when(here)
            def _():
                out[0:1] = sums[0][0].astype(BF16)
                out[1:3] = sums[0][1].astype(BF16)
    elif step == 3:
        up, down, first, second, third = refs
        first[...] = (sums[0][0] + up[0:1].astype(F32) + down[0:1].astype(F32))[0]
        rest = sums[0][1] + up[1:3].astype(F32) + down[1:3].astype(F32)
        second[...] = rest[0]
        third[...] = rest[1].astype(BF16)
    else:
        for k in range(2):
            arrived, out = refs[k][...].astype(F32), refs[2 + k]
            if step == 1:
                arrived = jnp.where(second, 0.0, arrived) if k == 0 else jnp.where(second, arrived, 0.0)
            out[0:1] = (sums[k][0] + arrived[0:1]).astype(BF16)
            out[1:3] = (sums[k][1] + arrived[1:3]).astype(BF16)


def combine_kernel(base, info, *refs):
    y_parts, (mask, out, ybuf, sems) = refs[:-4], refs[-4:]
    i = pl.program_id(0)
    slot = i % 2

    def fetch(j, buf, start):
        @pl.when(info[LIVE + base + j] == 1)
        def _():
            at = 0
            for e in range(EXPERTS):
                first, blocks = blocks_of(info, base + j, e)

                def move(k, carry, e=e, first=first, at=at):
                    copy = pltpu.make_async_copy(
                        y_parts[at_call(e)[0]].at[at_call(e)[1], pl.ds(pl.multiple_of((first + k) * FEW, FEW), FEW), :],
                        ybuf.at[buf, pl.ds(pl.multiple_of((at + k) * FEW, FEW), FEW), :],
                        sems.at[buf],
                    )
                    if start:
                        copy.start()
                    else:
                        copy.wait()
                    return carry

                lax.fori_loop(0, blocks, move, 0)
                at = at + blocks

    @pl.when(i == 0)
    def _():
        ybuf[...] = jnp.zeros(ybuf.shape, BF16)
        fetch(i, slot, True)

    @pl.when(i + 1 < pl.num_programs(0))
    def _():
        fetch(i + 1, 1 - slot, True)

    fetch(i, slot, False)

    @pl.when(info[LIVE + base + i] == 1)
    def _():
        place = places(info, base + i, mask)
        high = jnp.max(place, -1, keepdims=True)
        low = jnp.min(jnp.where(place < 0.0, 4096.0, place), -1, keepdims=True)
        lane = iota((ROWS, MOST), 1).astype(F32)
        pick = jnp.where((lane == high) | (lane == low), 1.0, 0.0).astype(BF16)
        if out.dtype == F32:
            out[0] = mm(pick, ybuf[slot])
        else:
            out[0, :, 0:1024] = mm(pick, ybuf[slot, :, 0:1024]).astype(BF16)
            aux = mm(pick, ybuf[slot, :, 1024:1152])
            both = jnp.where(iota((ROWS, LANES), 1) < 8, aux + pltpu.roll(aux, LANES - 8, 1), 0.0)
            high, low = split_low(both)
            out[0, :, 1024:1152] = (high + pltpu.roll(low, 8, 1)).astype(BF16)


def assemble_kernel(shares, info, *refs):
    parts, (out, scratch) = refs[:-2], refs[-2:]
    c = info[0]
    for micro in range(2):

        @pl.when(pl.program_id(0) == micro)
        def _():
            for side in range(shares):
                some = [(a, j) for a in parts[3 * side : 3 * side + 3] for j in range(a.shape[0])]
                here = some[: len(some) // 2] if micro == 0 else some[len(some) // 2 :]
                for slot, (part, j) in enumerate(here):
                    for k in range(4):
                        values = part[j, 0:SEQ, k * LANES : (k + 1) * LANES].astype(F32)
                        scratch[k, pl.ds(shares * slot + (c ^ side), SEQ, stride=8), :] = values

    for k in range(4):
        out[0, :, :, k * LANES : (k + 1) * LANES] = scratch[k].reshape(SEQ, 8, LANES).astype(BF16)


def backward_kernel(
    base,
    rel,
    order,
    rows,
    info,
    tok,
    gy_ref,
    comb_own,
    comb_oth,
    mid,
    proj,
    att,
    lse,
    gates,
    *refs,
):
    i = pl.program_id(0)
    c, me = info[0], info[1]
    scratch, refs = refs[-12:], refs[:-12]
    weights, gains, twice, xs, gs, wide, dproj, acc_qkv, acc_out, acc_router, acc_gain, sems = scratch
    shares, _, cols = weights.shape
    w_parts, refs = refs[:shares], refs[shares:]
    block_out, grad_tok = refs[:2]
    grads = refs[2:]
    local = (cols - LANES) // 4
    aux_at = 4 * local

    @pl.when(i == 0)
    def _():
        load_weights(info, w_parts, weights, sems, rel, rows)
        aux = weights[0, :, aux_at:].astype(F32)
        gains[...] = aux.T[0:16, :]
        lane = iota((512, LANES), 1)
        router = jnp.where(lane < 8, aux, 0.0)
        twice[...] = (router + pltpu.roll(router, 8, 1)).astype(BF16)
        wide[...] = jnp.zeros(wide.shape, F32)
        acc_qkv[...] = jnp.zeros(acc_qkv.shape, F32)
        acc_out[...] = jnp.zeros(acc_out.shape, F32)
        acc_router[...] = jnp.zeros(acc_router.shape, F32)
        acc_gain[...] = jnp.zeros(acc_gain.shape, F32)

    @pl.when(info[LIVE + base + i] == 0)
    def _():
        block_out[...] = jnp.zeros(block_out.shape, BF16)
        grad_tok[...] = jnp.zeros(grad_tok.shape, BF16)

    @pl.when(info[LIVE + base + i] == 1)
    def _():
        xs[192:ROWS, :] = jnp.zeros((ROWS - 192, 512), F32)
        xs[0:SEQ, :] = tok[0, 0].astype(F32)
        gs[192:ROWS, :] = jnp.zeros((ROWS - 192, 512), F32)
        gs[0:SEQ, :] = gy_ref[0, 0].astype(F32)
        gy = gs[...]
        lane = iota((ROWS, LANES), 1)
        middle = mid[0]
        mixed = comb_own[0, :, 0:512] + comb_oth[0, :, 0:512].astype(F32)
        block_out[0] = (middle + mixed).astype(BF16)
        normed2, factor2 = layer_stats(middle)
        act2 = (normed2 * gains[9:10, :]).astype(BF16)
        gate = gates[0]
        aux = comb_own[0, :, 1024:1152] + comb_oth[0, :, 1024:1152].astype(F32)
        dgate = jnp.where(lane < 8, aux + pltpu.roll(aux, LANES - 8, 1), 0.0)
        dlogits = gate * (dgate - jnp.sum(gate * dgate, -1, keepdims=True))
        high, low = split_low(dlogits)
        packed = (high + pltpu.roll(low, 8, 1)).astype(BF16)
        acc_router[...] += tn(act2, packed)
        dact2 = (
            comb_own[0, :, 512:1024] + comb_oth[0, :, 512:1024].astype(F32) + nt(packed, twice[...])
        )
        acc_gain[9:10, :] += jnp.sum(dact2 * normed2, 0, keepdims=True)
        dmiddle = gy + norm_back(dact2 * gains[9:10, :], normed2, factor2)
        gs[...] = dmiddle
        dbranch = dmiddle.astype(BF16)
        x = xs[...]
        normed1, factor1 = layer_stats(x)
        act1 = (normed1 * gains[8:9, :]).astype(BF16)
        key_ok = iota((ROWS, ROWS), 0) < SEQ
        wide[0:ROWS, :] = lse[0]
        sums = wide[...].T
        for t in range(shares):
            acc_out[t] += tn(dbranch, att[0, :, t * local : (t + 1) * local])
            datt_t = mm(dbranch, weights[t, :, 3 * local : aux_at]).astype(BF16)
            for p in range(local // LANES):
                at = t * 3 * local + p * LANES
                q = proj[0, :, at : at + LANES]
                k = proj[0, :, at + local : at + local + LANES]
                v = proj[0, :, at + 2 * local : at + 2 * local + LANES]
                datt = datt_t[:, p * LANES : (p + 1) * LANES]
                parts = []
                for h in range(2):
                    qm = jnp.where(head_mask(h), q.astype(F32), 0.0).astype(BF16)
                    dm = jnp.where(head_mask(h), datt.astype(F32), 0.0).astype(BF16)
                    head = (t * local + p * LANES) // HD + h
                    s = nt(k, qm) * (HD**-0.5) - sums[head : head + 1, 0:ROWS]
                    probs = jnp.where(key_ok, jnp.exp(jnp.where(key_ok, s, 0.0)), 0.0)
                    dprobs = nt(v, dm)
                    ds = (probs * (dprobs - jnp.sum(dprobs * probs, 0, keepdims=True))).astype(BF16)
                    parts.append((tn(ds, k), mm(ds, q), mm(probs.astype(BF16), datt)))
                for j in range(3):
                    both = jnp.where(lane < HD, parts[0][j], parts[1][j])
                    if j < 2:
                        both = both * (HD**-0.5)
                    dproj[:, at + j * local : at + j * local + LANES] = both.astype(BF16)
        dact1 = jnp.zeros((ROWS, 512), F32)
        for t in range(shares):
            dp = dproj[:, t * 3 * local : (t + 1) * 3 * local]
            acc_qkv[t] += tn(act1, dp)
            dact1 = dact1 + nt(dp, weights[t, :, 0 : 3 * local])
        acc_gain[8:9, :] += jnp.sum(dact1 * normed1, 0, keepdims=True)
        total = gs[...] + norm_back(dact1 * gains[8:9, :], normed1, factor1)
        grad_tok[0] = total.astype(BF16)

    @pl.when(i == pl.num_programs(0) - 1)
    def _():
        lane = iota((512, LANES), 1)
        router = acc_router[...]
        aux = jnp.where(lane < 8, router + pltpu.roll(router, LANES - 8, 1), acc_gain[...].T)
        acc_router[...] = aux
        for k, r in enumerate(order):
            where = pl.ds(pl.multiple_of((me ^ r) * rows, 16), rows)
            for side, out in enumerate(grads):
                out[k, :, 0 : 3 * local] = acc_qkv[c ^ side, where, :].astype(BF16)
                out[k, :, 3 * local : aux_at] = acc_out[c ^ side, where, :].astype(BF16)
                out[k, :, aux_at:] = acc_router[where, :].astype(BF16)


def swap(n, bit):
    return [(i, i ^ bit) for i in range(n)]


def hop(a, n, bits):
    return lax.ppermute(a, "dp", swap(n, bits))


def plus(*parts):
    return sum(a.astype(F32) for a in parts).astype(BF16)


def order(token, *lists):
    out = list(lax.optimization_barrier((token, *[a for arrays in lists for a in arrays])))
    got, out = [out[0]], out[1:]
    for arrays in lists:
        got.append(out[: len(arrays)])
        out = out[len(arrays) :]
    return got


def in_turn(kernel, operands):
    def run(info, earlier, *refs):
        ran, refs = refs[operands], refs[:operands] + refs[operands + 1 :]

        @pl.when(pl.program_id(0) == 0)
        def _():
            ran[...] = jnp.zeros(ran.shape, F32)

        kernel(info, *refs)

    return run


def cost(microseconds):
    return pl.CostEstimate(flops=int(microseconds * SCALE), bytes_accessed=1000, transcendentals=0)


def call(kernel, grid, token, args, in_specs, out_specs, out_shape, scratch, name, microseconds):
    token, info = token
    got = pl.pallas_call(
        in_turn(kernel, len(args)),
        grid_spec=pltpu.PrefetchScalarGridSpec(
            num_scalar_prefetch=1,
            grid=grid,
            in_specs=[any_spec()] + in_specs,
            out_specs=[pl.BlockSpec((8, LANES), lambda i, s: (0, 0))] + out_specs,
            scratch_shapes=scratch,
        ),
        out_shape=[shape((8, LANES), F32)] + out_shape,
        compiler_params=params(),
        cost_estimate=cost(microseconds),
        name=name,
    )(info, token, *args)
    return (got[0], info), got[1:]


def ring(a, n, way):
    pairs = []
    for at, here in enumerate(AROUND):
        there = AROUND[(at + way) % len(AROUND)]
        pairs += [(here, there), (here ^ 1, there ^ 1)]
    return lax.ppermute(a, "dp", pairs)


def shifted(r):
    return tuple(z ^ r for z in FAR)


def gather_line(shard, n):
    near = shard[None]
    near = jnp.concatenate([near, hop(near, n, 8)], 0)
    return jnp.concatenate([near, hop(near, n, 4)], 0)


def scatter_corner(whole, n):
    return [hop(whole[12:14], n, 1), hop(whole[14:16], n, 2)]


def scatter_square(whole, arrived, n):
    by_x, by_y = whole[4:8], whole[8:12]
    by_y = jnp.concatenate([plus(by_y[:2], arrived[0]), by_y[2:]], 0)
    by_x = jnp.concatenate([by_x[:2], plus(by_x[2:], arrived[1])], 0)
    return [whole[0:4], hop(by_x, n, 1), hop(by_y, n, 2)]


def any_spec():
    return pl.BlockSpec(memory_space=pl.ANY)


def params():
    return pltpu.CompilerParams(vmem_limit_bytes=VMEM)


def shape(s, d):
    return jax.ShapeDtypeStruct(s, d)


def body(
    n,
    shares,
    tokens,
    held,
    routes,
    ln1_gain,
    qkv_weight,
    out_weight,
    ln2_gain,
    router_weight,
    expert_in,
    expert_out,
    grad_out,
):
    rows = qkv_weight.shape[1]
    width = expert_in.shape[2]
    local = qkv_weight.shape[2]
    pack = 4 * local + LANES
    mine_count = 16 // shares
    per_micro = 8 // shares
    fast = n == 16 and rows % 16 == 0
    c = lax.axis_index("tensor")
    me = lax.axis_index("dp")
    if fast:
        block = rows
        rel = FAR + shifted(1) + shifted(2) + shifted(3)
        orders = (FAR, shifted(1), shifted(2), shifted(3))
    else:
        block = 512
        rel = (0,)
        orders = ((0,),)
    blocks = len(rel)
    spot = me if fast else jnp.zeros((), jnp.int32)

    def tables(routes, held):
        live = jnp.arange(8, dtype=jnp.int32)[None, :] < held
        lane = jnp.arange(LANES, dtype=jnp.int32)
        picked = (routes[..., 0:1] == lane) | (routes[..., 1:2] == lane)
        picked = (picked & live[:, :, None, None]).astype(BF16)
        mask = jnp.pad(picked, ((0, 0), (0, 0), (0, ROWS - SEQ), (0, 0)))
        counts = jnp.sum(
            (routes[..., None] == jnp.arange(EXPERTS, dtype=jnp.int32)).astype(jnp.int32), (2, 3)
        ) * live.astype(jnp.int32)[:, :, None]

        def own_first(a):
            a = a.reshape((2, per_micro, shares) + a.shape[2:])
            out = []
            for r in range(shares):
                part = a[:, :, 0]
                for t in range(1, shares):
                    part = jnp.where(c ^ r == t, a[:, :, t], part)
                out.append(part.reshape((mine_count,) + a.shape[3:]))
            return jnp.concatenate(out, 0)

        counts = own_first(counts)
        live_list = own_first(live.astype(jnp.int32))
        ends = jnp.sum(
            jnp.where(jnp.arange(16)[:, None, None] >= jnp.arange(16)[None, :, None], counts[None], 0), 1
        )
        tiles = jnp.maximum((ends[15] + TILE - 1) // TILE, 1)
        numbers = jnp.arange(EXPERTS)
        tile_ends = jnp.sum(jnp.where(numbers[:, None] >= numbers[None, :], tiles[None, :], 0), 1)
        listed = jnp.arange(TILES)
        passed = (listed[:, None] >= tile_ends[None, :]).astype(jnp.int32)
        owner = jnp.minimum(jnp.sum(passed, 1), EXPERTS - 1)
        part = listed - jnp.sum(passed * tiles[None, :], 1)
        places = jnp.array(AROUND, jnp.int32)
        at = jnp.sum(jnp.where(places == (spot & 14), numbers, 0))
        around = jnp.sum(jnp.where((at + numbers)[:, None] % 8 == numbers[None, :], places[None, :], 0), 1) | (spot & 1)
        call_ends = [tile_ends[first + count - 1] for first, count in CALLS]
        call_starts = jnp.stack([jnp.zeros((), jnp.int32), *call_ends])
        info = jnp.concatenate(
            [
                jnp.stack([c, spot]).astype(jnp.int32),
                jnp.zeros((LIVE - 2,), jnp.int32),
                live_list,
                jnp.zeros((START - LIVE - 16,), jnp.int32),
                (ends - counts).reshape(-1),
                ends[15],
                jnp.zeros((TABLE - TOTAL - EXPERTS,), jnp.int32),
                owner,
                part,
                call_starts,
                jnp.zeros((RING - FIRST - 1 - len(CALLS),), jnp.int32),
                around,
            ]
        ).astype(jnp.int32)
        return mask, info

    def image(i, s):
        j = i % mine_count
        return (j // per_micro, shares * (j % per_micro) + (s[0] ^ (i // mine_count)), 0, 0)

    tok_spec = pl.BlockSpec((1, 1, SEQ, 512), image)
    mask_spec = pl.BlockSpec((1, 1, ROWS, LANES), image)

    def row_spec(cols):
        return pl.BlockSpec((1, ROWS, cols), lambda i, s: (i, 0, 0))

    def dispatch(token, with_act, cols, specs, args):
        return call(
            functools.partial(dispatch_kernel, with_act, mine_count),
            (16,),
            token,
            args + [mask],
            specs + [mask_spec],
            [any_spec()],
            [shape((EXPERTS, SLOTS, cols), BF16)],
            [
                pltpu.VMEM((EXPERTS, SPAN, cols), BF16),
                pltpu.VMEM((TILE, cols), BF16),
                pltpu.VMEM((TILE, LANES), F32),
                pltpu.VMEM((MOST, cols), BF16),
                pltpu.SemaphoreType.DMA((EXPERTS, SLOTS // TILE)),
            ],
            "dispatch",
            20,
        )

    aux = jnp.concatenate(
        [router_weight, ln1_gain[:, None], ln2_gain[:, None], jnp.zeros((rows, LANES - 10), BF16)], 1
    )
    small = jnp.concatenate([qkv_weight[0], qkv_weight[1], qkv_weight[2], out_weight.T, aux], 1)
    if fast:
        line = gather_line(small, n)

        by_x, by_y = hop(line, n, 1), hop(line, n, 2)
    else:
        mask, info = tables(routes, held)
        w_own = lax.all_gather(small, "dp", axis=0, tiled=True)[None]
        token = (mask[0, 0, :8, :].astype(F32), info)

    def across(a, r):
        return lax.ppermute(a, "tensor", swap(shares, r))

    shard = jnp.stack([expert_in, jnp.swapaxes(expert_out, 1, 2)])
    half = EXPERTS // 2

    def next_ring(two):
        return [ring(two[0], n, 1), ring(two[1], n, -1)]

    def over_x(blocks, axis=0):
        return hop(jnp.concatenate([b[:1] for b in blocks], axis), n, 1)

    if not fast:
        gathered = lax.all_gather(shard, "dp", axis=2, tiled=True)
        plan = [[(0, [(0, side, 0, EXPERTS)])] for side in range(2)]
    else:
        x0 = [hop(shard[1:], n, 1)]
        shard, (line,) = order(shard, [line])
        one = next_ring([shard, shard])
        turned = next_ring([x0[0], x0[0]])
        by_x, (by_y, later), (routes, held, grad_out) = order(by_x, [by_y, shard[:1]], [routes, held, grad_out])
        x0.append(hop(later, n, 1))
        mask, info = tables(routes, held)
        w_own = jnp.concatenate([line, by_x, by_y, hop(by_y, n, 1)], 0)
        token = (mask[0, 0, :8, :].astype(F32), info)
        plan = [[], []]
        for side in range(2):
            plan[side].append(((0, 0), [(0, side, 0, EXPERTS)]))
            plan[side].append(((0, 1), [(2 - side, 0, 0, EXPERTS)]))
            for k in range(1, 4):
                for b, far in enumerate((-k, k)):
                    plan[side].append(((far, 0), [(2 * k + 1 + b, side, 0, EXPERTS)]))
                    others = [(2 * k + 1 + b, 2, 0, EXPERTS)] if side == 1 else [(10 + k, b, 0, EXPERTS)]
                    if side == 0 and k == 3:
                        others = [(13, b, 0, half), (14, b, half, EXPERTS)]
                    plan[side].append(((far, 1), others))
            plan[side].append(((4, 0), [(9, side, 0, half), (10, side, half, EXPERTS)]))
            others = [(9, 2, 0, half), (10, 2, half, EXPERTS)] if side == 1 else [(15, 0, 0, half), (16, 0, half, EXPERTS)]
            plan[side].append(((4, 1), others))

    w_parts = [w_own] + [across(w_own, r) for r in range(1, shares)]
    if fast:
        first, one, turned, (x0[1],), w_parts = order(token[0], one, turned, x0[1:], w_parts)
        token = (first, info)
        one = [jnp.concatenate(pair, 0) for pair in zip(one, turned)]
        two = next_ring(one)
        x1 = over_x(one)
    token, (src, mid, proj, att, lse, gates) = call(
        functools.partial(forward_kernel, rel, block),
        (mine_count,),
        token,
        [tokens, mask, *w_parts],
        [tok_spec, mask_spec] + [any_spec()] * shares,
        [row_spec(640), row_spec(512), row_spec(1536), row_spec(512), row_spec(LANES), row_spec(LANES)],
        [
            shape((mine_count, ROWS, 640), BF16),
            shape((mine_count, ROWS, 512), F32),
            shape((mine_count, ROWS, 1536), BF16),
            shape((mine_count, ROWS, 512), BF16),
            shape((mine_count, ROWS, LANES), F32),
            shape((mine_count, ROWS, LANES), F32),
        ],
        [
            pltpu.VMEM((shares, 512, pack), BF16),
            pltpu.VMEM((16, 512), F32),
            pltpu.VMEM((ROWS, 512), F32),
            pltpu.SemaphoreType.DMA((shares, blocks)),
        ],
        "forward",
        23,
    )

    if fast:
        first, (src, mid, proj, att, lse, gates), two, (x1,) = order(
            token[0], [src, mid, proj, att, lse, gates], two, [x1]
        )
        token = (first, info)
        three = next_ring(two)
        x2 = over_x(two)
    src_oth = [across(src, r) for r in range(1, shares)]
    src_oth = src_oth[0] if shares == 2 else jnp.concatenate(src_oth, 0)
    token, (rows_a,) = dispatch(
        token,
        True,
        640,
        [
            pl.BlockSpec((1, ROWS, 640), lambda i, s: (jnp.minimum(i, mine_count - 1), 0, 0)),
            pl.BlockSpec((1, ROWS, 640), lambda i, s: (jnp.maximum(i - mine_count, 0), 0, 0)),
        ],
        [src, src_oth],
    )
    if fast:
        first, (rows_a,), three, (x2,) = order(token[0], [rows_a], three, [x2])
        token = (first, info)
        four = [ring(three[0][:, :half], n, 1), ring(three[1][:, half:], n, -1)]
        x3 = [over_x([a[:, :half] for a in three])]
    token, (rows_g,) = dispatch(token, False, 512, [tok_spec], [grad_out])

    def run_experts(token, number, pieces):
        opening, count = CALLS[number]

        def tile_at(i, s):
            at = jnp.minimum(s[FIRST + number] + i, s[FIRST + number + 1] - 1)
            return s[OWNER + at], s[PART + at]

        def out_at(i, s):
            e, t = tile_at(i, s)
            return e - opening, t, 0

        if fast:
            grad_shapes = [shape((3, count, block, width), BF16)] * 8
            for far in (FIRST_FAR, THEN_FAR):
                grad_shapes.append(shape((len(far), count, block, width), BF16))
        else:
            grad_shapes = [shape((count, block, width), BF16)] * 2
        return call(
            functools.partial(expert_kernel, number, plan, fast, block, len(pieces)),
            (count * SLOTS // TILE,),
            token,
            [rows_a, rows_g, *pieces],
            [
                pl.BlockSpec((1, TILE, 640), lambda i, s: (*tile_at(i, s), 0)),
                pl.BlockSpec((1, TILE, 512), lambda i, s: (*tile_at(i, s), 0)),
            ]
            + [any_spec()] * len(pieces),
            [pl.BlockSpec((1, TILE, 1152), out_at)] + [any_spec()] * len(grad_shapes),
            [shape((count, SPAN, 1152), BF16)] + grad_shapes,
            [
                pltpu.VMEM((2, 512, width), BF16),
                pltpu.VMEM((2, 512, width), BF16),
                pltpu.VMEM((512, width), F32),
                pltpu.VMEM((512, width), F32),
                pltpu.VMEM((2, 512, width), BF16),
                pltpu.SemaphoreType.DMA((2, 2, blocks)),
                pltpu.SemaphoreType.DMA((32,)),
            ],
            "expert",
            10 * count,
        )

    def combine(token, base, dtype):
        return call(
            functools.partial(combine_kernel, base),
            (mine_count,),
            token,
            [*y_parts, mask],
            [any_spec()] * len(y_parts) + [pl.BlockSpec((1, 1, ROWS, LANES), lambda i, s: image(i + base, s))],
            [row_spec(1152)],
            [shape((mine_count, ROWS, 1152), dtype)],
            [pltpu.VMEM((2, MOST, 1152), BF16), pltpu.SemaphoreType.DMA((2,))],
            "combine",
            14,
        )

    def turn(k, side):
        return hop(got[k][9 + side], n, 1)

    def ring_sums(group, step, ks, *arrived):
        counts = [CALLS[c][1] for c in GROUPS[group]]
        half = sum(counts) // 2
        args, specs = [], []

        def add_spec(size, place, spread):
            specs.append(pl.BlockSpec((size, half, block, width), lambda e: (place, e if spread else 0, 0, 0)))

        spread = len(counts) == 1
        for k in ks:
            side, place = (0, k) if k < len(FIRST_FAR) else (1, k - len(FIRST_FAR))
            for c in GROUPS[group]:
                args.append(got[c][1 + k])
                add_spec(3, 0, spread)
            for c in GROUPS[group]:
                args.append(turns[c][side])
                add_spec(1, place, spread)
        for a in arrived:
            args.append(a)
            add_spec(3, 0, step != 1)
        if step == 3:
            out_specs = [pl.BlockSpec((half, block, width), lambda e: (e, 0, 0))] * 3
            out_shape = [shape((2 * half, block, width), t) for t in (F32, F32, BF16)]
        else:
            size = half if step == 0 else 2 * half
            out_specs = [
                pl.BlockSpec((3, half, block, width), lambda e: (0, 0 if step == 0 else e, 0, 0)) for k in range(2)
            ]
            out_shape = [shape((3, size, block, width), BF16)] * 2
        return pl.pallas_call(
            functools.partial(add_kernel, step, counts),
            grid=(2,),
            in_specs=specs,
            out_specs=out_specs,
            out_shape=out_shape,
            compiler_params=params(),
            cost_estimate=cost(3),
            name="add",
        )(*args)

    def round_on(group, step, ks, arrived=()):
        up, down = ring_sums(group, step, ks, *arrived)
        return [ring(up, n, 1), ring(down, n, -1)]

    def finish(group, arrived):
        first, second, third = ring_sums(group, 3, (7,), *arrived)
        return first, second + hop(third, n, 1).astype(F32)

    got, turns, rounds = [], [], []
    if fast:
        first, x3, four, (rows_g,) = order(token[0], x3, four, [rows_g])
        x4 = [over_x(four[:1])]
        first, x4, three, four = order(first, x4, three, four)
        token = (first, info)
        pieces = (shard, *x0, *one, *two, *three, four[0], four[0], x1, x2, x3[0], x3[0], x4[0], x4[0])
        token, some = run_experts(token, 0, pieces)
        x3.append(over_x([a[:, half:] for a in three]))
        x4.append(over_x(four[1:]))
        first, some, x3, x4, four = order(token[0], some, x3, x4, four)
        pieces = (shard, *x0, *one, *two, *three, *four, x1, x2, *x3, *x4)
        got.append(some)
        turns = [[turn(0, 0)]]
        token, some = run_experts((first, info), 1, pieces)
        first, some, turns[0], got[0] = order(token[0], some, turns[0], got[0])
        got.append(some)
        rounds.append(round_on(0, 0, (0,)))
        turns[0].append(turn(0, 1))
        turns.append([turn(1, 0)])
        token, some = run_experts((first, info), 2, pieces)
        first, some, rounds[0], turns[0], turns[1], got[1] = order(
            token[0], some, rounds[0], turns[0], turns[1], got[1]
        )
        got.append(some)
        rounds[0] = round_on(0, 1, (1, 2), rounds[0])
        turns[1].append(turn(1, 1))
        turns.append([turn(2, 0)])
        token = (first, info)
    else:
        for number in range(len(CALLS)):
            token, some = run_experts(token, number, (gathered,))
            got.append(some)
    y_parts = [some[0] for some in got]

    comb_oth = []
    for r in range(1, shares):
        token, (sent,) = combine(token, mine_count * r, BF16)
        if fast:
            first, (sent,), rounds[0] = order(token[0], [sent], rounds[0])
            token = (first, info)
            rounds[0] = round_on(0, 2, (3, 4), rounds[0])
        comb_oth.append(across(sent, r))
    comb_oth = comb_oth[0] if shares == 2 else sum(a.astype(F32) for a in comb_oth).astype(BF16)
    token, (comb_own,) = combine(token, 0, F32)
    if fast:
        first, (comb_own, comb_oth), rounds[0], turns[1], turns[2], got[2] = order(
            token[0], [comb_own, comb_oth], rounds[0], turns[1], turns[2], got[2]
        )
        token = (first, info)
        turns[2].append(turn(2, 1))
        rounds[0] = round_on(0, 2, (5, 6), rounds[0])
        rounds.append(round_on(1, 0, (0,)))

    small_spec = pl.BlockSpec((blocks, block, pack), lambda i, s: (0, 0, 0))
    tok_out = pl.BlockSpec((1, ROWS, 512), lambda i, s: (i, 0, 0))
    def backward(token, base, count):

        def later(spec):
            return pl.BlockSpec(spec.block_shape, lambda i, s: spec.index_map(i + base, s))

        return call(
            functools.partial(backward_kernel, base, rel, rel, block),
            (count,),
            token,
            [tokens, grad_out, comb_own, comb_oth, mid, proj, att, lse, gates, *w_parts],
            [
                later(spec)
                for spec in (
                    tok_spec,
                    tok_spec,
                    row_spec(1152),
                    row_spec(1152),
                    row_spec(512),
                    row_spec(1536),
                    row_spec(512),
                    row_spec(LANES),
                    row_spec(LANES),
                )
            ]
            + [any_spec()] * shares,
            [tok_out, tok_out] + [small_spec] * shares,
            [shape((count, ROWS, 512), BF16)] * 2 + [shape((blocks, block, pack), BF16)] * shares,
            [
                pltpu.VMEM((shares, 512, pack), BF16),
                pltpu.VMEM((16, 512), F32),
                pltpu.VMEM((512, LANES), BF16),
                pltpu.VMEM((ROWS, 512), F32),
                pltpu.VMEM((ROWS, 512), F32),
                pltpu.VMEM((TILE, LANES), F32),
                pltpu.VMEM((ROWS, 1536), BF16),
                pltpu.VMEM((shares, 512, 3 * local), F32),
                pltpu.VMEM((shares, 512, local), F32),
                pltpu.VMEM((512, LANES), F32),
                pltpu.VMEM((LANES, 512), F32),
                pltpu.SemaphoreType.DMA((shares, blocks)),
            ],
            "backward",
            22,
        )

    parts = []
    some = mine_count // 2
    token, part = backward(token, 0, some)
    if fast:
        first, part, rounds[0], rounds[1], turns[2] = order(token[0], part, rounds[0], rounds[1], turns[2])
        token = (first, info)
        rounds[1] = round_on(1, 1, (1, 2), rounds[1])
        total = [finish(0, rounds[0])]
        swapped = [[across(a, 1) for a in part[:2]]]
    parts.append(part)
    token, part = backward(token, some, some // 2)
    if fast:
        first, part, rounds[1], swapped[0] = order(token[0], part, rounds[1], swapped[0])
        token = (first, info)
        rounds[1] = round_on(1, 2, (3, 4), rounds[1])
        swapped.append([across(a, 1) for a in part[:2]])
    parts.append(part)
    token, part = backward(token, some + some // 2, some // 2)
    if fast:
        first, part, rounds[1], swapped[1] = order(token[0], part, rounds[1], swapped[1])
    parts.append(part)
    grads = [[part[2 + r] for part in parts] for r in range(shares)]
    def exchanged(which):
        return [across(part[which], r) if r else part[which] for r in range(shares) for part in parts]

    def assemble(token, pieces):
        token, (out,) = call(
            functools.partial(assemble_kernel, shares),
            (2,),
            token,
            pieces,
            [pl.BlockSpec(a.shape, lambda i, s: (0, 0, 0)) for a in pieces],
            [pl.BlockSpec((1, SEQ, 8, 512), lambda i, s: (i, 0, 0, 0))],
            [shape((2, SEQ, 8, 512), BF16)],
            [pltpu.VMEM((4, SEQ * 8, LANES), F32)],
            "assemble",
            6,
        )
        return token, jnp.swapaxes(out, 1, 2)

    both = sum(a.astype(F32) for a in grads[0])
    if fast:
        arrived = across(plus(*grads[1]), 1)
        first, (arrived, up, down) = order(first, [arrived, *ring_sums(1, 2, (5, 6), *rounds[1])])
        rounds[1] = [ring(up, n, 1), ring(down, n, -1)]
        swapped.append([across(a, 1) for a in parts[2][:2]])
        both = (both + arrived.astype(F32)).astype(BF16)
        square = scatter_corner(both, n)
        token, out = assemble((first, info), [part[0] for part in parts] + [pair[0] for pair in swapped])
        first, square, (out,) = order(token[0], square, [out])
        square = scatter_square(both, square, n)
        token, tok = assemble((first, info), [part[1] for part in parts] + [pair[1] for pair in swapped])
        first, square, rounds[1], (tok,) = order(token[0], square, rounds[1], [tok])
        line = plus(*square)
        near = hop(line[2:], n, 4)
        total.append(finish(1, rounds[1]))
        line = plus(line[:2], near)
        mine = line[0].astype(F32) + hop(line[1:], n, 8)[0].astype(F32)
        sums_in, sums_out = [[t[side] for t in total] for side in range(2)]
    else:
        for r in range(1, shares):
            both = both + across(plus(*grads[r]), r).astype(F32)
        mine = lax.psum_scatter(both[0].astype(BF16), "dp", scatter_dimension=0, tiled=True).astype(F32)
        token, out = assemble(token, exchanged(0))
        token, tok = assemble(token, exchanged(1))
        sums_in, sums_out = [
            [lax.psum_scatter(g[side], "dp", scatter_dimension=1, tiled=True).astype(F32) for g in got]
            for side in (1, 2)
        ]

    return (
        out,
        tok,
        mine[:, 4 * local + 8],
        jnp.stack([mine[:, j * local : (j + 1) * local] for j in range(3)]),
        mine[:, 3 * local : 4 * local].T,
        mine[:, 4 * local + 9],
        mine[:, 4 * local : 4 * local + 8],
        jnp.concatenate(sums_in, 0),
        jnp.swapaxes(jnp.concatenate(sums_out, 0), 1, 2),
    )


def solution(mesh):
    placed = (
        P(None, "dp", None, None),
        P(None, "dp"),
        P(None, "dp", None, None),
        P("dp"),
        P(None, "dp", "tensor"),
        P("tensor", "dp"),
        P("dp"),
        P("dp", None),
        P(None, "dp", "tensor"),
        P(None, "tensor", "dp"),
        P(None, "dp", None, None),
    )
    return jax.shard_map(
        functools.partial(body, mesh.shape["dp"], mesh.shape["tensor"]),
        mesh=mesh,
        in_specs=placed,
        out_specs=(
            P(None, "dp", None, None),
            P(None, "dp", None, None),
            P("dp"),
            P(None, "dp", "tensor"),
            P("tensor", "dp"),
            P("dp"),
            P("dp", None),
            P(None, "dp", "tensor"),
            P(None, "tensor", "dp"),
        ),
        check_vma=False,
    )
```

```python
import functools

import jax
import jax.numpy as jnp
from jax import lax
from jax.experimental import pallas as pl
from jax.experimental.pallas import tpu as pltpu
from jax.sharding import PartitionSpec as P

F32 = jnp.float32
BF16 = jnp.bfloat16
HD = 64
SEQ = 197
ROWS = 208
SLOTS = 1280
SPAN = 1536
SCALE = 100
FEW = 16
SEVERAL = 4
MOST = 640
TILE = 256
TILES = 40
EXPERTS = 8
LANES = 128
CALLS = ((0, 4), (4, 2), (6, 2))
GROUPS = ((0,), (1, 2))
FAR = (0, 8, 4, 12)
VMEM = 58 * 1024 * 1024

LIVE, START, TOTAL, TABLE = 8, 32, 160, 256
OWNER, PART, FIRST, RING = 256, 296, 336, 344
AROUND = (0, 4, 8, 12, 14, 10, 6, 2)
FIRST_FAR, THEN_FAR = (4, 3, -3), (2, -2, 1, -1, 0)


def nt(a, b):
    return lax.dot_general(a, b, (((1,), (1,)), ((), ())), preferred_element_type=F32)


def tn(a, b):
    return lax.dot_general(a, b, (((0,), (0,)), ((), ())), preferred_element_type=F32)


def mm(a, b):
    return jnp.dot(a, b, preferred_element_type=F32)


def iota(shape, dim):
    return lax.broadcasted_iota(jnp.int32, shape, dim)


def layer_stats(values):
    centre = values - jnp.mean(values, -1, keepdims=True)
    factor = lax.rsqrt(jnp.mean(centre * centre, -1, keepdims=True) + 1e-06)
    return centre * factor, factor


def norm_back(grad, normed, factor):
    return factor * (
        grad - jnp.mean(grad, -1, keepdims=True) - normed * jnp.mean(grad * normed, -1, keepdims=True)
    )


def gelu_both(u):
    t = 1.0 / (1.0 + (0.3275911 * 0.7071067811865476) * jnp.abs(u))
    bell = jnp.exp(u * (u * -0.5))
    poly = t * (
        0.127414796 + t * (-0.142248368 + t * (0.7107068705 + t * (-0.7265760135 + t * 0.5307027145)))
    )
    tail = poly * bell
    phi = jnp.where(u >= 0.0, 1.0 - tail, tail)
    return u * phi, phi + u * bell * 0.3989422804014327


def split_low(values):
    high = values.astype(BF16).astype(F32)
    return high, values - high


def load_weights(info, parts, weights, sems, rel, rows):
    c, me = info[0], info[1]
    copies = []
    for side, part in enumerate(parts):
        t = c ^ side
        for k, r in enumerate(rel):
            where = pl.multiple_of((me ^ r) * rows, 16)
            copies.append(
                pltpu.make_async_copy(part.at[k], weights.at[t, pl.ds(where, rows), :], sems.at[side, k])
            )
    for copy in copies:
        copy.start()
    for copy in copies:
        copy.wait()


def head_mask(which):
    lane = iota((ROWS, LANES), 1)
    return (lane < HD) if which == 0 else (lane >= HD)


def forward_kernel(rel, rows, info, tok, mask, *refs):
    i = pl.program_id(0)
    w_parts, refs = refs[:-10], refs[-10:]
    src, mid, proj, att, lse, gates, weights, gains, xs, sems = refs
    shares, _, cols = weights.shape
    local = (cols - LANES) // 4
    aux_at = 4 * local

    @pl.when(i == 0)
    def _():
        load_weights(info, w_parts, weights, sems, rel, rows)
        gains[...] = weights[0, :, aux_at:].astype(F32).T[0:16, :]

    @pl.when(info[LIVE + i] == 1)
    def _():
        xs[192:ROWS, :] = jnp.zeros((ROWS - 192, 512), F32)
        xs[0:SEQ, :] = tok[0, 0].astype(F32)
        x = xs[...]
        normed, _ = layer_stats(x)
        act = (normed * gains[8:9, :]).astype(BF16)
        for t in range(shares):
            proj[0, :, t * 3 * local : (t + 1) * 3 * local] = mm(act, weights[t, :, 0 : 3 * local]).astype(BF16)
        key_ok = iota((ROWS, ROWS), 1) < SEQ
        lane = iota((ROWS, LANES), 1)
        saved = jnp.zeros((ROWS, LANES), F32)
        for t in range(shares):
            for p in range(local // LANES):
                at = t * 3 * local + p * LANES
                q = proj[0, :, at : at + LANES]
                k = proj[0, :, at + local : at + local + LANES]
                v = proj[0, :, at + 2 * local : at + 2 * local + LANES]
                halves = []
                for h in range(2):
                    qm = jnp.where(head_mask(h), q.astype(F32), 0.0).astype(BF16)
                    s = jnp.where(key_ok, nt(qm, k) * (HD**-0.5), -1e30)
                    top = jnp.max(s, -1, keepdims=True)
                    e = jnp.exp(s - top)
                    total = jnp.sum(e, -1, keepdims=True)
                    probs = (e * (1.0 / total)).astype(BF16)
                    halves.append(mm(probs, v))
                    saved = jnp.where(lane == (t * local + p * LANES) // HD + h, top + jnp.log(total), saved)
                att[0, :, t * local + p * LANES : t * local + (p + 1) * LANES] = jnp.where(
                    lane < HD, halves[0], halves[1]
                ).astype(BF16)
        lse[0] = saved
        branch = nt(att[0, :, 0:local], weights[0, :, 3 * local : aux_at])
        for t in range(1, shares):
            branch = branch + nt(att[0, :, t * local : (t + 1) * local], weights[t, :, 3 * local : aux_at])
        middle = x + branch
        mid[0] = middle
        normed2, _ = layer_stats(middle)
        act2 = (normed2 * gains[9:10, :]).astype(BF16)
        src[0, :, 0:512] = act2
        chosen = mask[0, 0].astype(F32)
        logits = jnp.where(chosen > 0.0, mm(act2, weights[0, :, aux_at:]), -1e30)
        top = jnp.max(logits, -1, keepdims=True)
        e = jnp.exp(logits - top) * chosen
        gate = e / jnp.maximum(jnp.sum(e, -1, keepdims=True), 0.5)
        gates[0] = gate
        high, low = split_low(gate)
        src[0, :, 512:640] = (high + pltpu.roll(low, 8, 1)).astype(BF16)


def blocks_of(info, i, e):
    begin, end = info[START + i * 8 + e], info[START + i * 8 + 8 + e]
    first = begin // FEW
    return first, jnp.where(end > begin, (end + FEW - 1) // FEW - first, 0)


def places(info, i, mask):
    chosen = mask[0, 0]
    lower = (iota((ROWS, ROWS), 0) > iota((ROWS, ROWS), 1)).astype(F32).astype(BF16)
    lane = iota((1, LANES), 1)
    shift = jnp.zeros((1, LANES), F32)
    base = 0
    for e in range(EXPERTS):
        _, count = blocks_of(info, i, e)
        shift = jnp.where(lane == e, (base * FEW + info[START + i * 8 + e] % FEW).astype(F32), shift)
        base = base + count
    return jnp.where(chosen.astype(F32) > 0.0, mm(lower, chosen) + shift, -1.0)


def dispatch_kernel(with_act, count, info, *refs):
    i = pl.program_id(0)
    if with_act:
        own, oth, mask, x_hbm, xbuf, tbuf, pbuf, res, sems = refs
    else:
        gy, mask, x_hbm, xbuf, tbuf, pbuf, res, sems = refs
    cols = res.shape[1]

    @pl.when(i == 0)
    def _():
        tbuf[...] = jnp.zeros(tbuf.shape, BF16)
        pbuf[...] = jnp.full(pbuf.shape, -1.0, F32)

    @pl.when(info[LIVE + i] == 1)
    def _():
        if with_act:

            @pl.when(i < count)
            def _():
                tbuf[0:ROWS, :] = own[0]

            @pl.when(i >= count)
            def _():
                tbuf[0:ROWS, :] = oth[0]
        else:
            tbuf[0:SEQ, :] = gy[0, 0]
        pbuf[0:ROWS, :] = places(info, i, mask)
        place = pbuf[...].T[0:EXPERTS, :]
        high = jnp.max(place, 0, keepdims=True)
        low = jnp.min(jnp.where(place < 0.0, 4096.0, place), 0, keepdims=True)
        row = iota((MOST, TILE), 0).astype(F32)
        pick = jnp.where((row == high) | (row == low), 1.0, 0.0).astype(BF16)
        res[0:MOST, :] = mm(pick, tbuf[...]).astype(BF16)
        base = 0
        for e in range(EXPERTS):
            first, blocks = blocks_of(info, i, e)
            off = info[START + i * 8 + e] % FEW

            @pl.when(blocks > 0)
            def _():
                to = pl.ds(pl.multiple_of(first * FEW, FEW), FEW)
                new = res[pl.ds(pl.multiple_of(base * FEW, FEW), FEW), :].astype(F32)
                old = xbuf[e, to, :].astype(F32)
                xbuf[e, to, :] = jnp.where(iota((FEW, cols), 0) < off, old, new).astype(BF16)

            def move(k, carry):
                to = pl.ds(pl.multiple_of((first + 1 + SEVERAL * k) * FEW, FEW), SEVERAL * FEW)
                at = pl.ds(pl.multiple_of((base + 1 + SEVERAL * k) * FEW, FEW), SEVERAL * FEW)
                xbuf[e, to, :] = res[at, :]
                return carry

            lax.fori_loop(0, (blocks + SEVERAL - 2) // SEVERAL, move, 0)
            base = base + blocks

    @pl.when(i == 15)
    def _():
        for e in range(EXPERTS):
            end = pl.multiple_of((info[TOTAL + e] + FEW - 1) // FEW * FEW, FEW)
            xbuf[e, pl.ds(end, TILE), :] = jnp.zeros((TILE, cols), BF16)
        for start in (True, False):
            for e in range(EXPERTS):
                for k in range(SLOTS // TILE):

                    @pl.when(k * TILE < jnp.maximum(info[TOTAL + e], 1))
                    def _():
                        rows = pl.ds(k * TILE, TILE)
                        copy = pltpu.make_async_copy(xbuf.at[e, rows, :], x_hbm.at[e, rows, :], sems.at[e, k])
                        if start:
                            copy.start()
                        else:
                            copy.wait()


def expert_kernel(number, plan, fast, rows, n_pieces, info, xa, xg, *refs):
    pieces, refs = refs[:n_pieces], refs[n_pieces:]
    w_in, w_out, acc_in, acc_out, staged, sems, sent_sems = refs[-7:]
    y, grads = refs[0], refs[1:-7]
    i = pl.program_id(0)
    n = info[FIRST + number + 1] - info[FIRST + number]
    at = info[FIRST + number] + jnp.minimum(i, n - 1)
    expert = info[OWNER + at]
    slot = expert % 2

    def owned_by(far, flip):
        return pl.multiple_of((info[RING + far % 8] ^ flip) * rows, 16)

    def copies(ex, to, start):
        for side, (entries, buf) in enumerate(zip(plan, (w_in, w_out))):
            for k, (owner, sources) in enumerate(entries):
                where = owned_by(*owner) if isinstance(owner, tuple) else owner * rows
                for ref, b, low, high in sources:
                    copy = pltpu.make_async_copy(
                        pieces[ref].at[b, ex - low], buf.at[to, pl.ds(where, rows), :], sems.at[to, side, k]
                    )

                    @pl.when((ex >= low) & (ex < high))
                    def _():
                        if start:
                            copy.start()
                        else:
                            copy.wait()

    @pl.when(i == 0)
    def _():
        copies(expert, slot, True)

    @pl.when((info[PART + at] == 0) & (i < n))
    def _():
        copies(expert, slot, False)

        @pl.when(expert + 1 < sum(CALLS[number]))
        def _():
            copies(expert + 1, 1 - slot, True)

    @pl.when(i < n)
    def _():
        rows_x = xa[0, :, 0:512]
        g = xg[0].astype(F32)
        lane = iota((TILE, LANES), 1)
        mine = (lane == expert) | (lane == expert + 8)
        gate = jnp.sum(jnp.where(mine, xa[0, :, 512:640].astype(F32), 0.0), -1, keepdims=True)
        inner = mm(rows_x, w_in[slot])
        act, slope = gelu_both(inner)
        hid = act.astype(BF16)
        out = nt(hid, w_out[slot])
        deo = (gate * g).astype(BF16)
        dinner = (mm(deo, w_out[slot]) * slope).astype(BF16)
        dgate = jnp.sum(g * out, -1, keepdims=True)
        high, low = split_low(dgate)
        y[0, :, 0:512] = (gate * out).astype(BF16)
        y[0, :, 512:1024] = nt(dinner, w_in[slot]).astype(BF16)
        y[0, :, 1024:1152] = jnp.where(lane == expert, high, jnp.where(lane == expert + 8, low, 0.0)).astype(BF16)

        @pl.when(info[PART + at] == 0)
        def _():
            acc_in[...] = tn(rows_x, dinner)
            acc_out[...] = tn(deo, hid)

        @pl.when(info[PART + at] > 0)
        def _():
            acc_in[...] += tn(rows_x, dinner)
            acc_out[...] += tn(deo, hid)

    def sends(to, start):
        if fast:
            parts = []
            for k, far in enumerate(FIRST_FAR + THEN_FAR):
                turned, place = (8, k) if k < len(FIRST_FAR) else (9, k - len(FIRST_FAR))
                parts += [
                    (0, owned_by(far, 0), grads[k].at[0, to]),
                    (1, owned_by(far, 0), grads[k].at[1, to]),
                    (1, owned_by(far, 1), grads[k].at[2, to]),
                    (0, owned_by(far, 1), grads[turned].at[place, to]),
                ]
        else:
            parts = [(side, 0, grads[side].at[to]) for side in range(2)]
        for k, (side, where, out) in enumerate(parts):
            copy = pltpu.make_async_copy(staged.at[side, pl.ds(where, rows), :], out, sent_sems.at[k])
            if start:
                copy.start()
            else:
                copy.wait()

    opening = CALLS[number][0]

    @pl.when((i == n - 1) | ((i < n) & (info[PART + at + 1] == 0)))
    def _():
        @pl.when(expert > opening)
        def _():
            sends(expert - opening - 1, False)

        staged[0] = acc_in[...].astype(BF16)
        staged[1] = acc_out[...].astype(BF16)
        sends(expert - opening, True)

    @pl.when(i == pl.num_programs(0) - 1)
    def _():
        sends(CALLS[number][1] - 1, False)


def at_call(expert):
    return [(k, expert - first) for k, (first, count) in enumerate(CALLS) if first <= expert < first + count][0]


def add_kernel(step, counts, *refs):
    second = pl.program_id(0) == 1
    calls = len(counts)
    ways = 1 if step in (0, 3) else 2

    def pick(parts):
        if calls == 1:
            return parts[0][...].astype(F32)
        return jnp.where(second, parts[1][...].astype(F32), parts[0][...].astype(F32))

    sums = []
    for _ in range(ways):
        q, x, refs = pick(refs[:calls]), pick(refs[calls : 2 * calls]), refs[2 * calls :]
        sums.append((q[0:1] + x, q[1:3]))
    if step == 0:
        for out, here in zip(refs, (jnp.logical_not(second), second)):

            @pl.when(here)
            def _():
                out[0:1] = sums[0][0].astype(BF16)
                out[1:3] = sums[0][1].astype(BF16)
    elif step == 3:
        up, down, first, second, third = refs
        first[...] = (sums[0][0] + up[0:1].astype(F32) + down[0:1].astype(F32))[0]
        rest = sums[0][1] + up[1:3].astype(F32) + down[1:3].astype(F32)
        second[...] = rest[0]
        third[...] = rest[1].astype(BF16)
    else:
        for k in range(2):
            arrived, out = refs[k][...].astype(F32), refs[2 + k]
            if step == 1:
                arrived = jnp.where(second, 0.0, arrived) if k == 0 else jnp.where(second, arrived, 0.0)
            out[0:1] = (sums[k][0] + arrived[0:1]).astype(BF16)
            out[1:3] = (sums[k][1] + arrived[1:3]).astype(BF16)


def combine_kernel(base, info, *refs):
    y_parts, (mask, out, ybuf, sems) = refs[:-4], refs[-4:]
    i = pl.program_id(0)
    slot = i % 2

    def fetch(j, buf, start):
        @pl.when(info[LIVE + base + j] == 1)
        def _():
            at = 0
            for e in range(EXPERTS):
                first, blocks = blocks_of(info, base + j, e)

                def move(k, carry, e=e, first=first, at=at):
                    copy = pltpu.make_async_copy(
                        y_parts[at_call(e)[0]].at[at_call(e)[1], pl.ds(pl.multiple_of((first + k) * FEW, FEW), FEW), :],
                        ybuf.at[buf, pl.ds(pl.multiple_of((at + k) * FEW, FEW), FEW), :],
                        sems.at[buf],
                    )
                    if start:
                        copy.start()
                    else:
                        copy.wait()
                    return carry

                lax.fori_loop(0, blocks, move, 0)
                at = at + blocks

    @pl.when(i == 0)
    def _():
        ybuf[...] = jnp.zeros(ybuf.shape, BF16)
        fetch(i, slot, True)

    @pl.when(i + 1 < pl.num_programs(0))
    def _():
        fetch(i + 1, 1 - slot, True)

    fetch(i, slot, False)

    @pl.when(info[LIVE + base + i] == 1)
    def _():
        place = places(info, base + i, mask)
        high = jnp.max(place, -1, keepdims=True)
        low = jnp.min(jnp.where(place < 0.0, 4096.0, place), -1, keepdims=True)
        lane = iota((ROWS, MOST), 1).astype(F32)
        pick = jnp.where((lane == high) | (lane == low), 1.0, 0.0).astype(BF16)
        if out.dtype == F32:
            out[0] = mm(pick, ybuf[slot])
        else:
            out[0, :, 0:1024] = mm(pick, ybuf[slot, :, 0:1024]).astype(BF16)
            aux = mm(pick, ybuf[slot, :, 1024:1152])
            both = jnp.where(iota((ROWS, LANES), 1) < 8, aux + pltpu.roll(aux, LANES - 8, 1), 0.0)
            high, low = split_low(both)
            out[0, :, 1024:1152] = (high + pltpu.roll(low, 8, 1)).astype(BF16)


def assemble_kernel(shares, info, *refs):
    parts, (out, scratch) = refs[:-2], refs[-2:]
    c = info[0]
    for micro in range(2):

        @pl.when(pl.program_id(0) == micro)
        def _():
            for side in range(shares):
                some = [(a, j) for a in parts[3 * side : 3 * side + 3] for j in range(a.shape[0])]
                here = some[: len(some) // 2] if micro == 0 else some[len(some) // 2 :]
                for slot, (part, j) in enumerate(here):
                    for k in range(4):
                        values = part[j, 0:SEQ, k * LANES : (k + 1) * LANES].astype(F32)
                        scratch[k, pl.ds(shares * slot + (c ^ side), SEQ, stride=8), :] = values

    for k in range(4):
        out[0, :, :, k * LANES : (k + 1) * LANES] = scratch[k].reshape(SEQ, 8, LANES).astype(BF16)


def backward_kernel(
    base,
    rel,
    order,
    rows,
    info,
    tok,
    gy_ref,
    comb_own,
    comb_oth,
    mid,
    proj,
    att,
    lse,
    gates,
    *refs,
):
    i = pl.program_id(0)
    c, me = info[0], info[1]
    scratch, refs = refs[-12:], refs[:-12]
    weights, gains, twice, xs, gs, wide, dproj, acc_qkv, acc_out, acc_router, acc_gain, sems = scratch
    shares, _, cols = weights.shape
    w_parts, refs = refs[:shares], refs[shares:]
    block_out, grad_tok = refs[:2]
    grads = refs[2:]
    local = (cols - LANES) // 4
    aux_at = 4 * local

    @pl.when(i == 0)
    def _():
        load_weights(info, w_parts, weights, sems, rel, rows)
        aux = weights[0, :, aux_at:].astype(F32)
        gains[...] = aux.T[0:16, :]
        lane = iota((512, LANES), 1)
        router = jnp.where(lane < 8, aux, 0.0)
        twice[...] = (router + pltpu.roll(router, 8, 1)).astype(BF16)
        wide[...] = jnp.zeros(wide.shape, F32)
        acc_qkv[...] = jnp.zeros(acc_qkv.shape, F32)
        acc_out[...] = jnp.zeros(acc_out.shape, F32)
        acc_router[...] = jnp.zeros(acc_router.shape, F32)
        acc_gain[...] = jnp.zeros(acc_gain.shape, F32)

    @pl.when(info[LIVE + base + i] == 0)
    def _():
        block_out[...] = jnp.zeros(block_out.shape, BF16)
        grad_tok[...] = jnp.zeros(grad_tok.shape, BF16)

    @pl.when(info[LIVE + base + i] == 1)
    def _():
        xs[192:ROWS, :] = jnp.zeros((ROWS - 192, 512), F32)
        xs[0:SEQ, :] = tok[0, 0].astype(F32)
        gs[192:ROWS, :] = jnp.zeros((ROWS - 192, 512), F32)
        gs[0:SEQ, :] = gy_ref[0, 0].astype(F32)
        gy = gs[...]
        lane = iota((ROWS, LANES), 1)
        middle = mid[0]
        mixed = comb_own[0, :, 0:512] + comb_oth[0, :, 0:512].astype(F32)
        block_out[0] = (middle + mixed).astype(BF16)
        normed2, factor2 = layer_stats(middle)
        act2 = (normed2 * gains[9:10, :]).astype(BF16)
        gate = gates[0]
        aux = comb_own[0, :, 1024:1152] + comb_oth[0, :, 1024:1152].astype(F32)
        dgate = jnp.where(lane < 8, aux + pltpu.roll(aux, LANES - 8, 1), 0.0)
        dlogits = gate * (dgate - jnp.sum(gate * dgate, -1, keepdims=True))
        high, low = split_low(dlogits)
        packed = (high + pltpu.roll(low, 8, 1)).astype(BF16)
        acc_router[...] += tn(act2, packed)
        dact2 = (
            comb_own[0, :, 512:1024] + comb_oth[0, :, 512:1024].astype(F32) + nt(packed, twice[...])
        )
        acc_gain[9:10, :] += jnp.sum(dact2 * normed2, 0, keepdims=True)
        dmiddle = gy + norm_back(dact2 * gains[9:10, :], normed2, factor2)
        gs[...] = dmiddle
        dbranch = dmiddle.astype(BF16)
        x = xs[...]
        normed1, factor1 = layer_stats(x)
        act1 = (normed1 * gains[8:9, :]).astype(BF16)
        key_ok = iota((ROWS, ROWS), 0) < SEQ
        wide[0:ROWS, :] = lse[0]
        sums = wide[...].T
        for t in range(shares):
            acc_out[t] += tn(dbranch, att[0, :, t * local : (t + 1) * local])
            datt_t = mm(dbranch, weights[t, :, 3 * local : aux_at]).astype(BF16)
            for p in range(local // LANES):
                at = t * 3 * local + p * LANES
                q = proj[0, :, at : at + LANES]
                k = proj[0, :, at + local : at + local + LANES]
                v = proj[0, :, at + 2 * local : at + 2 * local + LANES]
                datt = datt_t[:, p * LANES : (p + 1) * LANES]
                parts = []
                for h in range(2):
                    qm = jnp.where(head_mask(h), q.astype(F32), 0.0).astype(BF16)
                    dm = jnp.where(head_mask(h), datt.astype(F32), 0.0).astype(BF16)
                    head = (t * local + p * LANES) // HD + h
                    s = nt(k, qm) * (HD**-0.5) - sums[head : head + 1, 0:ROWS]
                    probs = jnp.where(key_ok, jnp.exp(jnp.where(key_ok, s, 0.0)), 0.0)
                    dprobs = nt(v, dm)
                    ds = (probs * (dprobs - jnp.sum(dprobs * probs, 0, keepdims=True))).astype(BF16)
                    parts.append((tn(ds, k), mm(ds, q), mm(probs.astype(BF16), datt)))
                for j in range(3):
                    both = jnp.where(lane < HD, parts[0][j], parts[1][j])
                    if j < 2:
                        both = both * (HD**-0.5)
                    dproj[:, at + j * local : at + j * local + LANES] = both.astype(BF16)
        dact1 = jnp.zeros((ROWS, 512), F32)
        for t in range(shares):
            dp = dproj[:, t * 3 * local : (t + 1) * 3 * local]
            acc_qkv[t] += tn(act1, dp)
            dact1 = dact1 + nt(dp, weights[t, :, 0 : 3 * local])
        acc_gain[8:9, :] += jnp.sum(dact1 * normed1, 0, keepdims=True)
        total = gs[...] + norm_back(dact1 * gains[8:9, :], normed1, factor1)
        grad_tok[0] = total.astype(BF16)

    @pl.when(i == pl.num_programs(0) - 1)
    def _():
        lane = iota((512, LANES), 1)
        router = acc_router[...]
        aux = jnp.where(lane < 8, router + pltpu.roll(router, LANES - 8, 1), acc_gain[...].T)
        acc_router[...] = aux
        for k, r in enumerate(order):
            where = pl.ds(pl.multiple_of((me ^ r) * rows, 16), rows)
            for side, out in enumerate(grads):
                out[k, :, 0 : 3 * local] = acc_qkv[c ^ side, where, :].astype(BF16)
                out[k, :, 3 * local : aux_at] = acc_out[c ^ side, where, :].astype(BF16)
                out[k, :, aux_at:] = acc_router[where, :].astype(BF16)


def swap(n, bit):
    return [(i, i ^ bit) for i in range(n)]


def hop(a, n, bits):
    return lax.ppermute(a, "dp", swap(n, bits))


def plus(*parts):
    return sum(a.astype(F32) for a in parts).astype(BF16)


def order(token, *lists):
    out = list(lax.optimization_barrier((token, *[a for arrays in lists for a in arrays])))
    got, out = [out[0]], out[1:]
    for arrays in lists:
        got.append(out[: len(arrays)])
        out = out[len(arrays) :]
    return got


def in_turn(kernel, operands):
    def run(info, earlier, *refs):
        ran, refs = refs[operands], refs[:operands] + refs[operands + 1 :]

        @pl.when(pl.program_id(0) == 0)
        def _():
            ran[...] = jnp.zeros(ran.shape, F32)

        kernel(info, *refs)

    return run


def cost(microseconds):
    return pl.CostEstimate(flops=int(microseconds * SCALE), bytes_accessed=1000, transcendentals=0)


def call(kernel, grid, token, args, in_specs, out_specs, out_shape, scratch, name, microseconds):
    token, info = token
    got = pl.pallas_call(
        in_turn(kernel, len(args)),
        grid_spec=pltpu.PrefetchScalarGridSpec(
            num_scalar_prefetch=1,
            grid=grid,
            in_specs=[any_spec()] + in_specs,
            out_specs=[pl.BlockSpec((8, LANES), lambda i, s: (0, 0))] + out_specs,
            scratch_shapes=scratch,
        ),
        out_shape=[shape((8, LANES), F32)] + out_shape,
        compiler_params=params(),
        cost_estimate=cost(microseconds),
        name=name,
    )(info, token, *args)
    return (got[0], info), got[1:]


def ring(a, n, way):
    pairs = []
    for at, here in enumerate(AROUND):
        there = AROUND[(at + way) % len(AROUND)]
        pairs += [(here, there), (here ^ 1, there ^ 1)]
    return lax.ppermute(a, "dp", pairs)


def shifted(r):
    return tuple(z ^ r for z in FAR)


def gather_line(shard, n):
    near = shard[None]
    near = jnp.concatenate([near, hop(near, n, 8)], 0)
    return jnp.concatenate([near, hop(near, n, 4)], 0)


def scatter_corner(whole, n):
    return [hop(whole[12:14], n, 1), hop(whole[14:16], n, 2)]


def scatter_square(whole, arrived, n):
    by_x, by_y = whole[4:8], whole[8:12]
    by_y = jnp.concatenate([plus(by_y[:2], arrived[0]), by_y[2:]], 0)
    by_x = jnp.concatenate([by_x[:2], plus(by_x[2:], arrived[1])], 0)
    return [whole[0:4], hop(by_x, n, 1), hop(by_y, n, 2)]


def any_spec():
    return pl.BlockSpec(memory_space=pl.ANY)


def params():
    return pltpu.CompilerParams(vmem_limit_bytes=VMEM)


def shape(s, d):
    return jax.ShapeDtypeStruct(s, d)


def body(
    n,
    shares,
    tokens,
    held,
    routes,
    ln1_gain,
    qkv_weight,
    out_weight,
    ln2_gain,
    router_weight,
    expert_in,
    expert_out,
    grad_out,
):
    rows = qkv_weight.shape[1]
    width = expert_in.shape[2]
    local = qkv_weight.shape[2]
    pack = 4 * local + LANES
    mine_count = 16 // shares
    per_micro = 8 // shares
    fast = n == 16 and rows % 16 == 0
    c = lax.axis_index("tensor")
    me = lax.axis_index("dp")
    if fast:
        block = rows
        rel = FAR + shifted(1) + shifted(2) + shifted(3)
        orders = (FAR, shifted(1), shifted(2), shifted(3))
    else:
        block = 512
        rel = (0,)
        orders = ((0,),)
    blocks = len(rel)
    spot = me if fast else jnp.zeros((), jnp.int32)

    def tables(routes, held):
        live = jnp.arange(8, dtype=jnp.int32)[None, :] < held
        lane = jnp.arange(LANES, dtype=jnp.int32)
        picked = (routes[..., 0:1] == lane) | (routes[..., 1:2] == lane)
        picked = (picked & live[:, :, None, None]).astype(BF16)
        mask = jnp.pad(picked, ((0, 0), (0, 0), (0, ROWS - SEQ), (0, 0)))
        counts = jnp.sum(
            (routes[..., None] == jnp.arange(EXPERTS, dtype=jnp.int32)).astype(jnp.int32), (2, 3)
        ) * live.astype(jnp.int32)[:, :, None]

        def own_first(a):
            a = a.reshape((2, per_micro, shares) + a.shape[2:])
            out = []
            for r in range(shares):
                part = a[:, :, 0]
                for t in range(1, shares):
                    part = jnp.where(c ^ r == t, a[:, :, t], part)
                out.append(part.reshape((mine_count,) + a.shape[3:]))
            return jnp.concatenate(out, 0)

        counts = own_first(counts)
        live_list = own_first(live.astype(jnp.int32))
        ends = jnp.sum(
            jnp.where(jnp.arange(16)[:, None, None] >= jnp.arange(16)[None, :, None], counts[None], 0), 1
        )
        tiles = jnp.maximum((ends[15] + TILE - 1) // TILE, 1)
        numbers = jnp.arange(EXPERTS)
        tile_ends = jnp.sum(jnp.where(numbers[:, None] >= numbers[None, :], tiles[None, :], 0), 1)
        listed = jnp.arange(TILES)
        passed = (listed[:, None] >= tile_ends[None, :]).astype(jnp.int32)
        owner = jnp.minimum(jnp.sum(passed, 1), EXPERTS - 1)
        part = listed - jnp.sum(passed * tiles[None, :], 1)
        places = jnp.array(AROUND, jnp.int32)
        at = jnp.sum(jnp.where(places == (spot & 14), numbers, 0))
        around = jnp.sum(jnp.where((at + numbers)[:, None] % 8 == numbers[None, :], places[None, :], 0), 1) | (spot & 1)
        call_ends = [tile_ends[first + count - 1] for first, count in CALLS]
        call_starts = jnp.stack([jnp.zeros((), jnp.int32), *call_ends])
        info = jnp.concatenate(
            [
                jnp.stack([c, spot]).astype(jnp.int32),
                jnp.zeros((LIVE - 2,), jnp.int32),
                live_list,
                jnp.zeros((START - LIVE - 16,), jnp.int32),
                (ends - counts).reshape(-1),
                ends[15],
                jnp.zeros((TABLE - TOTAL - EXPERTS,), jnp.int32),
                owner,
                part,
                call_starts,
                jnp.zeros((RING - FIRST - 1 - len(CALLS),), jnp.int32),
                around,
            ]
        ).astype(jnp.int32)
        return mask, info

    def image(i, s):
        j = i % mine_count
        return (j // per_micro, shares * (j % per_micro) + (s[0] ^ (i // mine_count)), 0, 0)

    tok_spec = pl.BlockSpec((1, 1, SEQ, 512), image)
    mask_spec = pl.BlockSpec((1, 1, ROWS, LANES), image)

    def row_spec(cols):
        return pl.BlockSpec((1, ROWS, cols), lambda i, s: (i, 0, 0))

    def dispatch(token, with_act, cols, specs, args):
        return call(
            functools.partial(dispatch_kernel, with_act, mine_count),
            (16,),
            token,
            args + [mask],
            specs + [mask_spec],
            [any_spec()],
            [shape((EXPERTS, SLOTS, cols), BF16)],
            [
                pltpu.VMEM((EXPERTS, SPAN, cols), BF16),
                pltpu.VMEM((TILE, cols), BF16),
                pltpu.VMEM((TILE, LANES), F32),
                pltpu.VMEM((MOST + SEVERAL * FEW, cols), BF16),
                pltpu.SemaphoreType.DMA((EXPERTS, SLOTS // TILE)),
            ],
            "dispatch",
            20,
        )

    aux = jnp.concatenate(
        [router_weight, ln1_gain[:, None], ln2_gain[:, None], jnp.zeros((rows, LANES - 10), BF16)], 1
    )
    small = jnp.concatenate([qkv_weight[0], qkv_weight[1], qkv_weight[2], out_weight.T, aux], 1)
    if fast:
        line = gather_line(small, n)

        by_x, by_y = hop(line, n, 1), hop(line, n, 2)
    else:
        mask, info = tables(routes, held)
        w_own = lax.all_gather(small, "dp", axis=0, tiled=True)[None]
        token = (mask[0, 0, :8, :].astype(F32), info)

    def across(a, r):
        return lax.ppermute(a, "tensor", swap(shares, r))

    shard = jnp.stack([expert_in, jnp.swapaxes(expert_out, 1, 2)])
    half = EXPERTS // 2

    def next_ring(two):
        return [ring(two[0], n, 1), ring(two[1], n, -1)]

    def over_x(blocks, axis=0):
        return hop(jnp.concatenate([b[:1] for b in blocks], axis), n, 1)

    if not fast:
        gathered = lax.all_gather(shard, "dp", axis=2, tiled=True)
        plan = [[(0, [(0, side, 0, EXPERTS)])] for side in range(2)]
    else:
        x0 = [hop(shard[1:], n, 1)]
        shard, (line,) = order(shard, [line])
        one = next_ring([shard, shard])
        turned = next_ring([x0[0], x0[0]])
        by_x, (by_y, later), (routes, held, grad_out) = order(by_x, [by_y, shard[:1]], [routes, held, grad_out])
        x0.append(hop(later, n, 1))
        mask, info = tables(routes, held)
        w_own = jnp.concatenate([line, by_x, by_y, hop(by_y, n, 1)], 0)
        token = (mask[0, 0, :8, :].astype(F32), info)
        plan = [[], []]
        for side in range(2):
            plan[side].append(((0, 0), [(0, side, 0, EXPERTS)]))
            plan[side].append(((0, 1), [(2 - side, 0, 0, EXPERTS)]))
            for k in range(1, 4):
                for b, far in enumerate((-k, k)):
                    plan[side].append(((far, 0), [(2 * k + 1 + b, side, 0, EXPERTS)]))
                    others = [(2 * k + 1 + b, 2, 0, EXPERTS)] if side == 1 else [(10 + k, b, 0, EXPERTS)]
                    if side == 0 and k == 3:
                        others = [(13, b, 0, half), (14, b, half, EXPERTS)]
                    plan[side].append(((far, 1), others))
            plan[side].append(((4, 0), [(9, side, 0, half), (10, side, half, EXPERTS)]))
            others = [(9, 2, 0, half), (10, 2, half, EXPERTS)] if side == 1 else [(15, 0, 0, half), (16, 0, half, EXPERTS)]
            plan[side].append(((4, 1), others))

    w_parts = [w_own] + [across(w_own, r) for r in range(1, shares)]
    if fast:
        first, one, turned, (x0[1],), w_parts = order(token[0], one, turned, x0[1:], w_parts)
        token = (first, info)
        one = [jnp.concatenate(pair, 0) for pair in zip(one, turned)]
        two = next_ring(one)
        x1 = over_x(one)
    token, (src, mid, proj, att, lse, gates) = call(
        functools.partial(forward_kernel, rel, block),
        (mine_count,),
        token,
        [tokens, mask, *w_parts],
        [tok_spec, mask_spec] + [any_spec()] * shares,
        [row_spec(640), row_spec(512), row_spec(1536), row_spec(512), row_spec(LANES), row_spec(LANES)],
        [
            shape((mine_count, ROWS, 640), BF16),
            shape((mine_count, ROWS, 512), F32),
            shape((mine_count, ROWS, 1536), BF16),
            shape((mine_count, ROWS, 512), BF16),
            shape((mine_count, ROWS, LANES), F32),
            shape((mine_count, ROWS, LANES), F32),
        ],
        [
            pltpu.VMEM((shares, 512, pack), BF16),
            pltpu.VMEM((16, 512), F32),
            pltpu.VMEM((ROWS, 512), F32),
            pltpu.SemaphoreType.DMA((shares, blocks)),
        ],
        "forward",
        23,
    )

    if fast:
        first, (src, mid, proj, att, lse, gates), two, (x1,) = order(
            token[0], [src, mid, proj, att, lse, gates], two, [x1]
        )
        token = (first, info)
        three = next_ring(two)
        x2 = over_x(two)
    src_oth = [across(src, r) for r in range(1, shares)]
    src_oth = src_oth[0] if shares == 2 else jnp.concatenate(src_oth, 0)
    token, (rows_a,) = dispatch(
        token,
        True,
        640,
        [
            pl.BlockSpec((1, ROWS, 640), lambda i, s: (jnp.minimum(i, mine_count - 1), 0, 0)),
            pl.BlockSpec((1, ROWS, 640), lambda i, s: (jnp.maximum(i - mine_count, 0), 0, 0)),
        ],
        [src, src_oth],
    )
    if fast:
        first, (rows_a,), three, (x2,) = order(token[0], [rows_a], three, [x2])
        token = (first, info)
        four = [ring(three[0][:, :half], n, 1), ring(three[1][:, half:], n, -1)]
        x3 = [over_x([a[:, :half] for a in three])]
    token, (rows_g,) = dispatch(token, False, 512, [tok_spec], [grad_out])

    def run_experts(token, number, pieces):
        opening, count = CALLS[number]

        def tile_at(i, s):
            at = jnp.minimum(s[FIRST + number] + i, s[FIRST + number + 1] - 1)
            return s[OWNER + at], s[PART + at]

        def out_at(i, s):
            e, t = tile_at(i, s)
            return e - opening, t, 0

        if fast:
            grad_shapes = [shape((3, count, block, width), BF16)] * 8
            for far in (FIRST_FAR, THEN_FAR):
                grad_shapes.append(shape((len(far), count, block, width), BF16))
        else:
            grad_shapes = [shape((count, block, width), BF16)] * 2
        return call(
            functools.partial(expert_kernel, number, plan, fast, block, len(pieces)),
            (count * SLOTS // TILE,),
            token,
            [rows_a, rows_g, *pieces],
            [
                pl.BlockSpec((1, TILE, 640), lambda i, s: (*tile_at(i, s), 0)),
                pl.BlockSpec((1, TILE, 512), lambda i, s: (*tile_at(i, s), 0)),
            ]
            + [any_spec()] * len(pieces),
            [pl.BlockSpec((1, TILE, 1152), out_at)] + [any_spec()] * len(grad_shapes),
            [shape((count, SPAN, 1152), BF16)] + grad_shapes,
            [
                pltpu.VMEM((2, 512, width), BF16),
                pltpu.VMEM((2, 512, width), BF16),
                pltpu.VMEM((512, width), F32),
                pltpu.VMEM((512, width), F32),
                pltpu.VMEM((2, 512, width), BF16),
                pltpu.SemaphoreType.DMA((2, 2, blocks)),
                pltpu.SemaphoreType.DMA((32,)),
            ],
            "expert",
            10 * count,
        )

    def combine(token, base, dtype):
        return call(
            functools.partial(combine_kernel, base),
            (mine_count,),
            token,
            [*y_parts, mask],
            [any_spec()] * len(y_parts) + [pl.BlockSpec((1, 1, ROWS, LANES), lambda i, s: image(i + base, s))],
            [row_spec(1152)],
            [shape((mine_count, ROWS, 1152), dtype)],
            [pltpu.VMEM((2, MOST, 1152), BF16), pltpu.SemaphoreType.DMA((2,))],
            "combine",
            14,
        )

    def turn(k, side):
        return hop(got[k][9 + side], n, 1)

    def ring_sums(group, step, ks, *arrived):
        counts = [CALLS[c][1] for c in GROUPS[group]]
        half = sum(counts) // 2
        args, specs = [], []

        def add_spec(size, place, spread):
            specs.append(pl.BlockSpec((size, half, block, width), lambda e: (place, e if spread else 0, 0, 0)))

        spread = len(counts) == 1
        for k in ks:
            side, place = (0, k) if k < len(FIRST_FAR) else (1, k - len(FIRST_FAR))
            for c in GROUPS[group]:
                args.append(got[c][1 + k])
                add_spec(3, 0, spread)
            for c in GROUPS[group]:
                args.append(turns[c][side])
                add_spec(1, place, spread)
        for a in arrived:
            args.append(a)
            add_spec(3, 0, step != 1)
        if step == 3:
            out_specs = [pl.BlockSpec((half, block, width), lambda e: (e, 0, 0))] * 3
            out_shape = [shape((2 * half, block, width), t) for t in (F32, F32, BF16)]
        else:
            size = half if step == 0 else 2 * half
            out_specs = [
                pl.BlockSpec((3, half, block, width), lambda e: (0, 0 if step == 0 else e, 0, 0)) for k in range(2)
            ]
            out_shape = [shape((3, size, block, width), BF16)] * 2
        return pl.pallas_call(
            functools.partial(add_kernel, step, counts),
            grid=(2,),
            in_specs=specs,
            out_specs=out_specs,
            out_shape=out_shape,
            compiler_params=params(),
            cost_estimate=cost(3),
            name="add",
        )(*args)

    def round_on(group, step, ks, arrived=()):
        up, down = ring_sums(group, step, ks, *arrived)
        return [ring(up, n, 1), ring(down, n, -1)]

    def finish(group, arrived):
        first, second, third = ring_sums(group, 3, (7,), *arrived)
        return first, second + hop(third, n, 1).astype(F32)

    got, turns, rounds = [], [], []
    if fast:
        first, x3, four, (rows_g,) = order(token[0], x3, four, [rows_g])
        x4 = [over_x(four[:1])]
        first, x4, three, four = order(first, x4, three, four)
        token = (first, info)
        pieces = (shard, *x0, *one, *two, *three, four[0], four[0], x1, x2, x3[0], x3[0], x4[0], x4[0])
        token, some = run_experts(token, 0, pieces)
        x3.append(over_x([a[:, half:] for a in three]))
        x4.append(over_x(four[1:]))
        first, some, x3, x4, four = order(token[0], some, x3, x4, four)
        pieces = (shard, *x0, *one, *two, *three, *four, x1, x2, *x3, *x4)
        got.append(some)
        turns = [[turn(0, 0)]]
        token, some = run_experts((first, info), 1, pieces)
        first, some, turns[0], got[0] = order(token[0], some, turns[0], got[0])
        got.append(some)
        rounds.append(round_on(0, 0, (0,)))
        turns[0].append(turn(0, 1))
        turns.append([turn(1, 0)])
        token, some = run_experts((first, info), 2, pieces)
        first, some, rounds[0], turns[0], got[1] = order(token[0], some, rounds[0], turns[0], got[1])
        got.append(some)
        rounds[0] = round_on(0, 1, (1, 2), rounds[0])
        turns.append([turn(2, 0)])
        token = (first, info)
    else:
        for number in range(len(CALLS)):
            token, some = run_experts(token, number, (gathered,))
            got.append(some)
    y_parts = [some[0] for some in got]

    comb_oth = []
    for r in range(1, shares):
        token, (sent,) = combine(token, mine_count * r, BF16)
        if fast:
            first, (sent,), rounds[0], turns[1] = order(token[0], [sent], rounds[0], turns[1])
            token = (first, info)
            rounds[0] = round_on(0, 2, (3, 4), rounds[0])
        comb_oth.append(across(sent, r))
    comb_oth = comb_oth[0] if shares == 2 else sum(a.astype(F32) for a in comb_oth).astype(BF16)
    token, (comb_own,) = combine(token, 0, F32)
    if fast:
        first, (comb_own, comb_oth), rounds[0], turns[2], got[1], got[2] = order(
            token[0], [comb_own, comb_oth], rounds[0], turns[2], got[1], got[2]
        )
        token = (first, info)
        turns[1].append(turn(1, 1))
        rounds[0] = round_on(0, 2, (5, 6), rounds[0])
        rounds.append(round_on(1, 0, (0,)))

    small_spec = pl.BlockSpec((blocks, block, pack), lambda i, s: (0, 0, 0))
    tok_out = pl.BlockSpec((1, ROWS, 512), lambda i, s: (i, 0, 0))
    def backward(token, base, count):

        def later(spec):
            return pl.BlockSpec(spec.block_shape, lambda i, s: spec.index_map(i + base, s))

        return call(
            functools.partial(backward_kernel, base, rel, rel, block),
            (count,),
            token,
            [tokens, grad_out, comb_own, comb_oth, mid, proj, att, lse, gates, *w_parts],
            [
                later(spec)
                for spec in (
                    tok_spec,
                    tok_spec,
                    row_spec(1152),
                    row_spec(1152),
                    row_spec(512),
                    row_spec(1536),
                    row_spec(512),
                    row_spec(LANES),
                    row_spec(LANES),
                )
            ]
            + [any_spec()] * shares,
            [tok_out, tok_out] + [small_spec] * shares,
            [shape((count, ROWS, 512), BF16)] * 2 + [shape((blocks, block, pack), BF16)] * shares,
            [
                pltpu.VMEM((shares, 512, pack), BF16),
                pltpu.VMEM((16, 512), F32),
                pltpu.VMEM((512, LANES), BF16),
                pltpu.VMEM((ROWS, 512), F32),
                pltpu.VMEM((ROWS, 512), F32),
                pltpu.VMEM((TILE, LANES), F32),
                pltpu.VMEM((ROWS, 1536), BF16),
                pltpu.VMEM((shares, 512, 3 * local), F32),
                pltpu.VMEM((shares, 512, local), F32),
                pltpu.VMEM((512, LANES), F32),
                pltpu.VMEM((LANES, 512), F32),
                pltpu.SemaphoreType.DMA((shares, blocks)),
            ],
            "backward",
            22,
        )

    parts = []
    some = mine_count // 2
    token, part = backward(token, 0, some)
    if fast:
        first, part, rounds[0], rounds[1], turns[1], got[2] = order(
            token[0], part, rounds[0], rounds[1], turns[1], got[2]
        )
        token = (first, info)
        rounds[1] = round_on(1, 1, (1, 2), rounds[1])
        total = [finish(0, rounds[0])]
        swapped = [[across(a, 1) for a in part[:2]]]
        turns[2].append(turn(2, 1))
    parts.append(part)
    token, part = backward(token, some, some // 2)
    if fast:
        first, part, rounds[1], swapped[0], turns[2] = order(token[0], part, rounds[1], swapped[0], turns[2])
        token = (first, info)
        rounds[1] = round_on(1, 2, (3, 4), rounds[1])
        swapped.append([across(a, 1) for a in part[:2]])
    parts.append(part)
    token, part = backward(token, some + some // 2, some // 2)
    if fast:
        first, part, rounds[1], swapped[1] = order(token[0], part, rounds[1], swapped[1])
    parts.append(part)
    grads = [[part[2 + r] for part in parts] for r in range(shares)]
    def exchanged(which):
        return [across(part[which], r) if r else part[which] for r in range(shares) for part in parts]

    def assemble(token, pieces):
        token, (out,) = call(
            functools.partial(assemble_kernel, shares),
            (2,),
            token,
            pieces,
            [pl.BlockSpec(a.shape, lambda i, s: (0, 0, 0)) for a in pieces],
            [pl.BlockSpec((1, SEQ, 8, 512), lambda i, s: (i, 0, 0, 0))],
            [shape((2, SEQ, 8, 512), BF16)],
            [pltpu.VMEM((4, SEQ * 8, LANES), F32)],
            "assemble",
            6,
        )
        return token, jnp.swapaxes(out, 1, 2)

    both = sum(a.astype(F32) for a in grads[0])
    if fast:
        arrived = across(plus(*grads[1]), 1)
        first, (arrived, up, down) = order(first, [arrived, *ring_sums(1, 2, (5, 6), *rounds[1])])
        rounds[1] = [ring(up, n, 1), ring(down, n, -1)]
        swapped.append([across(a, 1) for a in parts[2][:2]])
        both = (both + arrived.astype(F32)).astype(BF16)
        square = scatter_corner(both, n)
        token, out = assemble((first, info), [part[0] for part in parts] + [pair[0] for pair in swapped])
        first, square, (out,) = order(token[0], square, [out])
        square = scatter_square(both, square, n)
        token, tok = assemble((first, info), [part[1] for part in parts] + [pair[1] for pair in swapped])
        first, square, rounds[1], (tok,) = order(token[0], square, rounds[1], [tok])
        line = plus(*square)
        near = hop(line[2:], n, 4)
        total.append(finish(1, rounds[1]))
        line = plus(line[:2], near)
        mine = line[0].astype(F32) + hop(line[1:], n, 8)[0].astype(F32)
        sums_in, sums_out = [[t[side] for t in total] for side in range(2)]
    else:
        for r in range(1, shares):
            both = both + across(plus(*grads[r]), r).astype(F32)
        mine = lax.psum_scatter(both[0].astype(BF16), "dp", scatter_dimension=0, tiled=True).astype(F32)
        token, out = assemble(token, exchanged(0))
        token, tok = assemble(token, exchanged(1))
        sums_in, sums_out = [
            [lax.psum_scatter(g[side], "dp", scatter_dimension=1, tiled=True).astype(F32) for g in got]
            for side in (1, 2)
        ]

    return (
        out,
        tok,
        mine[:, 4 * local + 8],
        jnp.stack([mine[:, j * local : (j + 1) * local] for j in range(3)]),
        mine[:, 3 * local : 4 * local].T,
        mine[:, 4 * local + 9],
        mine[:, 4 * local : 4 * local + 8],
        jnp.concatenate(sums_in, 0),
        jnp.swapaxes(jnp.concatenate(sums_out, 0), 1, 2),
    )


def solution(mesh):
    placed = (
        P(None, "dp", None, None),
        P(None, "dp"),
        P(None, "dp", None, None),
        P("dp"),
        P(None, "dp", "tensor"),
        P("tensor", "dp"),
        P("dp"),
        P("dp", None),
        P(None, "dp", "tensor"),
        P(None, "tensor", "dp"),
        P(None, "dp", None, None),
    )
    return jax.shard_map(
        functools.partial(body, mesh.shape["dp"], mesh.shape["tensor"]),
        mesh=mesh,
        in_specs=placed,
        out_specs=(
            P(None, "dp", None, None),
            P(None, "dp", None, None),
            P("dp"),
            P(None, "dp", "tensor"),
            P("tensor", "dp"),
            P("dp"),
            P("dp", None),
            P(None, "dp", "tensor"),
            P(None, "tensor", "dp"),
        ),
        check_vma=False,
    )
```

```python
import functools

import jax
import jax.numpy as jnp
from jax import lax
from jax.experimental import pallas as pl
from jax.experimental.pallas import tpu as pltpu
from jax.sharding import PartitionSpec as P

F32 = jnp.float32
BF16 = jnp.bfloat16
HD = 64
SEQ = 197
ROWS = 208
SLOTS = 1280
SPAN = 1536
SCALE = 100
FEW = 16
SEVERAL = 4
MOST = 640
TILE = 256
TILES = 40
EXPERTS = 8
LANES = 128
CALLS = ((0, 4), (4, 2), (6, 2))
GROUPS = ((0,), (1, 2))
FAR = (0, 8, 4, 12)
VMEM = 58 * 1024 * 1024

LIVE, START, TOTAL, TABLE = 8, 32, 160, 256
OWNER, PART, FIRST, RING = 256, 296, 336, 344
AROUND = (0, 4, 8, 12, 14, 10, 6, 2)
FIRST_FAR, THEN_FAR = (4, 3, -3), (2, -2, 1, -1, 0)


def nt(a, b):
    return lax.dot_general(a, b, (((1,), (1,)), ((), ())), preferred_element_type=F32)


def tn(a, b):
    return lax.dot_general(a, b, (((0,), (0,)), ((), ())), preferred_element_type=F32)


def mm(a, b):
    return jnp.dot(a, b, preferred_element_type=F32)


def iota(shape, dim):
    return lax.broadcasted_iota(jnp.int32, shape, dim)


def layer_stats(values):
    centre = values - jnp.mean(values, -1, keepdims=True)
    factor = lax.rsqrt(jnp.mean(centre * centre, -1, keepdims=True) + 1e-06)
    return centre * factor, factor


def norm_back(grad, normed, factor):
    return factor * (
        grad - jnp.mean(grad, -1, keepdims=True) - normed * jnp.mean(grad * normed, -1, keepdims=True)
    )


def gelu_both(u):
    t = pl.reciprocal(1.0 + (0.3275911 * 0.7071067811865476) * jnp.abs(u))
    bell = jnp.exp(u * (u * -0.5))
    poly = t * (
        0.127414796 + t * (-0.142248368 + t * (0.7107068705 + t * (-0.7265760135 + t * 0.5307027145)))
    )
    tail = poly * bell
    phi = jnp.where(u >= 0.0, 1.0 - tail, tail)
    return u * phi, phi + u * bell * 0.3989422804014327


def split_low(values):
    high = values.astype(BF16).astype(F32)
    return high, values - high


def load_weights(info, parts, weights, sems, rel, rows, beside=None):
    c, me = info[0], info[1]
    copies = []
    for side, part in enumerate(parts):
        t = c ^ side
        for k, r in enumerate(rel):
            where = pl.multiple_of((me ^ r) * rows, 16)
            copies.append(
                pltpu.make_async_copy(part.at[k], weights.at[t, pl.ds(where, rows), :], sems.at[side, k])
            )
    for copy in copies:
        copy.start()
    if beside is not None:
        beside()
    for copy in copies:
        copy.wait()


def head_mask(which):
    lane = iota((ROWS, LANES), 1)
    return (lane < HD) if which == 0 else (lane >= HD)


def forward_kernel(rel, rows, info, tok, mask, *refs):
    i = pl.program_id(0)
    w_parts, refs = refs[:-10], refs[-10:]
    src, mid, proj, att, lse, gates, weights, gains, xs, sems = refs
    shares, _, cols = weights.shape
    local = (cols - LANES) // 4
    aux_at = 4 * local

    @pl.when(i == 0)
    def _():
        load_weights(info, w_parts, weights, sems, rel, rows)
        gains[...] = weights[0, :, aux_at:].astype(F32).T[0:16, :]

    @pl.when(info[LIVE + i] == 1)
    def _():
        xs[192:ROWS, :] = jnp.zeros((ROWS - 192, 512), F32)
        xs[0:SEQ, :] = tok[0, 0].astype(F32)
        x = xs[...]
        normed, _ = layer_stats(x)
        act = (normed * gains[8:9, :]).astype(BF16)
        for t in range(shares):
            proj[0, :, t * 3 * local : (t + 1) * 3 * local] = mm(act, weights[t, :, 0 : 3 * local]).astype(BF16)
        key_ok = iota((ROWS, ROWS), 1) < SEQ
        lane = iota((ROWS, LANES), 1)
        saved = jnp.zeros((ROWS, LANES), F32)
        for t in range(shares):
            for p in range(local // LANES):
                at = t * 3 * local + p * LANES
                q = proj[0, :, at : at + LANES]
                k = proj[0, :, at + local : at + local + LANES]
                v = proj[0, :, at + 2 * local : at + 2 * local + LANES]
                halves = []
                for h in range(2):
                    qm = jnp.where(head_mask(h), q.astype(F32), 0.0).astype(BF16)
                    s = jnp.where(key_ok, nt(qm, k) * (HD**-0.5), -1e30)
                    top = jnp.max(s, -1, keepdims=True)
                    e = jnp.exp(s - top)
                    total = jnp.sum(e, -1, keepdims=True)
                    probs = (e * (1.0 / total)).astype(BF16)
                    halves.append(mm(probs, v))
                    saved = jnp.where(lane == (t * local + p * LANES) // HD + h, top + jnp.log(total), saved)
                att[0, :, t * local + p * LANES : t * local + (p + 1) * LANES] = jnp.where(
                    lane < HD, halves[0], halves[1]
                ).astype(BF16)
        lse[0] = saved
        branch = nt(att[0, :, 0:local], weights[0, :, 3 * local : aux_at])
        for t in range(1, shares):
            branch = branch + nt(att[0, :, t * local : (t + 1) * local], weights[t, :, 3 * local : aux_at])
        middle = x + branch
        mid[0] = middle
        normed2, _ = layer_stats(middle)
        act2 = (normed2 * gains[9:10, :]).astype(BF16)
        src[0, :, 0:512] = act2
        chosen = mask[0, 0].astype(F32)
        logits = jnp.where(chosen > 0.0, mm(act2, weights[0, :, aux_at:]), -1e30)
        top = jnp.max(logits, -1, keepdims=True)
        e = jnp.exp(logits - top) * chosen
        gate = e / jnp.maximum(jnp.sum(e, -1, keepdims=True), 0.5)
        gates[0] = gate
        high, low = split_low(gate)
        src[0, :, 512:640] = (high + pltpu.roll(low, 8, 1)).astype(BF16)


def blocks_of(info, i, e):
    begin, end = info[START + i * 8 + e], info[START + i * 8 + 8 + e]
    first = begin // FEW
    return first, jnp.where(end > begin, (end + FEW - 1) // FEW - first, 0)


def places(info, i, mask):
    chosen = mask[0, 0]
    lower = (iota((ROWS, ROWS), 0) > iota((ROWS, ROWS), 1)).astype(F32).astype(BF16)
    lane = iota((1, LANES), 1)
    shift = jnp.zeros((1, LANES), F32)
    base = 0
    for e in range(EXPERTS):
        _, count = blocks_of(info, i, e)
        shift = jnp.where(lane == e, (base * FEW + info[START + i * 8 + e] % FEW).astype(F32), shift)
        base = base + count
    return jnp.where(chosen.astype(F32) > 0.0, mm(lower, chosen) + shift, -1.0)


def dispatch_kernel(with_act, count, info, *refs):
    i = pl.program_id(0)
    if with_act:
        own, oth, mask, x_hbm, xbuf, tbuf, pbuf, res, sems = refs
    else:
        gy, mask, x_hbm, xbuf, tbuf, pbuf, res, sems = refs
    cols = res.shape[1]

    @pl.when(i == 0)
    def _():
        tbuf[...] = jnp.zeros(tbuf.shape, BF16)
        pbuf[...] = jnp.full(pbuf.shape, -1.0, F32)

    @pl.when(info[LIVE + i] == 1)
    def _():
        if with_act:

            @pl.when(i < count)
            def _():
                tbuf[0:ROWS, :] = own[0]

            @pl.when(i >= count)
            def _():
                tbuf[0:ROWS, :] = oth[0]
        else:
            tbuf[0:SEQ, :] = gy[0, 0]
        pbuf[0:ROWS, :] = places(info, i, mask)
        place = pbuf[...].T[0:EXPERTS, :]
        high = jnp.max(place, 0, keepdims=True)
        low = jnp.min(jnp.where(place < 0.0, 4096.0, place), 0, keepdims=True)
        row = iota((MOST, TILE), 0).astype(F32)
        pick = jnp.where((row == high) | (row == low), 1.0, 0.0).astype(BF16)
        res[0:MOST, :] = mm(pick, tbuf[...]).astype(BF16)
        base = 0
        for e in range(EXPERTS):
            first, blocks = blocks_of(info, i, e)
            off = info[START + i * 8 + e] % FEW

            @pl.when(blocks > 0)
            def _():
                to = pl.ds(pl.multiple_of(first * FEW, FEW), FEW)
                new = res[pl.ds(pl.multiple_of(base * FEW, FEW), FEW), :].astype(F32)
                old = xbuf[e, to, :].astype(F32)
                xbuf[e, to, :] = jnp.where(iota((FEW, cols), 0) < off, old, new).astype(BF16)

            def move(k, carry):
                to = pl.ds(pl.multiple_of((first + 1 + SEVERAL * k) * FEW, FEW), SEVERAL * FEW)
                at = pl.ds(pl.multiple_of((base + 1 + SEVERAL * k) * FEW, FEW), SEVERAL * FEW)
                xbuf[e, to, :] = res[at, :]
                return carry

            lax.fori_loop(0, (blocks + SEVERAL - 2) // SEVERAL, move, 0)
            base = base + blocks

    @pl.when(i == 15)
    def _():
        for e in range(EXPERTS):
            end = pl.multiple_of((info[TOTAL + e] + FEW - 1) // FEW * FEW, FEW)
            xbuf[e, pl.ds(end, TILE), :] = jnp.zeros((TILE, cols), BF16)
        for start in (True, False):
            for e in range(EXPERTS):
                for k in range(SLOTS // TILE):

                    @pl.when(k * TILE < jnp.maximum(info[TOTAL + e], 1))
                    def _():
                        rows = pl.ds(k * TILE, TILE)
                        copy = pltpu.make_async_copy(xbuf.at[e, rows, :], x_hbm.at[e, rows, :], sems.at[e, k])
                        if start:
                            copy.start()
                        else:
                            copy.wait()


def expert_kernel(number, plan, fast, rows, n_pieces, info, xa, xg, *refs):
    pieces, refs = refs[:n_pieces], refs[n_pieces:]
    w_in, w_out, acc_in, acc_out, staged, sems, sent_sems = refs[-7:]
    y, grads = refs[0], refs[1:-7]
    i = pl.program_id(0)
    n = info[FIRST + number + 1] - info[FIRST + number]
    at = info[FIRST + number] + jnp.minimum(i, n - 1)
    expert = info[OWNER + at]
    slot = expert % 2

    def owned_by(far, flip):
        return pl.multiple_of((info[RING + far % 8] ^ flip) * rows, 16)

    def copies(ex, to, start):
        for side, (entries, buf) in enumerate(zip(plan, (w_in, w_out))):
            for k, (owner, sources) in enumerate(entries):
                where = owned_by(*owner) if isinstance(owner, tuple) else owner * rows
                for ref, b, low, high in sources:
                    copy = pltpu.make_async_copy(
                        pieces[ref].at[b, ex - low], buf.at[to, pl.ds(where, rows), :], sems.at[to, side, k]
                    )

                    @pl.when((ex >= low) & (ex < high))
                    def _():
                        if start:
                            copy.start()
                        else:
                            copy.wait()

    @pl.when(i == 0)
    def _():
        copies(expert, slot, True)

    @pl.when((info[PART + at] == 0) & (i < n))
    def _():
        copies(expert, slot, False)

        @pl.when(expert + 1 < sum(CALLS[number]))
        def _():
            copies(expert + 1, 1 - slot, True)

    @pl.when(i < n)
    def _():
        rows_x = xa[0, :, 0:512]
        g = xg[0].astype(F32)
        lane = iota((TILE, LANES), 1)
        mine = (lane == expert) | (lane == expert + 8)
        gate = jnp.sum(jnp.where(mine, xa[0, :, 512:640].astype(F32), 0.0), -1, keepdims=True)
        inner = mm(rows_x, w_in[slot])
        act, slope = gelu_both(inner)
        hid = act.astype(BF16)
        out = nt(hid, w_out[slot])
        deo = (gate * g).astype(BF16)
        dinner = (mm(deo, w_out[slot]) * slope).astype(BF16)
        dgate = jnp.sum(g * out, -1, keepdims=True)
        high, low = split_low(dgate)
        y[0, :, 0:512] = (gate * out).astype(BF16)
        y[0, :, 512:1024] = nt(dinner, w_in[slot]).astype(BF16)
        y[0, :, 1024:1152] = jnp.where(lane == expert, high, jnp.where(lane == expert + 8, low, 0.0)).astype(BF16)

        @pl.when(info[PART + at] == 0)
        def _():
            acc_in[...] = tn(rows_x, dinner)
            acc_out[...] = tn(deo, hid)

        @pl.when(info[PART + at] > 0)
        def _():
            acc_in[...] += tn(rows_x, dinner)
            acc_out[...] += tn(deo, hid)

    def sends(to, start):
        if fast:
            parts = []
            for k, far in enumerate(FIRST_FAR + THEN_FAR):
                turned, place = (8, k) if k < len(FIRST_FAR) else (9, k - len(FIRST_FAR))
                parts += [
                    (0, owned_by(far, 0), grads[k].at[0, to]),
                    (1, owned_by(far, 0), grads[k].at[1, to]),
                    (1, owned_by(far, 1), grads[k].at[2, to]),
                    (0, owned_by(far, 1), grads[turned].at[place, to]),
                ]
        else:
            parts = [(side, 0, grads[side].at[to]) for side in range(2)]
        for k, (side, where, out) in enumerate(parts):
            copy = pltpu.make_async_copy(staged.at[side, pl.ds(where, rows), :], out, sent_sems.at[k])
            if start:
                copy.start()
            else:
                copy.wait()

    opening = CALLS[number][0]

    @pl.when((i == n - 1) | ((i < n) & (info[PART + at + 1] == 0)))
    def _():
        @pl.when(expert > opening)
        def _():
            sends(expert - opening - 1, False)

        staged[0] = acc_in[...].astype(BF16)
        staged[1] = acc_out[...].astype(BF16)
        sends(expert - opening, True)

    @pl.when(i == pl.num_programs(0) - 1)
    def _():
        sends(CALLS[number][1] - 1, False)


def at_call(expert):
    return [(k, expert - first) for k, (first, count) in enumerate(CALLS) if first <= expert < first + count][0]


def add_kernel(step, counts, *refs):
    second = pl.program_id(0) == 1
    calls = len(counts)
    ways = 1 if step in (0, 3) else 2

    def pick(parts):
        if calls == 1:
            return parts[0][...].astype(F32)
        return jnp.where(second, parts[1][...].astype(F32), parts[0][...].astype(F32))

    sums = []
    for _ in range(ways):
        q, x, refs = pick(refs[:calls]), pick(refs[calls : 2 * calls]), refs[2 * calls :]
        sums.append((q[0:1] + x, q[1:3]))
    if step == 0:
        for out, here in zip(refs, (jnp.logical_not(second), second)):

            @pl.when(here)
            def _():
                out[0:1] = sums[0][0].astype(BF16)
                out[1:3] = sums[0][1].astype(BF16)
    elif step == 3:
        up, down, first, second, third = refs
        first[...] = (sums[0][0] + up[0:1].astype(F32) + down[0:1].astype(F32))[0]
        rest = sums[0][1] + up[1:3].astype(F32) + down[1:3].astype(F32)
        second[...] = rest[0]
        third[...] = rest[1].astype(BF16)
    else:
        for k in range(2):
            arrived, out = refs[k][...].astype(F32), refs[2 + k]
            if step == 1:
                arrived = jnp.where(second, 0.0, arrived) if k == 0 else jnp.where(second, arrived, 0.0)
            out[0:1] = (sums[k][0] + arrived[0:1]).astype(BF16)
            out[1:3] = (sums[k][1] + arrived[1:3]).astype(BF16)


def combine_kernel(base, info, *refs):
    y_parts, (mask, out, ybuf, sems) = refs[:-4], refs[-4:]
    i = pl.program_id(0)
    slot = i % 2

    def fetch(j, buf, start):
        @pl.when(info[LIVE + base + j] == 1)
        def _():
            at = 0
            for e in range(EXPERTS):
                first, blocks = blocks_of(info, base + j, e)

                def move(k, carry, e=e, first=first, at=at):
                    copy = pltpu.make_async_copy(
                        y_parts[at_call(e)[0]].at[at_call(e)[1], pl.ds(pl.multiple_of((first + k) * FEW, FEW), FEW), :],
                        ybuf.at[buf, pl.ds(pl.multiple_of((at + k) * FEW, FEW), FEW), :],
                        sems.at[buf],
                    )
                    if start:
                        copy.start()
                    else:
                        copy.wait()
                    return carry

                lax.fori_loop(0, blocks, move, 0)
                at = at + blocks

    @pl.when(i == 0)
    def _():
        ybuf[...] = jnp.zeros(ybuf.shape, BF16)
        fetch(i, slot, True)

    @pl.when(i + 1 < pl.num_programs(0))
    def _():
        fetch(i + 1, 1 - slot, True)

    fetch(i, slot, False)

    @pl.when(info[LIVE + base + i] == 1)
    def _():
        place = places(info, base + i, mask)
        high = jnp.max(place, -1, keepdims=True)
        low = jnp.min(jnp.where(place < 0.0, 4096.0, place), -1, keepdims=True)
        lane = iota((ROWS, MOST), 1).astype(F32)
        pick = jnp.where((lane == high) | (lane == low), 1.0, 0.0).astype(BF16)
        if out.dtype == F32:
            out[0] = mm(pick, ybuf[slot])
        else:
            out[0, :, 0:1024] = mm(pick, ybuf[slot, :, 0:1024]).astype(BF16)
            aux = mm(pick, ybuf[slot, :, 1024:1152])
            both = jnp.where(iota((ROWS, LANES), 1) < 8, aux + pltpu.roll(aux, LANES - 8, 1), 0.0)
            high, low = split_low(both)
            out[0, :, 1024:1152] = (high + pltpu.roll(low, 8, 1)).astype(BF16)


def assemble_kernel(shares, info, *refs):
    parts, (out, scratch) = refs[:-2], refs[-2:]
    c = info[0]
    for micro in range(2):

        @pl.when(pl.program_id(0) == micro)
        def _():
            for side in range(shares):
                some = [(a, j) for a in parts[3 * side : 3 * side + 3] for j in range(a.shape[0])]
                here = some[: len(some) // 2] if micro == 0 else some[len(some) // 2 :]
                for slot, (part, j) in enumerate(here):
                    for k in range(4):
                        values = part[j, 0:SEQ, k * LANES : (k + 1) * LANES].astype(F32)
                        scratch[k, pl.ds(shares * slot + (c ^ side), SEQ, stride=8), :] = values

    for k in range(4):
        out[0, :, :, k * LANES : (k + 1) * LANES] = scratch[k].reshape(SEQ, 8, LANES).astype(BF16)


def backward_kernel(
    base,
    rel,
    order,
    rows,
    info,
    tok,
    gy_ref,
    comb_own,
    comb_oth,
    mid,
    proj,
    att,
    lse,
    gates,
    *refs,
):
    i = pl.program_id(0)
    c, me = info[0], info[1]
    scratch, refs = refs[-12:], refs[:-12]
    weights, gains, twice, xs, gs, wide, dproj, acc_qkv, acc_out, acc_router, acc_gain, sems = scratch
    shares, _, cols = weights.shape
    w_parts, refs = refs[:shares], refs[shares:]
    block_out, grad_tok = refs[:2]
    grads = refs[2:]
    local = (cols - LANES) // 4
    aux_at = 4 * local

    @pl.when(i == 0)
    def _():
        def clear():
            wide[...] = jnp.zeros(wide.shape, F32)
            acc_qkv[...] = jnp.zeros(acc_qkv.shape, F32)
            acc_out[...] = jnp.zeros(acc_out.shape, F32)
            acc_router[...] = jnp.zeros(acc_router.shape, F32)
            acc_gain[...] = jnp.zeros(acc_gain.shape, F32)

        load_weights(info, w_parts, weights, sems, rel, rows, clear)
        aux = weights[0, :, aux_at:].astype(F32)
        gains[...] = aux.T[0:16, :]
        lane = iota((512, LANES), 1)
        router = jnp.where(lane < 8, aux, 0.0)
        twice[...] = (router + pltpu.roll(router, 8, 1)).astype(BF16)

    @pl.when(info[LIVE + base + i] == 0)
    def _():
        block_out[...] = jnp.zeros(block_out.shape, BF16)
        grad_tok[...] = jnp.zeros(grad_tok.shape, BF16)

    @pl.when(info[LIVE + base + i] == 1)
    def _():
        xs[192:ROWS, :] = jnp.zeros((ROWS - 192, 512), F32)
        xs[0:SEQ, :] = tok[0, 0].astype(F32)
        gs[192:ROWS, :] = jnp.zeros((ROWS - 192, 512), F32)
        gs[0:SEQ, :] = gy_ref[0, 0].astype(F32)
        gy = gs[...]
        lane = iota((ROWS, LANES), 1)
        middle = mid[0]
        mixed = comb_own[0, :, 0:512] + comb_oth[0, :, 0:512].astype(F32)
        block_out[0] = (middle + mixed).astype(BF16)
        normed2, factor2 = layer_stats(middle)
        act2 = (normed2 * gains[9:10, :]).astype(BF16)
        gate = gates[0]
        aux = comb_own[0, :, 1024:1152] + comb_oth[0, :, 1024:1152].astype(F32)
        dgate = jnp.where(lane < 8, aux + pltpu.roll(aux, LANES - 8, 1), 0.0)
        dlogits = gate * (dgate - jnp.sum(gate * dgate, -1, keepdims=True))
        high, low = split_low(dlogits)
        packed = (high + pltpu.roll(low, 8, 1)).astype(BF16)
        acc_router[...] += tn(act2, packed)
        dact2 = (
            comb_own[0, :, 512:1024] + comb_oth[0, :, 512:1024].astype(F32) + nt(packed, twice[...])
        )
        acc_gain[9:10, :] += jnp.sum(dact2 * normed2, 0, keepdims=True)
        dmiddle = gy + norm_back(dact2 * gains[9:10, :], normed2, factor2)
        gs[...] = dmiddle
        dbranch = dmiddle.astype(BF16)
        x = xs[...]
        normed1, factor1 = layer_stats(x)
        act1 = (normed1 * gains[8:9, :]).astype(BF16)
        key_ok = iota((ROWS, ROWS), 0) < SEQ
        wide[0:ROWS, :] = lse[0]
        sums = wide[...].T
        for t in range(shares):
            acc_out[t] += tn(dbranch, att[0, :, t * local : (t + 1) * local])
            datt_t = mm(dbranch, weights[t, :, 3 * local : aux_at]).astype(BF16)
            for p in range(local // LANES):
                at = t * 3 * local + p * LANES
                q = proj[0, :, at : at + LANES]
                k = proj[0, :, at + local : at + local + LANES]
                v = proj[0, :, at + 2 * local : at + 2 * local + LANES]
                datt = datt_t[:, p * LANES : (p + 1) * LANES]
                parts = []
                for h in range(2):
                    qm = jnp.where(head_mask(h), q.astype(F32), 0.0).astype(BF16)
                    dm = jnp.where(head_mask(h), datt.astype(F32), 0.0).astype(BF16)
                    head = (t * local + p * LANES) // HD + h
                    s = nt(k, qm) * (HD**-0.5) - sums[head : head + 1, 0:ROWS]
                    probs = jnp.where(key_ok, jnp.exp(jnp.where(key_ok, s, 0.0)), 0.0)
                    dprobs = nt(v, dm)
                    ds = (probs * (dprobs - jnp.sum(dprobs * probs, 0, keepdims=True))).astype(BF16)
                    parts.append((tn(ds, k), mm(ds, q), mm(probs.astype(BF16), datt)))
                for j in range(3):
                    both = jnp.where(lane < HD, parts[0][j], parts[1][j])
                    if j < 2:
                        both = both * (HD**-0.5)
                    dproj[:, at + j * local : at + j * local + LANES] = both.astype(BF16)
        dact1 = jnp.zeros((ROWS, 512), F32)
        for t in range(shares):
            dp = dproj[:, t * 3 * local : (t + 1) * 3 * local]
            acc_qkv[t] += tn(act1, dp)
            dact1 = dact1 + nt(dp, weights[t, :, 0 : 3 * local])
        acc_gain[8:9, :] += jnp.sum(dact1 * normed1, 0, keepdims=True)
        total = gs[...] + norm_back(dact1 * gains[8:9, :], normed1, factor1)
        grad_tok[0] = total.astype(BF16)

    @pl.when(i == pl.num_programs(0) - 1)
    def _():
        lane = iota((512, LANES), 1)
        router = acc_router[...]
        aux = jnp.where(lane < 8, router + pltpu.roll(router, LANES - 8, 1), acc_gain[...].T)
        acc_router[...] = aux
        for k, r in enumerate(order):
            where = pl.ds(pl.multiple_of((me ^ r) * rows, 16), rows)
            for side, out in enumerate(grads):
                out[k, :, 0 : 3 * local] = acc_qkv[c ^ side, where, :].astype(BF16)
                out[k, :, 3 * local : aux_at] = acc_out[c ^ side, where, :].astype(BF16)
                out[k, :, aux_at:] = acc_router[where, :].astype(BF16)


def swap(n, bit):
    return [(i, i ^ bit) for i in range(n)]


def hop(a, n, bits):
    return lax.ppermute(a, "dp", swap(n, bits))


def plus(*parts):
    return sum(a.astype(F32) for a in parts).astype(BF16)


def order(token, *lists):
    out = list(lax.optimization_barrier((token, *[a for arrays in lists for a in arrays])))
    got, out = [out[0]], out[1:]
    for arrays in lists:
        got.append(out[: len(arrays)])
        out = out[len(arrays) :]
    return got


def in_turn(kernel, operands):
    def run(info, earlier, *refs):
        ran, refs = refs[operands], refs[:operands] + refs[operands + 1 :]

        @pl.when(pl.program_id(0) == 0)
        def _():
            ran[...] = jnp.zeros(ran.shape, F32)

        kernel(info, *refs)

    return run


def cost(microseconds):
    return pl.CostEstimate(flops=int(microseconds * SCALE), bytes_accessed=1000, transcendentals=0)


def call(kernel, grid, token, args, in_specs, out_specs, out_shape, scratch, name, microseconds):
    token, info = token
    got = pl.pallas_call(
        in_turn(kernel, len(args)),
        grid_spec=pltpu.PrefetchScalarGridSpec(
            num_scalar_prefetch=1,
            grid=grid,
            in_specs=[any_spec()] + in_specs,
            out_specs=[pl.BlockSpec((8, LANES), lambda i, s: (0, 0))] + out_specs,
            scratch_shapes=scratch,
        ),
        out_shape=[shape((8, LANES), F32)] + out_shape,
        compiler_params=params(),
        cost_estimate=cost(microseconds),
        name=name,
    )(info, token, *args)
    return (got[0], info), got[1:]


def ring(a, n, way):
    pairs = []
    for at, here in enumerate(AROUND):
        there = AROUND[(at + way) % len(AROUND)]
        pairs += [(here, there), (here ^ 1, there ^ 1)]
    return lax.ppermute(a, "dp", pairs)


def shifted(r):
    return tuple(z ^ r for z in FAR)


def gather_line(shard, n):
    near = shard[None]
    near = jnp.concatenate([near, hop(near, n, 8)], 0)
    return jnp.concatenate([near, hop(near, n, 4)], 0)


def scatter_corner(whole, n):
    return [hop(whole[12:14], n, 1), hop(whole[14:16], n, 2)]


def scatter_square(whole, arrived, n):
    by_x, by_y = whole[4:8], whole[8:12]
    by_y = jnp.concatenate([plus(by_y[:2], arrived[0]), by_y[2:]], 0)
    by_x = jnp.concatenate([by_x[:2], plus(by_x[2:], arrived[1])], 0)
    return [whole[0:4], hop(by_x, n, 1), hop(by_y, n, 2)]


def any_spec():
    return pl.BlockSpec(memory_space=pl.ANY)


def params():
    return pltpu.CompilerParams(vmem_limit_bytes=VMEM)


def shape(s, d):
    return jax.ShapeDtypeStruct(s, d)


def body(
    n,
    shares,
    tokens,
    held,
    routes,
    ln1_gain,
    qkv_weight,
    out_weight,
    ln2_gain,
    router_weight,
    expert_in,
    expert_out,
    grad_out,
):
    rows = qkv_weight.shape[1]
    width = expert_in.shape[2]
    local = qkv_weight.shape[2]
    pack = 4 * local + LANES
    mine_count = 16 // shares
    per_micro = 8 // shares
    fast = n == 16 and rows % 16 == 0
    c = lax.axis_index("tensor")
    me = lax.axis_index("dp")
    if fast:
        block = rows
        rel = FAR + shifted(1) + shifted(2) + shifted(3)
        orders = (FAR, shifted(1), shifted(2), shifted(3))
    else:
        block = 512
        rel = (0,)
        orders = ((0,),)
    blocks = len(rel)
    spot = me if fast else jnp.zeros((), jnp.int32)

    def tables(routes, held):
        live = jnp.arange(8, dtype=jnp.int32)[None, :] < held
        lane = jnp.arange(LANES, dtype=jnp.int32)
        picked = (routes[..., 0:1] == lane) | (routes[..., 1:2] == lane)
        picked = (picked & live[:, :, None, None]).astype(BF16)
        mask = jnp.pad(picked, ((0, 0), (0, 0), (0, ROWS - SEQ), (0, 0)))
        counts = jnp.sum(
            (routes[..., None] == jnp.arange(EXPERTS, dtype=jnp.int32)).astype(jnp.int32), (2, 3)
        ) * live.astype(jnp.int32)[:, :, None]

        def own_first(a):
            a = a.reshape((2, per_micro, shares) + a.shape[2:])
            out = []
            for r in range(shares):
                part = a[:, :, 0]
                for t in range(1, shares):
                    part = jnp.where(c ^ r == t, a[:, :, t], part)
                out.append(part.reshape((mine_count,) + a.shape[3:]))
            return jnp.concatenate(out, 0)

        counts = own_first(counts)
        live_list = own_first(live.astype(jnp.int32))
        ends = jnp.sum(
            jnp.where(jnp.arange(16)[:, None, None] >= jnp.arange(16)[None, :, None], counts[None], 0), 1
        )
        tiles = jnp.maximum((ends[15] + TILE - 1) // TILE, 1)
        numbers = jnp.arange(EXPERTS)
        tile_ends = jnp.sum(jnp.where(numbers[:, None] >= numbers[None, :], tiles[None, :], 0), 1)
        listed = jnp.arange(TILES)
        passed = (listed[:, None] >= tile_ends[None, :]).astype(jnp.int32)
        owner = jnp.minimum(jnp.sum(passed, 1), EXPERTS - 1)
        part = listed - jnp.sum(passed * tiles[None, :], 1)
        places = jnp.array(AROUND, jnp.int32)
        at = jnp.sum(jnp.where(places == (spot & 14), numbers, 0))
        around = jnp.sum(jnp.where((at + numbers)[:, None] % 8 == numbers[None, :], places[None, :], 0), 1) | (spot & 1)
        call_ends = [tile_ends[first + count - 1] for first, count in CALLS]
        call_starts = jnp.stack([jnp.zeros((), jnp.int32), *call_ends])
        info = jnp.concatenate(
            [
                jnp.stack([c, spot]).astype(jnp.int32),
                jnp.zeros((LIVE - 2,), jnp.int32),
                live_list,
                jnp.zeros((START - LIVE - 16,), jnp.int32),
                (ends - counts).reshape(-1),
                ends[15],
                jnp.zeros((TABLE - TOTAL - EXPERTS,), jnp.int32),
                owner,
                part,
                call_starts,
                jnp.zeros((RING - FIRST - 1 - len(CALLS),), jnp.int32),
                around,
            ]
        ).astype(jnp.int32)
        return mask, info

    def image(i, s):
        j = i % mine_count
        return (j // per_micro, shares * (j % per_micro) + (s[0] ^ (i // mine_count)), 0, 0)

    tok_spec = pl.BlockSpec((1, 1, SEQ, 512), image)
    mask_spec = pl.BlockSpec((1, 1, ROWS, LANES), image)

    def row_spec(cols):
        return pl.BlockSpec((1, ROWS, cols), lambda i, s: (i, 0, 0))

    def dispatch(token, with_act, cols, specs, args):
        return call(
            functools.partial(dispatch_kernel, with_act, mine_count),
            (16,),
            token,
            args + [mask],
            specs + [mask_spec],
            [any_spec()],
            [shape((EXPERTS, SLOTS, cols), BF16)],
            [
                pltpu.VMEM((EXPERTS, SPAN, cols), BF16),
                pltpu.VMEM((TILE, cols), BF16),
                pltpu.VMEM((TILE, LANES), F32),
                pltpu.VMEM((MOST + SEVERAL * FEW, cols), BF16),
                pltpu.SemaphoreType.DMA((EXPERTS, SLOTS // TILE)),
            ],
            "dispatch",
            20,
        )

    aux = jnp.concatenate(
        [router_weight, ln1_gain[:, None], ln2_gain[:, None], jnp.zeros((rows, LANES - 10), BF16)], 1
    )
    small = jnp.concatenate([qkv_weight[0], qkv_weight[1], qkv_weight[2], out_weight.T, aux], 1)
    if fast:
        line = gather_line(small, n)

        by_x, by_y = hop(line, n, 1), hop(line, n, 2)
    else:
        mask, info = tables(routes, held)
        w_own = lax.all_gather(small, "dp", axis=0, tiled=True)[None]
        token = (mask[0, 0, :8, :].astype(F32), info)

    def across(a, r):
        return lax.ppermute(a, "tensor", swap(shares, r))

    shard = jnp.stack([expert_in, jnp.swapaxes(expert_out, 1, 2)])
    half = EXPERTS // 2

    def next_ring(two):
        return [ring(two[0], n, 1), ring(two[1], n, -1)]

    def over_x(blocks, axis=0):
        return hop(jnp.concatenate([b[:1] for b in blocks], axis), n, 1)

    if not fast:
        gathered = lax.all_gather(shard, "dp", axis=2, tiled=True)
        plan = [[(0, [(0, side, 0, EXPERTS)])] for side in range(2)]
    else:
        x0 = [hop(shard[1:], n, 1)]
        shard, (line,) = order(shard, [line])
        one = next_ring([shard, shard])
        turned = next_ring([x0[0], x0[0]])
        by_x, (by_y, later), (routes, held, grad_out) = order(by_x, [by_y, shard[:1]], [routes, held, grad_out])
        x0.append(hop(later, n, 1))
        mask, info = tables(routes, held)
        w_own = jnp.concatenate([line, by_x, by_y, hop(by_y, n, 1)], 0)
        token = (mask[0, 0, :8, :].astype(F32), info)
        plan = [[], []]
        for side in range(2):
            plan[side].append(((0, 0), [(0, side, 0, EXPERTS)]))
            plan[side].append(((0, 1), [(2 - side, 0, 0, EXPERTS)]))
            for k in range(1, 4):
                for b, far in enumerate((-k, k)):
                    plan[side].append(((far, 0), [(2 * k + 1 + b, side, 0, EXPERTS)]))
                    others = [(2 * k + 1 + b, 2, 0, EXPERTS)] if side == 1 else [(10 + k, b, 0, EXPERTS)]
                    if side == 0 and k == 3:
                        others = [(13, b, 0, half), (14, b, half, EXPERTS)]
                    plan[side].append(((far, 1), others))
            plan[side].append(((4, 0), [(9, side, 0, half), (10, side, half, EXPERTS)]))
            others = [(9, 2, 0, half), (10, 2, half, EXPERTS)] if side == 1 else [(15, 0, 0, half), (16, 0, half, EXPERTS)]
            plan[side].append(((4, 1), others))

    w_parts = [w_own] + [across(w_own, r) for r in range(1, shares)]
    if fast:
        first, one, turned, (x0[1],), w_parts = order(token[0], one, turned, x0[1:], w_parts)
        token = (first, info)
        one = [jnp.concatenate(pair, 0) for pair in zip(one, turned)]
        two = next_ring(one)
        x1 = over_x(one)
    token, (src, mid, proj, att, lse, gates) = call(
        functools.partial(forward_kernel, rel, block),
        (mine_count,),
        token,
        [tokens, mask, *w_parts],
        [tok_spec, mask_spec] + [any_spec()] * shares,
        [row_spec(640), row_spec(512), row_spec(1536), row_spec(512), row_spec(LANES), row_spec(LANES)],
        [
            shape((mine_count, ROWS, 640), BF16),
            shape((mine_count, ROWS, 512), F32),
            shape((mine_count, ROWS, 1536), BF16),
            shape((mine_count, ROWS, 512), BF16),
            shape((mine_count, ROWS, LANES), F32),
            shape((mine_count, ROWS, LANES), F32),
        ],
        [
            pltpu.VMEM((shares, 512, pack), BF16),
            pltpu.VMEM((16, 512), F32),
            pltpu.VMEM((ROWS, 512), F32),
            pltpu.SemaphoreType.DMA((shares, blocks)),
        ],
        "forward",
        23,
    )

    if fast:
        first, (src, mid, proj, att, lse, gates), two, (x1,) = order(
            token[0], [src, mid, proj, att, lse, gates], two, [x1]
        )
        token = (first, info)
        three = next_ring(two)
        x2 = over_x(two)
    src_oth = [across(src, r) for r in range(1, shares)]
    src_oth = src_oth[0] if shares == 2 else jnp.concatenate(src_oth, 0)
    token, (rows_a,) = dispatch(
        token,
        True,
        640,
        [
            pl.BlockSpec((1, ROWS, 640), lambda i, s: (jnp.minimum(i, mine_count - 1), 0, 0)),
            pl.BlockSpec((1, ROWS, 640), lambda i, s: (jnp.maximum(i - mine_count, 0), 0, 0)),
        ],
        [src, src_oth],
    )
    if fast:
        first, (rows_a,), three, (x2,) = order(token[0], [rows_a], three, [x2])
        token = (first, info)
        four = [ring(three[0][:, :half], n, 1), ring(three[1][:, half:], n, -1)]
        x3 = [over_x([a[:, :half] for a in three])]
    token, (rows_g,) = dispatch(token, False, 512, [tok_spec], [grad_out])

    def run_experts(token, number, pieces):
        opening, count = CALLS[number]

        def tile_at(i, s):
            at = jnp.minimum(s[FIRST + number] + i, s[FIRST + number + 1] - 1)
            return s[OWNER + at], s[PART + at]

        def out_at(i, s):
            e, t = tile_at(i, s)
            return e - opening, t, 0

        if fast:
            grad_shapes = [shape((3, count, block, width), BF16)] * 8
            for far in (FIRST_FAR, THEN_FAR):
                grad_shapes.append(shape((len(far), count, block, width), BF16))
        else:
            grad_shapes = [shape((count, block, width), BF16)] * 2
        return call(
            functools.partial(expert_kernel, number, plan, fast, block, len(pieces)),
            (count * SLOTS // TILE,),
            token,
            [rows_a, rows_g, *pieces],
            [
                pl.BlockSpec((1, TILE, 640), lambda i, s: (*tile_at(i, s), 0)),
                pl.BlockSpec((1, TILE, 512), lambda i, s: (*tile_at(i, s), 0)),
            ]
            + [any_spec()] * len(pieces),
            [pl.BlockSpec((1, TILE, 1152), out_at)] + [any_spec()] * len(grad_shapes),
            [shape((count, SPAN, 1152), BF16)] + grad_shapes,
            [
                pltpu.VMEM((2, 512, width), BF16),
                pltpu.VMEM((2, 512, width), BF16),
                pltpu.VMEM((512, width), F32),
                pltpu.VMEM((512, width), F32),
                pltpu.VMEM((2, 512, width), BF16),
                pltpu.SemaphoreType.DMA((2, 2, blocks)),
                pltpu.SemaphoreType.DMA((32,)),
            ],
            "expert",
            10 * count,
        )

    def combine(token, base, dtype):
        return call(
            functools.partial(combine_kernel, base),
            (mine_count,),
            token,
            [*y_parts, mask],
            [any_spec()] * len(y_parts) + [pl.BlockSpec((1, 1, ROWS, LANES), lambda i, s: image(i + base, s))],
            [row_spec(1152)],
            [shape((mine_count, ROWS, 1152), dtype)],
            [pltpu.VMEM((2, MOST, 1152), BF16), pltpu.SemaphoreType.DMA((2,))],
            "combine",
            14,
        )

    def turn(k, side):
        return hop(got[k][9 + side], n, 1)

    def ring_sums(group, step, ks, *arrived):
        counts = [CALLS[c][1] for c in GROUPS[group]]
        half = sum(counts) // 2
        args, specs = [], []

        def add_spec(size, place, spread):
            specs.append(pl.BlockSpec((size, half, block, width), lambda e: (place, e if spread else 0, 0, 0)))

        spread = len(counts) == 1
        for k in ks:
            side, place = (0, k) if k < len(FIRST_FAR) else (1, k - len(FIRST_FAR))
            for c in GROUPS[group]:
                args.append(got[c][1 + k])
                add_spec(3, 0, spread)
            for c in GROUPS[group]:
                args.append(turns[c][side])
                add_spec(1, place, spread)
        for a in arrived:
            args.append(a)
            add_spec(3, 0, step != 1)
        if step == 3:
            out_specs = [pl.BlockSpec((half, block, width), lambda e: (e, 0, 0))] * 3
            out_shape = [shape((2 * half, block, width), t) for t in (F32, F32, BF16)]
        else:
            size = half if step == 0 else 2 * half
            out_specs = [
                pl.BlockSpec((3, half, block, width), lambda e: (0, 0 if step == 0 else e, 0, 0)) for k in range(2)
            ]
            out_shape = [shape((3, size, block, width), BF16)] * 2
        return pl.pallas_call(
            functools.partial(add_kernel, step, counts),
            grid=(2,),
            in_specs=specs,
            out_specs=out_specs,
            out_shape=out_shape,
            compiler_params=params(),
            cost_estimate=cost(3),
            name="add",
        )(*args)

    def round_on(group, step, ks, arrived=()):
        up, down = ring_sums(group, step, ks, *arrived)
        return [ring(up, n, 1), ring(down, n, -1)]

    def finish(group, arrived):
        first, second, third = ring_sums(group, 3, (7,), *arrived)
        return first, second + hop(third, n, 1).astype(F32)

    got, turns, rounds = [], [], []
    if fast:
        first, x3, four, (rows_g,) = order(token[0], x3, four, [rows_g])
        x4 = [over_x(four[:1])]
        first, x4, three, four = order(first, x4, three, four)
        token = (first, info)
        pieces = (shard, *x0, *one, *two, *three, four[0], four[0], x1, x2, x3[0], x3[0], x4[0], x4[0])
        token, some = run_experts(token, 0, pieces)
        x3.append(over_x([a[:, half:] for a in three]))
        x4.append(over_x(four[1:]))
        first, some, x3, x4, four = order(token[0], some, x3, x4, four)
        pieces = (shard, *x0, *one, *two, *three, *four, x1, x2, *x3, *x4)
        got.append(some)
        turns = [[turn(0, 0)]]
        token, some = run_experts((first, info), 1, pieces)
        first, some, turns[0], got[0] = order(token[0], some, turns[0], got[0])
        got.append(some)
        rounds.append(round_on(0, 0, (0,)))
        turns[0].append(turn(0, 1))
        turns.append([turn(1, 0)])
        token, some = run_experts((first, info), 2, pieces)
        first, some, rounds[0], turns[0], got[1] = order(token[0], some, rounds[0], turns[0], got[1])
        got.append(some)
        rounds[0] = round_on(0, 1, (1, 2), rounds[0])
        turns.append([turn(2, 0)])
        token = (first, info)
    else:
        for number in range(len(CALLS)):
            token, some = run_experts(token, number, (gathered,))
            got.append(some)
    y_parts = [some[0] for some in got]

    comb_oth = []
    for r in range(1, shares):
        token, (sent,) = combine(token, mine_count * r, BF16)
        if fast:
            first, (sent,), rounds[0], turns[1] = order(token[0], [sent], rounds[0], turns[1])
            token = (first, info)
            rounds[0] = round_on(0, 2, (3, 4), rounds[0])
        comb_oth.append(across(sent, r))
    comb_oth = comb_oth[0] if shares == 2 else sum(a.astype(F32) for a in comb_oth).astype(BF16)
    token, (comb_own,) = combine(token, 0, F32)
    if fast:
        first, (comb_own, comb_oth), rounds[0], turns[2], got[1], got[2] = order(
            token[0], [comb_own, comb_oth], rounds[0], turns[2], got[1], got[2]
        )
        token = (first, info)
        turns[1].append(turn(1, 1))
        rounds[0] = round_on(0, 2, (5, 6), rounds[0])
        rounds.append(round_on(1, 0, (0,)))

    small_spec = pl.BlockSpec((blocks, block, pack), lambda i, s: (0, 0, 0))
    tok_out = pl.BlockSpec((1, ROWS, 512), lambda i, s: (i, 0, 0))
    def backward(token, base, count):

        def later(spec):
            return pl.BlockSpec(spec.block_shape, lambda i, s: spec.index_map(i + base, s))

        return call(
            functools.partial(backward_kernel, base, rel, rel, block),
            (count,),
            token,
            [tokens, grad_out, comb_own, comb_oth, mid, proj, att, lse, gates, *w_parts],
            [
                later(spec)
                for spec in (
                    tok_spec,
                    tok_spec,
                    row_spec(1152),
                    row_spec(1152),
                    row_spec(512),
                    row_spec(1536),
                    row_spec(512),
                    row_spec(LANES),
                    row_spec(LANES),
                )
            ]
            + [any_spec()] * shares,
            [tok_out, tok_out] + [small_spec] * shares,
            [shape((count, ROWS, 512), BF16)] * 2 + [shape((blocks, block, pack), BF16)] * shares,
            [
                pltpu.VMEM((shares, 512, pack), BF16),
                pltpu.VMEM((16, 512), F32),
                pltpu.VMEM((512, LANES), BF16),
                pltpu.VMEM((ROWS, 512), F32),
                pltpu.VMEM((ROWS, 512), F32),
                pltpu.VMEM((TILE, LANES), F32),
                pltpu.VMEM((ROWS, 1536), BF16),
                pltpu.VMEM((shares, 512, 3 * local), F32),
                pltpu.VMEM((shares, 512, local), F32),
                pltpu.VMEM((512, LANES), F32),
                pltpu.VMEM((LANES, 512), F32),
                pltpu.SemaphoreType.DMA((shares, blocks)),
            ],
            "backward",
            22,
        )

    parts = []
    some = mine_count // 2
    token, part = backward(token, 0, some)
    if fast:
        first, part, rounds[0], rounds[1], turns[1], got[2] = order(
            token[0], part, rounds[0], rounds[1], turns[1], got[2]
        )
        token = (first, info)
        rounds[1] = round_on(1, 1, (1, 2), rounds[1])
        total = [finish(0, rounds[0])]
        swapped = [[across(a, 1) for a in part[:2]]]
        turns[2].append(turn(2, 1))
    parts.append(part)
    token, part = backward(token, some, some // 2)
    if fast:
        first, part, rounds[1], swapped[0], turns[2] = order(token[0], part, rounds[1], swapped[0], turns[2])
        token = (first, info)
        rounds[1] = round_on(1, 2, (3, 4), rounds[1])
        swapped.append([across(a, 1) for a in part[:2]])
    parts.append(part)
    token, part = backward(token, some + some // 2, some // 2)
    if fast:
        first, part, rounds[1], swapped[1] = order(token[0], part, rounds[1], swapped[1])
    parts.append(part)
    grads = [[part[2 + r] for part in parts] for r in range(shares)]
    def exchanged(which):
        return [across(part[which], r) if r else part[which] for r in range(shares) for part in parts]

    def assemble(token, pieces):
        token, (out,) = call(
            functools.partial(assemble_kernel, shares),
            (2,),
            token,
            pieces,
            [pl.BlockSpec(a.shape, lambda i, s: (0, 0, 0)) for a in pieces],
            [pl.BlockSpec((1, SEQ, 8, 512), lambda i, s: (i, 0, 0, 0))],
            [shape((2, SEQ, 8, 512), BF16)],
            [pltpu.VMEM((4, SEQ * 8, LANES), F32)],
            "assemble",
            6,
        )
        return token, jnp.swapaxes(out, 1, 2)

    both = sum(a.astype(F32) for a in grads[0])
    if fast:
        arrived = across(plus(*grads[1]), 1)
        first, (arrived, up, down) = order(first, [arrived, *ring_sums(1, 2, (5, 6), *rounds[1])])
        rounds[1] = [ring(up, n, 1), ring(down, n, -1)]
        swapped.append([across(a, 1) for a in parts[2][:2]])
        both = (both + arrived.astype(F32)).astype(BF16)
        square = scatter_corner(both, n)
        token, out = assemble((first, info), [part[0] for part in parts] + [pair[0] for pair in swapped])
        first, square, (out,) = order(token[0], square, [out])
        square = scatter_square(both, square, n)
        token, tok = assemble((first, info), [part[1] for part in parts] + [pair[1] for pair in swapped])
        first, square, rounds[1], (tok,) = order(token[0], square, rounds[1], [tok])
        line = plus(*square)
        near = hop(line[2:], n, 4)
        total.append(finish(1, rounds[1]))
        line = plus(line[:2], near)
        mine = line[0].astype(F32) + hop(line[1:], n, 8)[0].astype(F32)
        sums_in, sums_out = [[t[side] for t in total] for side in range(2)]
    else:
        for r in range(1, shares):
            both = both + across(plus(*grads[r]), r).astype(F32)
        mine = lax.psum_scatter(both[0].astype(BF16), "dp", scatter_dimension=0, tiled=True).astype(F32)
        token, out = assemble(token, exchanged(0))
        token, tok = assemble(token, exchanged(1))
        sums_in, sums_out = [
            [lax.psum_scatter(g[side], "dp", scatter_dimension=1, tiled=True).astype(F32) for g in got]
            for side in (1, 2)
        ]

    return (
        out,
        tok,
        mine[:, 4 * local + 8],
        jnp.stack([mine[:, j * local : (j + 1) * local] for j in range(3)]),
        mine[:, 3 * local : 4 * local].T,
        mine[:, 4 * local + 9],
        mine[:, 4 * local : 4 * local + 8],
        jnp.concatenate(sums_in, 0),
        jnp.swapaxes(jnp.concatenate(sums_out, 0), 1, 2),
    )


def solution(mesh):
    placed = (
        P(None, "dp", None, None),
        P(None, "dp"),
        P(None, "dp", None, None),
        P("dp"),
        P(None, "dp", "tensor"),
        P("tensor", "dp"),
        P("dp"),
        P("dp", None),
        P(None, "dp", "tensor"),
        P(None, "tensor", "dp"),
        P(None, "dp", None, None),
    )
    return jax.shard_map(
        functools.partial(body, mesh.shape["dp"], mesh.shape["tensor"]),
        mesh=mesh,
        in_specs=placed,
        out_specs=(
            P(None, "dp", None, None),
            P(None, "dp", None, None),
            P("dp"),
            P(None, "dp", "tensor"),
            P("tensor", "dp"),
            P("dp"),
            P("dp", None),
            P(None, "dp", "tensor"),
            P(None, "tensor", "dp"),
        ),
        check_vma=False,
    )
```
